32 devices in a mesh: dp: 2 (over x), orient: 16 (over z, y, core).
Axes of the slice: x: 2, y: 2, z: 4, core: 2. Of those that a mesh axis runs over, the one named last changes fastest.
Arguments:
- images: bfloat16 [384, 16384], P(('dp', 'orient')), may hold values from -80 to 80
- templates: bfloat16 [4096, 16384], P('orient'), as said below
- index: int32 [4096, 128], P('orient'), may hold values from 0 to 16383
- interp: float32 [4096, 128], P('orient'), may hold values from 0.25 to 1
- inv_noise: float32 [128, 128], replicated, may hold values from 0.5 to 2, as said below
Outputs:
- recon: float32 [16384, 128], P(('dp', 'orient'))
- recon_weight: float32 [16384, 128], P(('dp', 'orient'))
The draws below stay inside these ranges and needn't reach their ends.
Inputs may be any that keep to these rules, and one draw needn't show every extreme that they name: `templates`: every entry has magnitude at most 18 / 128. `inv_noise`: every entry is 0.5, 1 or 2.
All inputs are finite; a program needn't handle non-finite values.
Results may differ from the reference program's by a relative error of at most 0.0029.
Values may be sent and summed in bfloat16 or wider, within the bound.
A program may use at most 128 MiB of HBM per device.

```python
import math
import jax
import jax.numpy as jnp
from jax import lax

PIX = 128
F = 16384
VROWS = 16384
TPL_DEV = 256
NIMG = 384
NTPL = 4096
N_ORIENT = 16


def template_parts(key):
    amp = jnp.exp(jax.random.uniform(jax.random.fold_in(key, 11), (NTPL, 1), jnp.float32, math.log(0.5), math.log(2.0)))
    base = jnp.clip(jax.random.normal(jax.random.fold_in(key, 12), (NTPL, F), jnp.float32), -6.0, 6.0)
    return base * amp * (1.5 / math.sqrt(F))


def draw_templates(key, part):
    values = template_parts(key)
    return values.astype(jnp.bfloat16)


def draw_inv_noise(key, part):
    powers = jax.random.randint(jax.random.fold_in(key, 31), (PIX, PIX), -1, 2)
    return jnp.exp2(powers.astype(jnp.float32))


def draw_images(key, part):
    noise = jnp.clip(jax.random.normal(jax.random.fold_in(key, 21), (NIMG, F), jnp.float32), -6.0, 6.0)
    return noise.astype(jnp.bfloat16)


def touch_ends(array, own_key, least, largest):
    shape = array.shape
    index_at = [jax.random.randint(jax.random.fold_in(own_key, axis), (), 0, shape[axis]) for axis in range(len(shape))]
    array = array.at[tuple(index_at)].set(least)
    longest = shape.index(max(shape))
    index_at[longest] = (index_at[longest] + 1) % shape[longest]
    return array.at[tuple(index_at)].set(largest)


def block_levels(own_key, dims, pieces, low, top_value):
    def one(dim, shards_of):
        heights = jax.random.uniform(jax.random.fold_in(jax.random.fold_in(own_key, 6), dim), (shards_of,), jnp.float32, low / len(pieces), top_value / len(pieces))
        return jnp.repeat(jnp.exp(heights), dims[dim] // shards_of).reshape((-1,) + (1,) * (len(dims) - dim - 1))

    factor_of = one(*pieces[0])
    for cut in pieces[1:]:
        factor_of = factor_of * one(*cut)
    return factor_of


def setup_inputs(seed: int = 0) -> dict:
    seeds = jax.random.split(jax.random.key(seed), 6)
    images = draw_images(jax.random.fold_in(seeds[5], 71), 0)
    templates = draw_templates(jax.random.fold_in(seeds[5], 71), 0)
    index = touch_ends(jax.random.randint(seeds[2], (NTPL, PIX), 0, VROWS), jax.random.fold_in(seeds[2], 1), 0, VROWS - 1).astype(jnp.int32)
    interp = jnp.clip(0.25 + 0.75 * jax.random.uniform(seeds[3], (NTPL, PIX), jnp.float32) ** block_levels(seeds[3], (NTPL, PIX), ((0, 16),), -0.2, 0.2), 0.25, 1.0)
    inv_noise = draw_inv_noise(jax.random.fold_in(seeds[5], 71), 0)
    return dict(images=images, templates=templates, index=index, interp=interp, inv_noise=inv_noise)


def reference(images, templates, index, interp, inv_noise):
    noise_flat = inv_noise.reshape(-1)
    tpl_f = templates.astype(jnp.float32)
    weighted = (tpl_f * noise_flat[None, :]).astype(jnp.bfloat16)
    tnorm = 0.5 * jnp.sum(tpl_f * tpl_f * noise_flat[None, :], axis=1)
    image_f = images.astype(jnp.float32)
    scores = jnp.dot(image_f, weighted.astype(jnp.float32).T) - tnorm[None, :]
    peak = jnp.max(scores, axis=1, keepdims=True)
    expo = jnp.exp(scores - peak)
    posterior = expo / jnp.sum(expo, axis=1, keepdims=True)
    post_b = posterior.astype(jnp.bfloat16)
    mass = jnp.sum(posterior, axis=0)

    def insert(carry, block):
        recon, recw = carry
        start = (block * TPL_DEV).astype(jnp.int32)
        post_blk = lax.dynamic_slice_in_dim(post_b, start, TPL_DEV, 1).astype(jnp.float32)
        sums = jnp.dot(post_blk.T, image_f)
        rows_idx = lax.dynamic_slice_in_dim(index, start, TPL_DEV, 0).reshape(-1)
        weights = lax.dynamic_slice_in_dim(interp, start, TPL_DEV, 0)
        mass_blk = lax.dynamic_slice_in_dim(mass, start, TPL_DEV, 0)
        data_rows = sums.reshape(TPL_DEV * PIX, PIX) * weights.reshape(-1, 1)
        weight_rows = ((weights * mass_blk[:, None])[:, :, None] * inv_noise[None, :, :]).reshape(TPL_DEV * PIX, PIX)
        return (recon.at[rows_idx].add(data_rows), recw.at[rows_idx].add(weight_rows)), None

    init = (jnp.zeros((VROWS, PIX), jnp.float32), jnp.zeros((VROWS, PIX), jnp.float32))
    (recon, recw), unused = lax.scan(insert, init, jnp.arange(N_ORIENT, dtype=jnp.int32))
    return recon, recw
```

```python
import functools

import jax
import jax.numpy as jnp
from jax import lax
from jax.experimental import pallas as pl
from jax.experimental.pallas import tpu as pltpu
from jax.sharding import PartitionSpec as P

LANES = 128
ROWS_STEP = 8
ACCS = 4
SUB = 4
BATCH = 128
LINES = 4
PARTS = 4
NORM_COLS = 1024
LEVELS = 65535
SHIFT = 65536
LOW_BITS = 5
LOW = 1 << LOW_BITS
VMEM_LIMIT = 56 * 2**20


def data_kernel(post_ref, images_ref, interp_ref, idx_ref, clash_ref, out_ref, rows_ref, *more):
    accs = (out_ref,) + more
    step = pl.program_id(0)
    count, side = post_ref.shape[0], out_ref.shape[1]
    volume_rows = out_ref.shape[0]
    halves = count // BATCH

    @pl.when(step == 0)
    def _():
        @pl.loop(0, volume_rows // 64)
        def _(c):
            rows = pl.ds(pl.multiple_of(c * 64, 64), 64)
            for acc in accs:
                acc[rows, :] = jnp.zeros((64, side), jnp.float32)

    interp = pltpu.roll(interp_ref[...], lax.rem(side - step * ROWS_STEP, side), axis=1)
    for j in range(ROWS_STEP):
        block = jnp.dot(
            post_ref[...],
            images_ref[:, j * side : (j + 1) * side],
            preferred_element_type=jnp.float32,
        )
        rows_ref[j * count : (j + 1) * count, :] = block * interp[:, j : j + 1]

    @pl.loop(0, ROWS_STEP * halves)
    def _(g):
        base = pl.multiple_of(g * BATCH, BATCH)
        voxels = idx_ref.at[g]
        clash = clash_ref[lax.rem(g, halves), step * ROWS_STEP + lax.div(g, halves)]

        @pl.when(clash == 0)
        def _():
            pending = [None] * ACCS

            def flush(a):
                for voxel, value in pending[a] or ():
                    accs[a][pl.ds(voxel, 1), :] = value

            for n in range(BATCH // SUB):
                a = n % ACCS
                flush(a)
                pending[a] = []
                for k in range(n * SUB, (n + 1) * SUB):
                    voxel = voxels[k]
                    value = accs[a][pl.ds(voxel, 1), :] + rows_ref[pl.ds(base + k, 1), :]
                    pending[a].append((voxel, value))
            for a in range(ACCS):
                flush(a)

        @pl.when(clash != 0)
        def _():
            @pl.loop(0, BATCH // ACCS)
            def _(q):
                first = q * ACCS
                targets = [voxels[first + a] for a in range(ACCS)]
                summed = [
                    accs[a][pl.ds(targets[a], 1), :]
                    + rows_ref[pl.ds(base + first + a, 1), :]
                    for a in range(ACCS)
                ]
                for a in range(ACCS):
                    accs[a][pl.ds(targets[a], 1), :] = summed[a]

    @pl.when(step == pl.num_programs(0) - 1)
    def _():
        @pl.loop(0, volume_rows // 64)
        def _(c):
            rows = pl.ds(pl.multiple_of(c * 64, 64), 64)
            total = accs[0][rows, :]
            for acc in accs[1:]:
                total = total + acc[rows, :]
            out_ref[rows, :] = total


def insert_data(post, gathered, interp, voxels, clash, volume_rows):
    count, images = post.shape
    side = interp.shape[1]
    steps = side // ROWS_STEP
    batches = ROWS_STEP * count // BATCH
    return pl.pallas_call(
        data_kernel,
        grid=(steps,),
        out_shape=jax.ShapeDtypeStruct((volume_rows, side), jnp.float32),
        in_specs=[
            pl.BlockSpec((count, images), lambda i: (0, 0)),
            pl.BlockSpec((images, ROWS_STEP * side), lambda i: (0, i)),
            pl.BlockSpec((count, side), lambda i: (0, 0)),
            pl.BlockSpec((batches, BATCH), lambda i: (i, 0), memory_space=pltpu.SMEM),
            pl.BlockSpec(memory_space=pltpu.SMEM),
        ],
        out_specs=pl.BlockSpec(
            (volume_rows, side), lambda i: (0, 0), pipeline_mode=pl.Buffered(1)
        ),
        scratch_shapes=[pltpu.VMEM((ROWS_STEP * count, side), jnp.float32)]
        + [pltpu.VMEM((volume_rows, side), jnp.float32)] * (ACCS - 1),
        compiler_params=pltpu.CompilerParams(vmem_limit_bytes=VMEM_LIMIT),
        cost_estimate=pl.CostEstimate(
            flops=200_000_000_000, bytes_accessed=200_000_000, transcendentals=0
        ),
    )(post, gathered, interp, voxels, clash)


def reduce_kernel(
    groups,
    orient,
    blocks_ref,
    mass_ref,
    places_ref,
    noise_ref,
    out_ref,
    weight_ref,
    grid_ref,
    mass_row,
    mine,
    theirs,
    ready,
    landed,
    masses,
    own_sem,
    pair_send,
    pair_recv,
    send_sem,
    recv_sem,
    mass_send,
    mass_recv,
):
    half = orient // 2
    chips = groups * half
    group, place = lax.axis_index("dp"), lax.axis_index("orient")
    core = lax.rem(place, 2)
    me = group * half + lax.div(place, 2)
    partner = (group, place + 1 - 2 * core)
    mesh_ids = pl.DeviceIdType.MESH

    def device(chip):
        return (lax.div(chip, half), lax.rem(chip, half) * 2 + core)

    devices = 2 * chips
    rank = group * orient + place

    def ranked(d):
        return (lax.div(d, orient), lax.rem(d, orient))

    barrier = pltpu.get_barrier_semaphore()

    @pl.loop(1, devices)
    def _(s):
        pl.semaphore_signal(
            barrier,
            inc=1,
            device_id=ranked(lax.rem(rank + s, devices)),
            device_id_type=mesh_ids,
        )

    pl.semaphore_wait(barrier, devices - 1)

    def mass_copy(s):
        return pltpu.make_async_remote_copy(
            src_ref=mass_ref,
            dst_ref=masses.at[s],
            send_sem=mass_send.at[s],
            recv_sem=mass_recv.at[s],
            device_id=ranked(lax.rem(rank + s, devices)),
            device_id_type=mesh_ids,
        )

    def own_copy(s):
        return pltpu.make_async_copy(
            blocks_ref.at[lax.rem(me + s, chips), core], mine.at[s], own_sem.at[s]
        )

    def pair_copy(s):
        return pltpu.make_async_remote_copy(
            src_ref=blocks_ref.at[lax.rem(me + s, chips), 1 - core],
            dst_ref=theirs.at[s],
            send_sem=pair_send.at[s],
            recv_sem=pair_recv.at[s],
            device_id=partner,
            device_id_type=mesh_ids,
        )

    def chip_copy(s):
        return pltpu.make_async_remote_copy(
            src_ref=ready.at[s],
            dst_ref=landed.at[s],
            send_sem=send_sem.at[s],
            recv_sem=recv_sem.at[s],
            device_id=device(lax.rem(me + s, chips)),
            device_id_type=mesh_ids,
        )

    @pl.loop(1, devices)
    def _(s):
        mass_copy(s).start()

    @pl.loop(1, chips + 1)
    def _(k):
        s = lax.rem(k, chips)
        own_copy(s).start()
        pair_copy(s).start()

    @pl.loop(1, chips)
    def _(s):
        own_copy(s).wait()
        pair_copy(s).wait()
        ready[s] = (mine[s] + theirs[s]).astype(ready.dtype)
        chip_copy(s).start()

    own_copy(0).wait()
    pair_copy(0).wait()
    out_ref[...] = mine[0] + theirs[0]
    mass_row[...] = jnp.zeros_like(mass_row)
    mass_rows = mass_ref.shape[0]

    def add_mass(d, ref):
        start = lax.rem(d, orient) * (mass_rows * LANES)
        for k in range(mass_rows):
            lanes = pl.ds(pl.multiple_of(start + k * LANES, LANES), LANES)
            mass_row[:, lanes] += ref[k : k + 1, :]

    add_mass(rank, mass_ref)

    @pl.loop(1, devices)
    def _(s):
        mass_copy(s).wait()
        add_mass(lax.rem(rank + devices - s, devices), masses.at[s])

    insert_weights(rank, places_ref, mass_row, noise_ref, weight_ref, grid_ref)

    @pl.loop(1, chips)
    def _(s):
        chip_copy(s).wait()
        out_ref[...] += landed[s].astype(jnp.float32)


def reduce_rows(volume, mass_rows, places_t, inv_noise, groups, orient):
    chips = groups * orient // 2
    rows, side = volume.shape[0] // (2 * chips), volume.shape[1]
    parts = (chips, rows, side)
    masses = (2 * chips,) + mass_rows.shape
    return pl.pallas_call(
        functools.partial(reduce_kernel, groups, orient),
        out_shape=(
            jax.ShapeDtypeStruct((rows, side), jnp.float32),
            jax.ShapeDtypeStruct((rows, side), jnp.float32),
        ),
        in_specs=[pl.BlockSpec(memory_space=pl.ANY)]
        + [pl.BlockSpec(memory_space=pltpu.VMEM)] * 3,
        out_specs=(
            pl.BlockSpec(memory_space=pltpu.VMEM),
            pl.BlockSpec(memory_space=pltpu.VMEM),
        ),
        scratch_shapes=[
            pltpu.VMEM((side * max(8, rows // LOW), LANES), jnp.float32),
            pltpu.VMEM((1, places_t.shape[0] * places_t.shape[2]), jnp.float32),
        ]
        + [pltpu.VMEM(parts, jnp.float32)] * 2
        + [pltpu.VMEM(parts, jnp.bfloat16)] * 2
        + [pltpu.VMEM(masses, jnp.float32)]
        + [pltpu.SemaphoreType.DMA((chips,))] * 5
        + [pltpu.SemaphoreType.DMA((2 * chips,))] * 2,
        compiler_params=pltpu.CompilerParams(
            collective_id=0, has_side_effects=True, vmem_limit_bytes=VMEM_LIMIT
        ),
    )(volume.reshape(chips, 2, rows, side), mass_rows, places_t, inv_noise)


def split(value):
    high = value.astype(jnp.bfloat16)
    return high, (value - high.astype(jnp.float32)).astype(jnp.bfloat16)


def insert_weights(rank, places_ref, mass_row, noise_ref, out_ref, grid_ref):
    first = rank * out_ref.shape[0]
    blocks, _, each = places_ref.shape
    count = blocks * each
    side = noise_ref.shape[0]
    high_rows = grid_ref.shape[0] // side
    nt = (((1,), (1,)), ((), ()))
    tn = (((0,), (0,)), ((), ()))
    one, zero = jnp.float32(1), jnp.float32(0)

    @pl.loop(0, side // ROWS_STEP)
    def _(step):
        iota_high = lax.broadcasted_iota(jnp.int32, (high_rows, count), 0)
        iota_low = lax.broadcasted_iota(jnp.int32, (LOW, count), 0)
        block = pl.ds(pl.multiple_of(step * ROWS_STEP, ROWS_STEP), ROWS_STEP)
        words = jnp.concatenate([places_ref[d, block, :] for d in range(blocks)], axis=1)
        locals_ = (words >> 16) - first
        weights = (words & (SHIFT - 1)).astype(jnp.float32) * (1 / LEVELS) * mass_row[...]
        for j in range(ROWS_STEP):
            local = locals_[j : j + 1, :]
            hot = jnp.where(iota_high == (local >> LOW_BITS), one, zero)
            low = jnp.where(iota_low == (local & (LOW - 1)), weights[j : j + 1, :], zero)
            part = lax.dot_general(
                hot.astype(jnp.bfloat16),
                low.astype(jnp.bfloat16),
                nt,
                preferred_element_type=jnp.float32,
            )
            row = pl.multiple_of((step * ROWS_STEP + j) * high_rows, 8)
            grid_ref[pl.ds(row, high_rows), :LOW] = part

    noise = noise_ref[...].astype(jnp.bfloat16)
    for h in range(out_ref.shape[0] // LOW):
        high, low = split(grid_ref[pl.ds(h, side, stride=high_rows), :])
        block = lax.dot_general(
            high, noise, tn, preferred_element_type=jnp.float32
        ) + lax.dot_general(low, noise, tn, preferred_element_type=jnp.float32)
        out_ref[h * LOW : (h + 1) * LOW, :] = block[:LOW]


def gather_kernel(
    orient,
    images_ref,
    templates_ref,
    noise_ref,
    index_ref,
    interp_ref,
    gathered_ref,
    post_ref,
    mass_ref,
    words_ref,
    rows_ref,
    clash_ref,
    raw,
    weighted,
    whole,
    scores,
    norms,
    stats,
    landed,
    load_sem,
    store_sem,
    send_sem,
    recv_sem,
    stat_send,
    stat_recv,
):
    lines, across = LINES, orient // (2 * LINES)
    group, place = lax.axis_index("dp"), lax.axis_index("orient")
    core = lax.rem(place, 2)
    chip = lax.div(place, 2)
    row, col = lax.div(chip, across), lax.rem(chip, across)
    mesh_ids = pl.DeviceIdType.MESH
    block_rows, width = images_ref.shape
    part = width // PARTS
    count = templates_ref.shape[0]
    fold = templates_ref.shape[1] // width
    line_images = 2 * across * block_rows // fold
    images = line_images * lines

    def at(r, q, c):
        return (r * across + q) * 2 + c

    barrier = pltpu.get_barrier_semaphore()

    @pl.loop(1, orient)
    def _(s):
        pl.semaphore_signal(
            barrier,
            inc=1,
            device_id=(group, lax.rem(place + s, orient)),
            device_id_type=mesh_ids,
        )

    def load_copy(k):
        cols = pl.ds(pl.multiple_of(k * width, width), width)
        return pltpu.make_async_copy(
            templates_ref.at[:, cols], weighted.at[:, cols], load_sem.at[k]
        )

    for k in range(fold):
        load_copy(k).start()

    pl.semaphore_wait(barrier, orient - 1)

    def copy(source, r, q, s, way, target):
        cols = pl.ds(pl.multiple_of(s * part, part), part)
        slot = at(r, q, core)
        ref = images_ref if source is None else raw.at[slot]
        return pltpu.make_async_remote_copy(
            src_ref=ref.at[:, cols],
            dst_ref=raw.at[slot, :, cols],
            send_sem=send_sem.at[lax.div(slot, 2), s, way],
            recv_sem=recv_sem.at[slot, s],
            device_id=(group, target),
            device_id_type=mesh_ids,
        )

    def arrived(r, q, c, s):
        cols = pl.ds(pl.multiple_of(s * part, part), part)
        slot = at(r, q, c)
        pltpu.make_async_remote_copy(
            src_ref=raw.at[slot, :, cols],
            dst_ref=raw.at[slot, :, cols],
            send_sem=send_sem.at[0, 0, 0],
            recv_sem=recv_sem.at[slot, s],
            device_id=(group, place + 1 - 2 * core),
            device_id_type=mesh_ids,
        ).wait_recv()

    def each_send(r, q, s, act, source=raw):
        for way, step in ((0, 1), (1, -1)):
            onward = row + step
            if source is None:
                along = (onward >= 0) & (onward < lines)
            else:
                along = (q == col) & (onward >= 0) & (onward < lines) & ((row - r) * step > 0)

            @pl.when(along)
            def _(way=way, onward=onward):
                act(copy(source, r, q, s, way, at(onward, col, core)))

        for way, step in ((2, 1), (3, -1)):
            onward = col + step
            beside = (onward >= 0) & (onward < across) & ((col - q) * step >= 0)

            @pl.when(beside)
            def _(way=way, onward=onward):
                act(copy(source, r, q, s, way, at(row, onward, core)))

        act(copy(source, r, q, s, 4, place + 1 - 2 * core))

    @pl.loop(0, PARTS)
    def _(s):
        each_send(row, col, s, lambda c: c.start(), None)

    raw[place] = images_ref[...]
    scores[...] = jnp.zeros_like(scores)
    norms[...] = jnp.zeros_like(norms)

    index = index_ref[...]
    near = jnp.zeros(index.shape, jnp.int32)
    spot = lax.broadcasted_iota(jnp.int32, index.shape, 0) % SUB
    for d in range(1, SUB):
        same = (index == pltpu.roll(index, d, axis=0)) & (spot >= d)
        near = near | same.astype(jnp.int32)
    clash_ref[...] = jnp.zeros_like(clash_ref)
    for h in range(count // BATCH):
        clash_ref[h : h + 1, :] = jnp.max(
            near[h * BATCH : (h + 1) * BATCH, :], axis=0, keepdims=True
        )
    index_t = index.T
    for h in range(count // BATCH):
        rows_ref[pl.ds(h, index_t.shape[0], stride=count // BATCH), :] = index_t[
            :, h * BATCH : (h + 1) * BATCH
        ]
    level = (interp_ref[...] * LEVELS + 0.5).astype(jnp.int32)
    words_ref[...] = (index * SHIFT + level).T

    def weigh(k):
        load_copy(k).wait()

        @pl.loop(0, width // NORM_COLS)
        def _(g):
            cols = pl.ds(pl.multiple_of(k * width + g * NORM_COLS, NORM_COLS), NORM_COLS)
            for h in range(0, count, 64):
                tpl = weighted[h : h + 64, cols].astype(jnp.float32)
                noise = noise_ref[:, cols]
                scaled = tpl * noise
                square = tpl * tpl * noise
                total = square[:, :LANES]
                for j in range(1, NORM_COLS // LANES):
                    total = total + square[:, j * LANES : (j + 1) * LANES]
                norms[h : h + 64, :] += total
                weighted[h : h + 64, cols] = scaled.astype(jnp.bfloat16)

    def score(r, s):
        for q in range(across):
            arrived(r, q, 1 - core, s)
        cols = pl.ds(pl.multiple_of(s * part, part), part)
        slots = pl.ds(pl.multiple_of(r * (2 * across), 2 * across), 2 * across)
        block = raw[slots, :, cols].reshape(2 * across * block_rows, part)
        total = 2 * across * block_rows
        out_row = lax.broadcasted_iota(jnp.int32, (total, total), 0)
        from_row = lax.broadcasted_iota(jnp.int32, (total, total), 1)
        wanted = (out_row % line_images) * fold + out_row // line_images
        pick = jnp.where(from_row == wanted, 1.0, 0.0).astype(jnp.bfloat16)
        sorted_ = jnp.dot(pick, block, preferred_element_type=jnp.float32)
        sorted_ = sorted_.astype(jnp.bfloat16)
        rows = pl.ds(pl.multiple_of(r * line_images, line_images), line_images)
        added = scores[rows, :]
        for k in range(fold):
            piece = sorted_[k * line_images : (k + 1) * line_images, :]
            span = pl.ds(pl.multiple_of(k * width + s * part, part), part)
            whole[rows, span] = piece
            added = added + lax.dot_general(
                piece,
                weighted[:, span],
                (((1,), (1,)), ((), ())),
                preferred_element_type=jnp.float32,
            )
        scores[rows, :] = added

    def store_copy(r):
        rows = pl.ds(pl.multiple_of(r * line_images, line_images), line_images)
        return pltpu.make_async_copy(whole.at[rows], gathered_ref.at[rows], store_sem.at[r])

    def score_store(r, s):
        score(r, s)

        @pl.when(s == PARTS - 1)
        def _():
            store_copy(r).start()

    @pl.loop(0, lines * PARTS + 1)
    def _(k):
        n, s = lax.div(k, PARTS) + 1, lax.rem(k, PARTS)
        for sign in (1, -1):
            r = row + sign * n

            @pl.when((r >= 0) & (r < lines) & (n < lines))
            def _(r=r):
                arrived(r, col, core, s)
                each_send(r, col, s, lambda c: c.start())

        for sign in (1, -1):
            r = row + sign * (n - 1)
            live = (r >= 0) & (r < lines) & (n <= lines)
            if sign < 0:
                live = live & (n > 1)
            for e in range(1, across):
                for side in (1, -1):
                    q = col + side * e

                    @pl.when(live & (q >= 0) & (q < across))
                    def _(r=r, q=q):
                        arrived(r, q, core, s)
                        each_send(r, q, s, lambda c: c.start())

        @pl.when(n == 1)
        def _():
            @pl.loop(0, fold // PARTS)
            def _(j):
                weigh(s * (fold // PARTS) + j)

        last = jnp.maximum(k - 1, 0)
        m, t = lax.div(last, PARTS) + 1, lax.rem(last, PARTS)

        @pl.when((m == 2) & (k > 0))
        def _():
            score_store(row, t)

        for sign in (1, -1):
            r = row + sign * (m - 1)

            @pl.when((m > 1) & (r >= 0) & (r < lines))
            def _(r=r):
                score_store(r, t)

    norm = 0.5 * jnp.sum(norms[...].T, axis=0, keepdims=True)
    value = (scores[...] - norm).T
    peak_own = jnp.max(value, axis=0, keepdims=True)
    expo = jnp.exp(value - peak_own)
    stats[...] = jnp.zeros_like(stats)
    stats[0:1, :] = peak_own
    stats[1:2, :] = jnp.sum(expo, axis=0, keepdims=True)

    def stat_copy(s):
        return pltpu.make_async_remote_copy(
            src_ref=stats,
            dst_ref=landed.at[s],
            send_sem=stat_send.at[s],
            recv_sem=stat_recv.at[s],
            device_id=(group, lax.rem(place + s, orient)),
            device_id_type=mesh_ids,
        )

    @pl.loop(1, orient)
    def _(s):
        stat_copy(s).start()

    landed[0] = stats[...]

    @pl.loop(1, orient)
    def _(s):
        stat_copy(s).wait()

    peak = peak_own
    for s in range(1, orient):
        peak = jnp.maximum(peak, landed[s, 0:1, :])
    total = jnp.zeros_like(peak)
    for s in range(orient):
        total = total + landed[s, 1:2, :] * jnp.exp(landed[s, 0:1, :] - peak)
    posterior = (expo * (jnp.exp(peak_own - peak) / total))[:, :images]
    post_ref[...] = posterior.astype(jnp.bfloat16)
    mass = jnp.sum(posterior, axis=1, keepdims=True)
    mass_ref[...] = jnp.broadcast_to(mass, (count, LANES)).T[:8, :]

    for r in range(lines):
        store_copy(r).wait()

    @pl.loop(0, PARTS)
    def _(s):
        each_send(row, col, s, lambda c: c.wait_send(), None)
        for r in range(lines):
            for q in range(across):

                @pl.when((row != r) | (col != q))
                def _(r=r, q=q):
                    each_send(r, q, s, lambda c: c.wait_send())


def gather_scores(images, templates, index, interp, noise_flat, orient):
    own, pixels = images.shape
    count, side = index.shape
    fold = PARTS
    while own * fold % 16:
        fold += PARTS
    width = pixels // fold
    total = own * orient
    padded = -(-total // LANES) * LANES
    vmem = pl.BlockSpec(memory_space=pltpu.VMEM)
    hbm = pl.BlockSpec(memory_space=pl.ANY)
    chips = orient // 2
    return pl.pallas_call(
        functools.partial(gather_kernel, orient),
        out_shape=(
            jax.ShapeDtypeStruct((total, pixels), jnp.bfloat16),
            jax.ShapeDtypeStruct((count, total), jnp.bfloat16),
            jax.ShapeDtypeStruct((8, count), jnp.float32),
            jax.ShapeDtypeStruct((side, count), jnp.int32),
            jax.ShapeDtypeStruct((side * count // BATCH, BATCH), jnp.int32),
            jax.ShapeDtypeStruct((8, side), jnp.int32),
        ),
        in_specs=[vmem, hbm, vmem, vmem, vmem],
        out_specs=(hbm, vmem, vmem, vmem, vmem, vmem),
        scratch_shapes=[
            pltpu.VMEM((orient, own * fold, width), jnp.bfloat16),
            pltpu.VMEM((count, pixels), jnp.bfloat16),
            pltpu.VMEM((total, pixels), jnp.bfloat16),
            pltpu.VMEM((padded, count), jnp.float32),
            pltpu.VMEM((count, LANES), jnp.float32),
            pltpu.VMEM((8, padded), jnp.float32),
            pltpu.VMEM((orient, 8, padded), jnp.float32),
            pltpu.SemaphoreType.DMA((fold,)),
            pltpu.SemaphoreType.DMA((LINES,)),
            pltpu.SemaphoreType.DMA((chips, PARTS, 5)),
            pltpu.SemaphoreType.DMA((orient, PARTS)),
            pltpu.SemaphoreType.DMA((orient,)),
            pltpu.SemaphoreType.DMA((orient,)),
        ],
        compiler_params=pltpu.CompilerParams(
            collective_id=1, has_side_effects=True, vmem_limit_bytes=VMEM_LIMIT
        ),
    )(images.reshape(own * fold, width), templates, noise_flat, index, interp)


def shards(groups, orient, images, templates, index, interp, inv_noise):
    side = inv_noise.shape[0]
    gathered, post, mass, words, voxels, clash = gather_scores(
        images, templates, index, interp, inv_noise.reshape(1, -1), orient
    )
    places = lax.all_gather(words, "orient", axis=0)
    volume = insert_data(post, gathered, interp, voxels, clash, side * side)
    return reduce_rows(
        volume, mass[0].reshape(-1, LANES), places, inv_noise, groups, orient
    )


def solution(mesh):
    placed = (
        P(("dp", "orient"), None),
        P("orient", None),
        P("orient", None),
        P("orient", None),
        P(),
    )
    return jax.shard_map(
        functools.partial(shards, mesh.shape["dp"], mesh.shape["orient"]),
        mesh=mesh,
        in_specs=placed,
        out_specs=(P(("dp", "orient"), None), P(("dp", "orient"), None)),
        check_vma=False,
    )
```

```python
import functools

import jax
import jax.numpy as jnp
from jax import lax
from jax.experimental import pallas as pl
from jax.experimental.pallas import tpu as pltpu
from jax.sharding import PartitionSpec as P

LANES = 128
ROWS_STEP = 8
ACCS = 4
SUB = 4
BATCH = 128
LINES = 4
PARTS = 4
NORM_COLS = 1024
LEVELS = 65535
SHIFT = 65536
LOW_BITS = 5
LOW = 1 << LOW_BITS
VMEM_LIMIT = 56 * 2**20


def data_kernel(post_ref, images_ref, interp_ref, idx_ref, clash_ref, out_ref, rows_ref, *more):
    accs = (out_ref,) + more
    step = pl.program_id(0)
    count, side = post_ref.shape[0], out_ref.shape[1]
    volume_rows = out_ref.shape[0]
    halves = count // BATCH

    @pl.when(step == 0)
    def _():
        @pl.loop(0, volume_rows // 64)
        def _(c):
            rows = pl.ds(pl.multiple_of(c * 64, 64), 64)
            for acc in accs:
                acc[rows, :] = jnp.zeros((64, side), jnp.float32)

    interp = pltpu.roll(interp_ref[...], lax.rem(side - step * ROWS_STEP, side), axis=1)
    for j in range(ROWS_STEP):
        block = jnp.dot(
            post_ref[...],
            images_ref[:, j * side : (j + 1) * side],
            preferred_element_type=jnp.float32,
        )
        rows_ref[j * count : (j + 1) * count, :] = block * interp[:, j : j + 1]

    @pl.loop(0, ROWS_STEP * halves)
    def _(g):
        base = pl.multiple_of(g * BATCH, BATCH)
        voxels = idx_ref.at[g]
        clash = clash_ref[lax.rem(g, halves), step * ROWS_STEP + lax.div(g, halves)]

        @pl.when(clash == 0)
        def _():
            pending = [None] * ACCS

            def flush(a):
                for voxel, value in pending[a] or ():
                    accs[a][pl.ds(voxel, 1), :] = value

            for n in range(BATCH // SUB):
                a = n % ACCS
                flush(a)
                pending[a] = []
                for k in range(n * SUB, (n + 1) * SUB):
                    voxel = voxels[k]
                    value = accs[a][pl.ds(voxel, 1), :] + rows_ref[pl.ds(base + k, 1), :]
                    pending[a].append((voxel, value))
            for a in range(ACCS):
                flush(a)

        @pl.when(clash != 0)
        def _():
            @pl.loop(0, BATCH // ACCS)
            def _(q):
                first = q * ACCS
                targets = [voxels[first + a] for a in range(ACCS)]
                summed = [
                    accs[a][pl.ds(targets[a], 1), :]
                    + rows_ref[pl.ds(base + first + a, 1), :]
                    for a in range(ACCS)
                ]
                for a in range(ACCS):
                    accs[a][pl.ds(targets[a], 1), :] = summed[a]

    @pl.when(step == pl.num_programs(0) - 1)
    def _():
        @pl.loop(0, volume_rows // 64)
        def _(c):
            rows = pl.ds(pl.multiple_of(c * 64, 64), 64)
            total = accs[0][rows, :]
            for acc in accs[1:]:
                total = total + acc[rows, :]
            out_ref[rows, :] = total


def insert_data(post, gathered, interp, voxels, clash, volume_rows):
    count, images = post.shape
    side = interp.shape[1]
    steps = side // ROWS_STEP
    batches = ROWS_STEP * count // BATCH
    return pl.pallas_call(
        data_kernel,
        grid=(steps,),
        out_shape=jax.ShapeDtypeStruct((volume_rows, side), jnp.float32),
        in_specs=[
            pl.BlockSpec((count, images), lambda i: (0, 0)),
            pl.BlockSpec((images, ROWS_STEP * side), lambda i: (0, i)),
            pl.BlockSpec((count, side), lambda i: (0, 0)),
            pl.BlockSpec((batches, BATCH), lambda i: (i, 0), memory_space=pltpu.SMEM),
            pl.BlockSpec(memory_space=pltpu.SMEM),
        ],
        out_specs=pl.BlockSpec(
            (volume_rows, side), lambda i: (0, 0), pipeline_mode=pl.Buffered(1)
        ),
        scratch_shapes=[pltpu.VMEM((ROWS_STEP * count, side), jnp.float32)]
        + [pltpu.VMEM((volume_rows, side), jnp.float32)] * (ACCS - 1),
        compiler_params=pltpu.CompilerParams(vmem_limit_bytes=VMEM_LIMIT),
        cost_estimate=pl.CostEstimate(
            flops=200_000_000_000, bytes_accessed=200_000_000, transcendentals=0
        ),
    )(post, gathered, interp, voxels, clash)


def reduce_kernel(
    groups,
    orient,
    blocks_ref,
    mass_ref,
    places_ref,
    noise_ref,
    out_ref,
    weight_ref,
    grid_ref,
    mass_row,
    mine,
    theirs,
    first_x,
    first_x_in,
    first_y,
    first_y_in,
    second_x,
    second_x_in,
    second_y,
    second_y_in,
    last,
    last_in,
    masses,
    own_sem,
    pair_send,
    pair_recv,
    fx_send,
    fx_recv,
    fy_send,
    fy_recv,
    sx_send,
    sx_recv,
    sy_send,
    sy_recv,
    last_send,
    last_recv,
    mass_send,
    mass_recv,
):
    lines, across = LINES, orient // (2 * LINES)
    devices = groups * orient
    group, place = lax.axis_index("dp"), lax.axis_index("orient")
    core, chip = lax.rem(place, 2), lax.div(place, 2)
    row, col = lax.div(chip, across), lax.rem(chip, across)
    rank = group * orient + place
    half = out_ref.shape[0] // 2
    mesh_ids = pl.DeviceIdType.MESH

    def ranked(d):
        return (lax.div(d, orient), lax.rem(d, orient))

    def line(k):
        return lax.rem(row + k + 1, lines)

    def group_at(i):
        return lax.rem(group + i, groups)

    def col_at(j):
        return lax.rem(col + j, across)

    def block(x, r, q):
        return (x * lines + r) * across + q

    def remote(source, target, send, recv, x, r, q, c):
        return pltpu.make_async_remote_copy(
            src_ref=source,
            dst_ref=target,
            send_sem=send,
            recv_sem=recv,
            device_id=(x, (r * across + q) * 2 + c),
            device_id_type=mesh_ids,
        )

    barrier = pltpu.get_barrier_semaphore()

    @pl.loop(1, devices)
    def _(s):
        pl.semaphore_signal(
            barrier,
            inc=1,
            device_id=ranked(lax.rem(rank + s, devices)),
            device_id_type=mesh_ids,
        )

    def own_copy(k, i, j):
        p = block(group_at(i), line(k), col_at(j))
        return pltpu.make_async_copy(
            blocks_ref.at[p, core], mine.at[p], own_sem.at[k, i * across + j]
        )

    for i in reversed(range(groups)):
        for j in reversed(range(across)):

            @pl.loop(0, lines)
            def _(k, i=i, j=j):
                own_copy(k, i, j).start()

    pl.semaphore_wait(barrier, devices - 1)

    def mass_copy(s):
        return pltpu.make_async_remote_copy(
            src_ref=mass_ref,
            dst_ref=masses.at[s],
            send_sem=mass_send.at[s],
            recv_sem=mass_recv.at[s],
            device_id=ranked(lax.rem(rank + s, devices)),
            device_id_type=mesh_ids,
        )

    def pair_copy(k, i, j):
        p, n = block(group_at(i), line(k), col_at(j)), i * across + j
        return remote(
            blocks_ref.at[p, 1 - core],
            theirs.at[p],
            pair_send.at[k, n],
            pair_recv.at[k, n],
            group,
            row,
            col,
            1 - core,
        )

    def first_x_copy(k, i):
        return remote(
            first_x.at[i - 1, k],
            first_x_in.at[i - 1, k],
            fx_send.at[i - 1, k],
            fx_recv.at[i - 1, k],
            group_at(i),
            row,
            col,
            core,
        )

    def first_y_copy(k, j):
        return remote(
            first_y.at[j - 1, k],
            first_y_in.at[j - 1, k],
            fy_send.at[j - 1, k],
            fy_recv.at[j - 1, k],
            group,
            row,
            col_at(j),
            core,
        )

    def second_x_copy(k, i):
        return remote(
            second_x.at[i - 1, k],
            second_x_in.at[i - 1, k],
            sx_send.at[i - 1, k],
            sx_recv.at[i - 1, k],
            group_at(i),
            row,
            col,
            core,
        )

    def second_y_copy(k, j):
        return remote(
            second_y.at[j - 1, k],
            second_y_in.at[j - 1, k],
            sy_send.at[j - 1, k],
            sy_recv.at[j - 1, k],
            group,
            row,
            col_at(j),
            core,
        )

    def last_copy(k):
        return remote(
            last.at[k],
            last_in.at[k],
            last_send.at[k],
            last_recv.at[k],
            group,
            line(k),
            col,
            core,
        )

    @pl.loop(0, lines)
    def _(k):
        for i in reversed(range(groups)):
            for j in reversed(range(across)):
                pair_copy(k, i, j).start()

    @pl.loop(1, devices)
    def _(s):
        mass_copy(s).start()

    def narrow(value):
        return value.astype(jnp.bfloat16)

    def begin(k):
        for i in reversed(range(groups)):
            for j in reversed(range(across)):
                x, q = group_at(i), col_at(j)
                p = block(x, line(k), q)
                own_copy(k, i, j).wait()
                pair_copy(k, i, j).wait()
                if i == 0 or j == 0:
                    total = mine[p] + theirs[p]
                    mine[p] = total
                    if i:
                        first_x[i - 1, k, q] = narrow(total[:half])
                    if j:
                        first_y[j - 1, k, x] = narrow(total[half:])
                else:
                    first_x[i - 1, k, q] = narrow(mine[p, :half] + theirs[p, :half])
                    first_y[j - 1, k, x] = narrow(mine[p, half:] + theirs[p, half:])
            if i:
                first_x_copy(k, i).start()
        for j in range(1, across):
            first_y_copy(k, j).start()

    def middle(k):
        for i in range(1, groups):
            first_x_copy(k, i).wait()
        for j in reversed(range(across)):
            q = col_at(j)
            p = block(group, line(k), q)
            total = mine[p, :half]
            for i in range(1, groups):
                total = total + first_x_in[i - 1, k, q].astype(jnp.float32)
            if j:
                second_y[j - 1, k] = narrow(total)
                second_y_copy(k, j).start()
            else:
                mine[p, :half] = total
        for j in range(1, across):
            first_y_copy(k, j).wait()
        for i in reversed(range(groups)):
            x = group_at(i)
            p = block(x, line(k), col)
            total = mine[p, half:]
            for j in range(1, across):
                total = total + first_y_in[j - 1, k, x].astype(jnp.float32)
            if i:
                second_x[i - 1, k] = narrow(total)
                second_x_copy(k, i).start()
            else:
                mine[p, half:] = total

    def end(k):
        p = block(group, line(k), col)
        for j in range(1, across):
            second_y_copy(k, j).wait()
        top = mine[p, :half]
        for j in range(1, across):
            top = top + second_y_in[j - 1, k].astype(jnp.float32)
        for i in range(1, groups):
            second_x_copy(k, i).wait()
        low = mine[p, half:]
        for i in range(1, groups):
            low = low + second_x_in[i - 1, k].astype(jnp.float32)

        @pl.when(k < lines - 1)
        def _():
            last[k, :half] = narrow(top)
            last[k, half:] = narrow(low)
            last_copy(k).start()

        @pl.when(k == lines - 1)
        def _():
            out_ref[:half] = top
            out_ref[half:] = low

    mass_row[...] = jnp.zeros_like(mass_row)
    mass_rows = mass_ref.shape[0]

    def add_mass(d, ref):
        start = lax.rem(d, orient) * (mass_rows * LANES)
        for k in range(mass_rows):
            lanes = pl.ds(pl.multiple_of(start + k * LANES, LANES), LANES)
            mass_row[:, lanes] += ref[k : k + 1, :]

    steps, slots = noise_ref.shape[0] // ROWS_STEP, 3 * (lines + 2)

    def weigh(w):
        weight_step(w, rank * out_ref.shape[0], places_ref, mass_row, grid_ref)

    @pl.loop(0, slots)
    def _(slot):
        k, turn = lax.div(slot, 3), lax.rem(slot, 3)

        @pl.when((turn == 0) & (k < lines))
        def _():
            begin(k)

        @pl.when((turn == 1) & (k >= 1) & (k < lines + 1))
        def _():
            middle(k - 1)

        @pl.when((turn == 2) & (k >= 2))
        def _():
            end(k - 2)

        @pl.when(slot == 1)
        def _():
            add_mass(rank, mass_ref)

            @pl.loop(1, devices)
            def _(s):
                mass_copy(s).wait()
                add_mass(lax.rem(rank + devices - s, devices), masses.at[s])

        @pl.when((slot >= 2) & (slot < 2 + steps))
        def _():
            weigh(slot - 2)

    @pl.loop(slots - 2, max(steps, slots - 2))
    def _(w):
        weigh(w)

    weight_rows(noise_ref, weight_ref, grid_ref)
    for k in range(lines - 1):
        last_copy(k).wait()
        out_ref[...] += last_in[k].astype(jnp.float32)


def reduce_rows(volume, mass_rows, places_t, inv_noise, groups, orient):
    chips = groups * orient // 2
    lines, across = LINES, orient // (2 * LINES)
    rows, side = volume.shape[0] // (2 * chips), volume.shape[1]
    half = rows // 2
    parts = (chips, rows, side)
    masses = (2 * chips,) + mass_rows.shape
    shapes = [
        (groups - 1, lines, across, half, side),
        (across - 1, lines, groups, half, side),
        (groups - 1, lines, half, side),
        (across - 1, lines, half, side),
        (lines - 1, rows, side),
    ]
    sems = [
        (groups - 1, lines),
        (across - 1, lines),
        (groups - 1, lines),
        (across - 1, lines),
        (lines - 1,),
        (2 * chips,),
    ]
    return pl.pallas_call(
        functools.partial(reduce_kernel, groups, orient),
        out_shape=(
            jax.ShapeDtypeStruct((rows, side), jnp.float32),
            jax.ShapeDtypeStruct((rows, side), jnp.float32),
        ),
        in_specs=[pl.BlockSpec(memory_space=pl.ANY)]
        + [pl.BlockSpec(memory_space=pltpu.VMEM)] * 3,
        out_specs=(
            pl.BlockSpec(memory_space=pltpu.VMEM),
            pl.BlockSpec(memory_space=pltpu.VMEM),
        ),
        scratch_shapes=[
            pltpu.VMEM((side * max(8, rows // LOW), LANES), jnp.float32),
            pltpu.VMEM((1, places_t.shape[0] * places_t.shape[2]), jnp.float32),
        ]
        + [pltpu.VMEM(parts, jnp.float32)] * 2
        + [pltpu.VMEM(s, jnp.bfloat16) for s in shapes for _ in range(2)]
        + [pltpu.VMEM(masses, jnp.float32)]
        + [pltpu.SemaphoreType.DMA((lines, groups * across))] * 3
        + [pltpu.SemaphoreType.DMA(s) for s in sems for _ in range(2)],
        compiler_params=pltpu.CompilerParams(
            collective_id=0, has_side_effects=True, vmem_limit_bytes=VMEM_LIMIT
        ),
    )(volume.reshape(chips, 2, rows, side), mass_rows, places_t, inv_noise)


def split(value):
    high = value.astype(jnp.bfloat16)
    return high, (value - high.astype(jnp.float32)).astype(jnp.bfloat16)


def weight_step(step, first, places_ref, mass_row, grid_ref):
    blocks, side, each = places_ref.shape
    count = blocks * each
    high_rows = grid_ref.shape[0] // side
    nt = (((1,), (1,)), ((), ()))
    one, zero = jnp.float32(1), jnp.float32(0)
    iota_high = lax.broadcasted_iota(jnp.int32, (high_rows, count), 0)
    iota_low = lax.broadcasted_iota(jnp.int32, (LOW, count), 0)
    block = pl.ds(pl.multiple_of(step * ROWS_STEP, ROWS_STEP), ROWS_STEP)
    words = jnp.concatenate([places_ref[d, block, :] for d in range(blocks)], axis=1)
    locals_ = (words >> 16) - first
    weights = (words & (SHIFT - 1)).astype(jnp.float32) * (1 / LEVELS) * mass_row[...]
    for j in range(ROWS_STEP):
        local = locals_[j : j + 1, :]
        hot = jnp.where(iota_high == (local >> LOW_BITS), one, zero)
        low = jnp.where(iota_low == (local & (LOW - 1)), weights[j : j + 1, :], zero)
        part = lax.dot_general(
            hot.astype(jnp.bfloat16),
            low.astype(jnp.bfloat16),
            nt,
            preferred_element_type=jnp.float32,
        )
        row = pl.multiple_of((step * ROWS_STEP + j) * high_rows, 8)
        grid_ref[pl.ds(row, high_rows), :LOW] = part


def weight_rows(noise_ref, out_ref, grid_ref):
    side = noise_ref.shape[0]
    high_rows = grid_ref.shape[0] // side
    tn = (((0,), (0,)), ((), ()))
    noise = noise_ref[...].astype(jnp.bfloat16)
    for h in range(out_ref.shape[0] // LOW):
        high, low = split(grid_ref[pl.ds(h, side, stride=high_rows), :])
        block = lax.dot_general(
            high, noise, tn, preferred_element_type=jnp.float32
        ) + lax.dot_general(low, noise, tn, preferred_element_type=jnp.float32)
        out_ref[h * LOW : (h + 1) * LOW, :] = block[:LOW]


def gather_kernel(
    orient,
    images_ref,
    templates_ref,
    noise_ref,
    index_ref,
    interp_ref,
    gathered_ref,
    post_ref,
    mass_ref,
    words_ref,
    rows_ref,
    clash_ref,
    raw,
    weighted,
    whole,
    scores,
    norms,
    stats,
    landed,
    load_sem,
    store_sem,
    send_sem,
    recv_sem,
    stat_send,
    stat_recv,
):
    lines, across = LINES, orient // (2 * LINES)
    group, place = lax.axis_index("dp"), lax.axis_index("orient")
    core = lax.rem(place, 2)
    chip = lax.div(place, 2)
    row, col = lax.div(chip, across), lax.rem(chip, across)
    mesh_ids = pl.DeviceIdType.MESH
    block_rows, width = images_ref.shape
    part = width // PARTS
    count = templates_ref.shape[0]
    fold = templates_ref.shape[1] // width
    line_images = 2 * across * block_rows // fold
    images = line_images * lines

    def at(r, q, c):
        return (r * across + q) * 2 + c

    barrier = pltpu.get_barrier_semaphore()

    @pl.loop(1, orient)
    def _(s):
        pl.semaphore_signal(
            barrier,
            inc=1,
            device_id=(group, lax.rem(place + s, orient)),
            device_id_type=mesh_ids,
        )

    def load_copy(k):
        cols = pl.ds(pl.multiple_of(k * width, width), width)
        return pltpu.make_async_copy(
            templates_ref.at[:, cols], weighted.at[:, cols], load_sem.at[k]
        )

    for k in range(fold):
        load_copy(k).start()

    pl.semaphore_wait(barrier, orient - 1)

    def copy(source, r, q, s, way, target):
        cols = pl.ds(pl.multiple_of(s * part, part), part)
        slot = at(r, q, core)
        ref = images_ref if source is None else raw.at[slot]
        return pltpu.make_async_remote_copy(
            src_ref=ref.at[:, cols],
            dst_ref=raw.at[slot, :, cols],
            send_sem=send_sem.at[lax.div(slot, 2), s, way],
            recv_sem=recv_sem.at[slot, s],
            device_id=(group, target),
            device_id_type=mesh_ids,
        )

    def arrived(r, q, c, s):
        cols = pl.ds(pl.multiple_of(s * part, part), part)
        slot = at(r, q, c)
        pltpu.make_async_remote_copy(
            src_ref=raw.at[slot, :, cols],
            dst_ref=raw.at[slot, :, cols],
            send_sem=send_sem.at[0, 0, 0],
            recv_sem=recv_sem.at[slot, s],
            device_id=(group, place + 1 - 2 * core),
            device_id_type=mesh_ids,
        ).wait_recv()

    def each_send(r, q, s, act, source=raw):
        for way, step in ((0, 1), (1, -1)):
            onward = row + step
            if source is None:
                along = (onward >= 0) & (onward < lines)
            else:
                along = (q == col) & (onward >= 0) & (onward < lines) & ((row - r) * step > 0)

            @pl.when(along)
            def _(way=way, onward=onward):
                act(copy(source, r, q, s, way, at(onward, col, core)))

        for way, step in ((2, 1), (3, -1)):
            onward = col + step
            beside = (onward >= 0) & (onward < across) & ((col - q) * step >= 0)

            @pl.when(beside)
            def _(way=way, onward=onward):
                act(copy(source, r, q, s, way, at(row, onward, core)))

        act(copy(source, r, q, s, 4, place + 1 - 2 * core))

    @pl.loop(0, PARTS)
    def _(s):
        each_send(row, col, s, lambda c: c.start(), None)

    raw[place] = images_ref[...]
    scores[...] = jnp.zeros_like(scores)
    norms[...] = jnp.zeros_like(norms)

    index = index_ref[...]
    near = jnp.zeros(index.shape, jnp.int32)
    spot = lax.broadcasted_iota(jnp.int32, index.shape, 0) % SUB
    for d in range(1, SUB):
        same = (index == pltpu.roll(index, d, axis=0)) & (spot >= d)
        near = near | same.astype(jnp.int32)
    clash_ref[...] = jnp.zeros_like(clash_ref)
    for h in range(count // BATCH):
        clash_ref[h : h + 1, :] = jnp.max(
            near[h * BATCH : (h + 1) * BATCH, :], axis=0, keepdims=True
        )
    index_t = index.T
    for h in range(count // BATCH):
        rows_ref[pl.ds(h, index_t.shape[0], stride=count // BATCH), :] = index_t[
            :, h * BATCH : (h + 1) * BATCH
        ]
    level = (interp_ref[...] * LEVELS + 0.5).astype(jnp.int32)
    words_ref[...] = (index * SHIFT + level).T

    def weigh(k):
        load_copy(k).wait()

        @pl.loop(0, width // NORM_COLS)
        def _(g):
            cols = pl.ds(pl.multiple_of(k * width + g * NORM_COLS, NORM_COLS), NORM_COLS)
            for h in range(0, count, 64):
                tpl = weighted[h : h + 64, cols].astype(jnp.float32)
                noise = noise_ref[:, cols]
                scaled = tpl * noise
                square = tpl * tpl * noise
                total = square[:, :LANES]
                for j in range(1, NORM_COLS // LANES):
                    total = total + square[:, j * LANES : (j + 1) * LANES]
                norms[h : h + 64, :] += total
                weighted[h : h + 64, cols] = scaled.astype(jnp.bfloat16)

    def score(r, s):
        for q in range(across):
            arrived(r, q, 1 - core, s)
        cols = pl.ds(pl.multiple_of(s * part, part), part)
        slots = pl.ds(pl.multiple_of(r * (2 * across), 2 * across), 2 * across)
        block = raw[slots, :, cols].reshape(2 * across * block_rows, part)
        total = 2 * across * block_rows
        out_row = lax.broadcasted_iota(jnp.int32, (total, total), 0)
        from_row = lax.broadcasted_iota(jnp.int32, (total, total), 1)
        wanted = (out_row % line_images) * fold + out_row // line_images
        pick = jnp.where(from_row == wanted, 1.0, 0.0).astype(jnp.bfloat16)
        sorted_ = jnp.dot(pick, block, preferred_element_type=jnp.float32)
        sorted_ = sorted_.astype(jnp.bfloat16)
        rows = pl.ds(pl.multiple_of(r * line_images, line_images), line_images)
        added = scores[rows, :]
        for k in range(fold):
            piece = sorted_[k * line_images : (k + 1) * line_images, :]
            span = pl.ds(pl.multiple_of(k * width + s * part, part), part)
            whole[rows, span] = piece
            added = added + lax.dot_general(
                piece,
                weighted[:, span],
                (((1,), (1,)), ((), ())),
                preferred_element_type=jnp.float32,
            )
        scores[rows, :] = added

    def store_copy(r):
        rows = pl.ds(pl.multiple_of(r * line_images, line_images), line_images)
        return pltpu.make_async_copy(whole.at[rows], gathered_ref.at[rows], store_sem.at[r])

    def score_store(r, s):
        score(r, s)

        @pl.when(s == PARTS - 1)
        def _():
            store_copy(r).start()

    @pl.loop(0, lines * PARTS + 1)
    def _(k):
        n, s = lax.div(k, PARTS) + 1, lax.rem(k, PARTS)
        for sign in (1, -1):
            r = row + sign * n

            @pl.when((r >= 0) & (r < lines) & (n < lines))
            def _(r=r):
                arrived(r, col, core, s)
                each_send(r, col, s, lambda c: c.start())

        for sign in (1, -1):
            r = row + sign * (n - 1)
            live = (r >= 0) & (r < lines) & (n <= lines)
            if sign < 0:
                live = live & (n > 1)
            for e in range(1, across):
                for side in (1, -1):
                    q = col + side * e

                    @pl.when(live & (q >= 0) & (q < across))
                    def _(r=r, q=q):
                        arrived(r, q, core, s)
                        each_send(r, q, s, lambda c: c.start())

        @pl.when(n == 1)
        def _():
            @pl.loop(0, fold // PARTS)
            def _(j):
                weigh(s * (fold // PARTS) + j)

        last = jnp.maximum(k - 1, 0)
        m, t = lax.div(last, PARTS) + 1, lax.rem(last, PARTS)

        @pl.when((m == 2) & (k > 0))
        def _():
            score_store(row, t)

        for sign in (1, -1):
            r = row + sign * (m - 1)

            @pl.when((m > 1) & (r >= 0) & (r < lines))
            def _(r=r):
                score_store(r, t)

    norm = 0.5 * jnp.sum(norms[...].T, axis=0, keepdims=True)
    value = (scores[...] - norm).T
    peak_own = jnp.max(value, axis=0, keepdims=True)
    expo = jnp.exp(value - peak_own)
    stats[...] = jnp.zeros_like(stats)
    stats[0:1, :] = peak_own
    stats[1:2, :] = jnp.sum(expo, axis=0, keepdims=True)

    def stat_copy(s):
        return pltpu.make_async_remote_copy(
            src_ref=stats,
            dst_ref=landed.at[s],
            send_sem=stat_send.at[s],
            recv_sem=stat_recv.at[s],
            device_id=(group, lax.rem(place + s, orient)),
            device_id_type=mesh_ids,
        )

    @pl.loop(1, orient)
    def _(s):
        stat_copy(s).start()

    landed[0] = stats[...]

    @pl.loop(1, orient)
    def _(s):
        stat_copy(s).wait()

    peak = peak_own
    for s in range(1, orient):
        peak = jnp.maximum(peak, landed[s, 0:1, :])
    total = jnp.zeros_like(peak)
    for s in range(orient):
        total = total + landed[s, 1:2, :] * jnp.exp(landed[s, 0:1, :] - peak)
    posterior = (expo * (jnp.exp(peak_own - peak) / total))[:, :images]
    post_ref[...] = posterior.astype(jnp.bfloat16)
    mass = jnp.sum(posterior, axis=1, keepdims=True)
    mass_t = jnp.broadcast_to(mass, (count, LANES)).T
    for h in range(count // LANES):
        mass_ref[h : h + 1, :] = mass_t[:1, h * LANES : (h + 1) * LANES]

    for r in range(lines):
        store_copy(r).wait()

    @pl.loop(0, PARTS)
    def _(s):
        each_send(row, col, s, lambda c: c.wait_send(), None)
        for r in range(lines):
            for q in range(across):

                @pl.when((row != r) | (col != q))
                def _(r=r, q=q):
                    each_send(r, q, s, lambda c: c.wait_send())


def gather_scores(images, templates, index, interp, noise_flat, orient):
    own, pixels = images.shape
    count, side = index.shape
    fold = PARTS
    while own * fold % 16:
        fold += PARTS
    width = pixels // fold
    total = own * orient
    padded = -(-total // LANES) * LANES
    vmem = pl.BlockSpec(memory_space=pltpu.VMEM)
    hbm = pl.BlockSpec(memory_space=pl.ANY)
    chips = orient // 2
    return pl.pallas_call(
        functools.partial(gather_kernel, orient),
        out_shape=(
            jax.ShapeDtypeStruct((total, pixels), jnp.bfloat16),
            jax.ShapeDtypeStruct((count, total), jnp.bfloat16),
            jax.ShapeDtypeStruct((count // LANES, LANES), jnp.float32),
            jax.ShapeDtypeStruct((side, count), jnp.int32),
            jax.ShapeDtypeStruct((side * count // BATCH, BATCH), jnp.int32),
            jax.ShapeDtypeStruct((8, side), jnp.int32),
        ),
        in_specs=[vmem, hbm, vmem, vmem, vmem],
        out_specs=(hbm, vmem, vmem, vmem, vmem, vmem),
        scratch_shapes=[
            pltpu.VMEM((orient, own * fold, width), jnp.bfloat16),
            pltpu.VMEM((count, pixels), jnp.bfloat16),
            pltpu.VMEM((total, pixels), jnp.bfloat16),
            pltpu.VMEM((padded, count), jnp.float32),
            pltpu.VMEM((count, LANES), jnp.float32),
            pltpu.VMEM((8, padded), jnp.float32),
            pltpu.VMEM((orient, 8, padded), jnp.float32),
            pltpu.SemaphoreType.DMA((fold,)),
            pltpu.SemaphoreType.DMA((LINES,)),
            pltpu.SemaphoreType.DMA((chips, PARTS, 5)),
            pltpu.SemaphoreType.DMA((orient, PARTS)),
            pltpu.SemaphoreType.DMA((orient,)),
            pltpu.SemaphoreType.DMA((orient,)),
        ],
        compiler_params=pltpu.CompilerParams(
            collective_id=1, has_side_effects=True, vmem_limit_bytes=VMEM_LIMIT
        ),
    )(images.reshape(own * fold, width), templates, noise_flat, index, interp)


def shards(groups, orient, images, templates, index, interp, inv_noise):
    side = inv_noise.shape[0]
    gathered, post, mass, words, voxels, clash = gather_scores(
        images, templates, index, interp, inv_noise.reshape(1, -1), orient
    )
    places = lax.all_gather(words, "orient", axis=0)
    volume = insert_data(post, gathered, interp, voxels, clash, side * side)
    return reduce_rows(
        volume, mass, places, inv_noise, groups, orient
    )


def solution(mesh):
    placed = (
        P(("dp", "orient"), None),
        P("orient", None),
        P("orient", None),
        P("orient", None),
        P(),
    )
    return jax.shard_map(
        functools.partial(shards, mesh.shape["dp"], mesh.shape["orient"]),
        mesh=mesh,
        in_specs=placed,
        out_specs=(P(("dp", "orient"), None), P(("dp", "orient"), None)),
        check_vma=False,
    )
```

```python
import functools

import jax
import jax.numpy as jnp
from jax import lax
from jax.experimental import pallas as pl
from jax.experimental.pallas import tpu as pltpu
from jax.sharding import PartitionSpec as P

LANES = 128
ROWS_STEP = 8
ACCS = 4
SUB = 4
BATCH = 128
LINES = 4
PARTS = 4
NORM_COLS = 1024
LEVELS = 65535
SHIFT = 65536
LOW_BITS = 6
LOW = 1 << LOW_BITS
VMEM_LIMIT = 56 * 2**20


def data_kernel(post_ref, images_ref, interp_ref, idx_ref, clash_ref, out_ref, rows_ref, *more):
    accs = (out_ref,) + more
    step = pl.program_id(0)
    count, side = post_ref.shape[0], out_ref.shape[1]
    volume_rows = out_ref.shape[0]
    halves = count // BATCH

    @pl.when(step == 0)
    def _():
        @pl.loop(0, volume_rows // 64)
        def _(c):
            rows = pl.ds(pl.multiple_of(c * 64, 64), 64)
            for acc in accs:
                acc[rows, :] = jnp.zeros((64, side), jnp.float32)

    interp = pltpu.roll(interp_ref[...], lax.rem(side - step * ROWS_STEP, side), axis=1)
    for j in range(ROWS_STEP):
        block = jnp.dot(
            post_ref[...],
            images_ref[:, j * side : (j + 1) * side],
            preferred_element_type=jnp.float32,
        )
        rows_ref[j * count : (j + 1) * count, :] = block * interp[:, j : j + 1]

    @pl.loop(0, ROWS_STEP * halves)
    def _(g):
        base = pl.multiple_of(g * BATCH, BATCH)
        voxels = idx_ref.at[g]
        clash = clash_ref[lax.rem(g, halves), step * ROWS_STEP + lax.div(g, halves)]

        @pl.when(clash == 0)
        def _():
            pending = [None] * ACCS

            def flush(a):
                for voxel, value in pending[a] or ():
                    accs[a][pl.ds(voxel, 1), :] = value

            for n in range(BATCH // SUB):
                a = n % ACCS
                flush(a)
                pending[a] = []
                for k in range(n * SUB, (n + 1) * SUB):
                    voxel = voxels[k]
                    value = accs[a][pl.ds(voxel, 1), :] + rows_ref[pl.ds(base + k, 1), :]
                    pending[a].append((voxel, value))
            for a in range(ACCS):
                flush(a)

        @pl.when(clash != 0)
        def _():
            @pl.loop(0, BATCH // ACCS)
            def _(q):
                first = q * ACCS
                targets = [voxels[first + a] for a in range(ACCS)]
                summed = [
                    accs[a][pl.ds(targets[a], 1), :]
                    + rows_ref[pl.ds(base + first + a, 1), :]
                    for a in range(ACCS)
                ]
                for a in range(ACCS):
                    accs[a][pl.ds(targets[a], 1), :] = summed[a]

    @pl.when(step == pl.num_programs(0) - 1)
    def _():
        @pl.loop(0, volume_rows // 64)
        def _(c):
            rows = pl.ds(pl.multiple_of(c * 64, 64), 64)
            total = accs[0][rows, :]
            for acc in accs[1:]:
                total = total + acc[rows, :]
            out_ref[rows, :] = total


def insert_data(post, gathered, interp, voxels, clash, volume_rows):
    count, images = post.shape
    side = interp.shape[1]
    steps = side // ROWS_STEP
    batches = ROWS_STEP * count // BATCH
    return pl.pallas_call(
        data_kernel,
        grid=(steps,),
        out_shape=jax.ShapeDtypeStruct((volume_rows, side), jnp.float32),
        in_specs=[
            pl.BlockSpec((count, images), lambda i: (0, 0)),
            pl.BlockSpec((images, ROWS_STEP * side), lambda i: (0, i)),
            pl.BlockSpec((count, side), lambda i: (0, 0)),
            pl.BlockSpec((batches, BATCH), lambda i: (i, 0), memory_space=pltpu.SMEM),
            pl.BlockSpec(memory_space=pltpu.SMEM),
        ],
        out_specs=pl.BlockSpec(
            (volume_rows, side), lambda i: (0, 0), pipeline_mode=pl.Buffered(1)
        ),
        scratch_shapes=[pltpu.VMEM((ROWS_STEP * count, side), jnp.float32)]
        + [pltpu.VMEM((volume_rows, side), jnp.float32)] * (ACCS - 1),
        compiler_params=pltpu.CompilerParams(vmem_limit_bytes=VMEM_LIMIT),
        cost_estimate=pl.CostEstimate(
            flops=200_000_000_000, bytes_accessed=200_000_000, transcendentals=0
        ),
    )(post, gathered, interp, voxels, clash)


def reduce_kernel(
    groups,
    orient,
    blocks_ref,
    mass_ref,
    places_ref,
    noise_ref,
    out_ref,
    weight_ref,
    grid_ref,
    mass_row,
    mine,
    theirs,
    first_x,
    first_x_in,
    first_y,
    first_y_in,
    second_x,
    second_x_in,
    second_y,
    second_y_in,
    last,
    last_in,
    masses,
    twin,
    twin_in,
    own_sem,
    pair_send,
    pair_recv,
    fx_send,
    fx_recv,
    fy_send,
    fy_recv,
    sx_send,
    sx_recv,
    sy_send,
    sy_recv,
    last_send,
    last_recv,
    mass_send,
    mass_recv,
    twin_send,
    twin_recv,
):
    lines, across = LINES, orient // (2 * LINES)
    devices = groups * orient
    group, place = lax.axis_index("dp"), lax.axis_index("orient")
    core, chip = lax.rem(place, 2), lax.div(place, 2)
    row, col = lax.div(chip, across), lax.rem(chip, across)
    rank = group * orient + place
    half = out_ref.shape[0] // 2
    mesh_ids = pl.DeviceIdType.MESH

    def ranked(d):
        return (lax.div(d, orient), lax.rem(d, orient))

    def line(k):
        return lax.rem(row + k + 1, lines)

    def group_at(i):
        return lax.rem(group + i, groups)

    def col_at(j):
        return lax.rem(col + j, across)

    def block(x, r, q):
        return (x * lines + r) * across + q

    def remote(source, target, send, recv, x, r, q, c):
        return pltpu.make_async_remote_copy(
            src_ref=source,
            dst_ref=target,
            send_sem=send,
            recv_sem=recv,
            device_id=(x, (r * across + q) * 2 + c),
            device_id_type=mesh_ids,
        )

    barrier = pltpu.get_barrier_semaphore()

    @pl.loop(1, devices)
    def _(s):
        pl.semaphore_signal(
            barrier,
            inc=1,
            device_id=ranked(lax.rem(rank + s, devices)),
            device_id_type=mesh_ids,
        )

    def own_copy(k, i, j):
        p = block(group_at(i), line(k), col_at(j))
        return pltpu.make_async_copy(
            blocks_ref.at[p, core], mine.at[p], own_sem.at[k, i * across + j]
        )

    for i in reversed(range(groups)):
        for j in reversed(range(across)):

            @pl.loop(0, lines)
            def _(k, i=i, j=j):
                own_copy(k, i, j).start()

    pl.semaphore_wait(barrier, devices - 1)

    def mass_copy(s):
        return pltpu.make_async_remote_copy(
            src_ref=mass_ref,
            dst_ref=masses.at[s],
            send_sem=mass_send.at[s],
            recv_sem=mass_recv.at[s],
            device_id=ranked(lax.rem(rank + s, devices)),
            device_id_type=mesh_ids,
        )

    def pair_copy(k, i, j):
        p, n = block(group_at(i), line(k), col_at(j)), i * across + j
        return remote(
            blocks_ref.at[p, 1 - core],
            theirs.at[p],
            pair_send.at[k, n],
            pair_recv.at[k, n],
            group,
            row,
            col,
            1 - core,
        )

    def first_x_copy(k, i):
        return remote(
            first_x.at[i - 1, k],
            first_x_in.at[i - 1, k],
            fx_send.at[i - 1, k],
            fx_recv.at[i - 1, k],
            group_at(i),
            row,
            col,
            core,
        )

    def first_y_copy(k, j):
        return remote(
            first_y.at[j - 1, k],
            first_y_in.at[j - 1, k],
            fy_send.at[j - 1, k],
            fy_recv.at[j - 1, k],
            group,
            row,
            col_at(j),
            core,
        )

    def second_x_copy(k, i):
        return remote(
            second_x.at[i - 1, k],
            second_x_in.at[i - 1, k],
            sx_send.at[i - 1, k],
            sx_recv.at[i - 1, k],
            group_at(i),
            row,
            col,
            core,
        )

    def second_y_copy(k, j):
        return remote(
            second_y.at[j - 1, k],
            second_y_in.at[j - 1, k],
            sy_send.at[j - 1, k],
            sy_recv.at[j - 1, k],
            group,
            row,
            col_at(j),
            core,
        )

    def last_copy(k):
        return remote(
            last.at[k],
            last_in.at[k],
            last_send.at[k],
            last_recv.at[k],
            group,
            line(k),
            col,
            core,
        )

    @pl.loop(0, lines)
    def _(k):
        for i in reversed(range(groups)):
            for j in reversed(range(across)):
                pair_copy(k, i, j).start()

    twin_group = group + 1 - 2 * lax.rem(group, 2)

    def mass_sent(s):
        return lax.rem(lax.div(lax.rem(rank + s, devices), orient), 2) == core

    @pl.loop(1, devices)
    def _(s):
        @pl.when(mass_sent(s))
        def _():
            mass_copy(s).start()

    def narrow(value):
        return value.astype(jnp.bfloat16)

    def begin(k):
        for i in reversed(range(groups)):
            for j in reversed(range(across)):
                x, q = group_at(i), col_at(j)
                p = block(x, line(k), q)
                own_copy(k, i, j).wait()
                pair_copy(k, i, j).wait()
                if i == 0 or j == 0:
                    total = mine[p] + theirs[p]
                    mine[p] = total
                    if i:
                        first_x[i - 1, k, q] = narrow(total[:half])
                    if j:
                        first_y[j - 1, k, x] = narrow(total[half:])
                else:
                    first_x[i - 1, k, q] = narrow(mine[p, :half] + theirs[p, :half])
                    first_y[j - 1, k, x] = narrow(mine[p, half:] + theirs[p, half:])
            if i:
                first_x_copy(k, i).start()
        for j in range(1, across):
            first_y_copy(k, j).start()

    def middle(k):
        for i in range(1, groups):
            first_x_copy(k, i).wait()
        for j in reversed(range(across)):
            q = col_at(j)
            p = block(group, line(k), q)
            total = mine[p, :half]
            for i in range(1, groups):
                total = total + first_x_in[i - 1, k, q].astype(jnp.float32)
            if j:
                second_y[j - 1, k] = narrow(total)
                second_y_copy(k, j).start()
            else:
                mine[p, :half] = total
        for j in range(1, across):
            first_y_copy(k, j).wait()
        for i in reversed(range(groups)):
            x = group_at(i)
            p = block(x, line(k), col)
            total = mine[p, half:]
            for j in range(1, across):
                total = total + first_y_in[j - 1, k, x].astype(jnp.float32)
            if i:
                second_x[i - 1, k] = narrow(total)
                second_x_copy(k, i).start()
            else:
                mine[p, half:] = total

    def end(k):
        p = block(group, line(k), col)
        for j in range(1, across):
            second_y_copy(k, j).wait()
        top = mine[p, :half]
        for j in range(1, across):
            top = top + second_y_in[j - 1, k].astype(jnp.float32)
        for i in range(1, groups):
            second_x_copy(k, i).wait()
        low = mine[p, half:]
        for i in range(1, groups):
            low = low + second_x_in[i - 1, k].astype(jnp.float32)

        @pl.when(k < lines - 1)
        def _():
            last[k, :half] = narrow(top)
            last[k, half:] = narrow(low)
            last_copy(k).start()

        @pl.when(k == lines - 1)
        def _():
            out_ref[:half] = top
            out_ref[half:] = low

    mass_row[...] = jnp.zeros_like(mass_row)
    mass_rows = mass_ref.shape[0]

    def add_mass(d, ref):
        start = lax.div(lax.rem(d, orient), 2) * (mass_rows * LANES)
        for k in range(mass_rows):
            lanes = pl.ds(pl.multiple_of(start + k * LANES, LANES), LANES)
            mass_row[:, lanes] += ref[k : k + 1, :]

    steps, slots = noise_ref.shape[0] // ROWS_STEP, 3 * (lines + 2)

    def weigh(w):
        rows = out_ref.shape[0]
        firsts = (rank * rows, (twin_group * orient + place) * rows)
        weight_step(w, firsts, places_ref, mass_row, grid_ref)

    @pl.loop(0, slots)
    def _(slot):
        k, turn = lax.div(slot, 3), lax.rem(slot, 3)

        @pl.when((turn == 0) & (k < lines))
        def _():
            begin(k)

        @pl.when((turn == 1) & (k >= 1) & (k < lines + 1))
        def _():
            middle(k - 1)

        @pl.when((turn == 2) & (k >= 2))
        def _():
            end(k - 2)

        @pl.when(slot == 1)
        def _():
            @pl.when(core == lax.rem(group, 2))
            def _():
                add_mass(rank, mass_ref)

            @pl.loop(1, devices)
            def _(s):
                sender = lax.rem(rank + devices - s, devices)

                @pl.when(lax.rem(sender, 2) == lax.rem(group, 2))
                def _():
                    mass_copy(s).wait_recv()
                    add_mass(sender, masses.at[s])

                @pl.when(mass_sent(s))
                def _():
                    mass_copy(s).wait_send()

        @pl.when((slot >= 2) & (slot < 2 + steps))
        def _():
            weigh(slot - 2)

    @pl.loop(slots - 2, max(steps, slots - 2))
    def _(w):
        weigh(w)

    weight_rows(noise_ref, twin, grid_ref, 1)
    exchange = remote(
        twin, twin_in, twin_send, twin_recv, twin_group, row, col, core
    )
    exchange.start()
    weight_rows(noise_ref, weight_ref, grid_ref, 0)
    for k in range(lines - 1):
        last_copy(k).wait()
        out_ref[...] += last_in[k].astype(jnp.float32)
    exchange.wait()
    weight_ref[...] += twin_in[...].astype(jnp.float32)


def reduce_rows(volume, mass_rows, places_t, inv_noise, groups, orient):
    chips = groups * orient // 2
    lines, across = LINES, orient // (2 * LINES)
    rows, side = volume.shape[0] // (2 * chips), volume.shape[1]
    half = rows // 2
    parts = (chips, rows, side)
    masses = (2 * chips,) + mass_rows.shape
    shapes = [
        (groups - 1, lines, across, half, side),
        (across - 1, lines, groups, half, side),
        (groups - 1, lines, half, side),
        (across - 1, lines, half, side),
        (lines - 1, rows, side),
    ]
    sems = [
        (groups - 1, lines),
        (across - 1, lines),
        (groups - 1, lines),
        (across - 1, lines),
        (lines - 1,),
        (2 * chips,),
    ]
    return pl.pallas_call(
        functools.partial(reduce_kernel, groups, orient),
        out_shape=(
            jax.ShapeDtypeStruct((rows, side), jnp.float32),
            jax.ShapeDtypeStruct((rows, side), jnp.float32),
        ),
        in_specs=[pl.BlockSpec(memory_space=pl.ANY)]
        + [pl.BlockSpec(memory_space=pltpu.VMEM)] * 3,
        out_specs=(
            pl.BlockSpec(memory_space=pltpu.VMEM),
            pl.BlockSpec(memory_space=pltpu.VMEM),
        ),
        scratch_shapes=[
            pltpu.VMEM((2 * side * max(8, rows // LOW), LANES), jnp.float32),
            pltpu.VMEM((1, places_t.shape[0] * places_t.shape[2]), jnp.float32),
        ]
        + [pltpu.VMEM(parts, jnp.float32)] * 2
        + [pltpu.VMEM(s, jnp.bfloat16) for s in shapes for _ in range(2)]
        + [pltpu.VMEM(masses, jnp.float32)]
        + [pltpu.VMEM((rows, side), jnp.bfloat16)] * 2
        + [pltpu.SemaphoreType.DMA((lines, groups * across))] * 3
        + [pltpu.SemaphoreType.DMA(s) for s in sems for _ in range(2)]
        + [pltpu.SemaphoreType.DMA] * 2,
        compiler_params=pltpu.CompilerParams(
            collective_id=0, has_side_effects=True, vmem_limit_bytes=VMEM_LIMIT
        ),
    )(volume.reshape(chips, 2, rows, side), mass_rows, places_t, inv_noise)


def split(value):
    high = value.astype(jnp.bfloat16)
    return high, (value - high.astype(jnp.float32)).astype(jnp.bfloat16)


def weight_step(step, firsts, places_ref, mass_row, grid_ref):
    blocks, side, each = places_ref.shape
    count = blocks * each
    high_rows = grid_ref.shape[0] // side
    nt = (((1,), (1,)), ((), ()))
    one, zero = jnp.float32(1), jnp.float32(0)
    spot = lax.broadcasted_iota(jnp.int32, (high_rows, count), 0)
    each_high = high_rows // 2
    iota_high = jnp.where(
        spot < each_high,
        (firsts[0] >> LOW_BITS) + spot,
        (firsts[1] >> LOW_BITS) + spot - each_high,
    )
    iota_low = lax.broadcasted_iota(jnp.int32, (LOW, count), 0)
    block = pl.ds(pl.multiple_of(step * ROWS_STEP, ROWS_STEP), ROWS_STEP)
    words = jnp.concatenate([places_ref[d, block, :] for d in range(blocks)], axis=1)
    voxels = words >> 16
    weights = (words & (SHIFT - 1)).astype(jnp.float32) * (1 / LEVELS) * mass_row[...]
    for j in range(ROWS_STEP):
        local = voxels[j : j + 1, :]
        hot = jnp.where(iota_high == (local >> LOW_BITS), one, zero)
        low = jnp.where(iota_low == (local & (LOW - 1)), weights[j : j + 1, :], zero)
        part = lax.dot_general(
            hot.astype(jnp.bfloat16),
            low.astype(jnp.bfloat16),
            nt,
            preferred_element_type=jnp.float32,
        )
        row = pl.multiple_of((step * ROWS_STEP + j) * high_rows, 8)
        grid_ref[pl.ds(row, high_rows), :LOW] = part


def weight_rows(noise_ref, out_ref, grid_ref, part):
    side = noise_ref.shape[0]
    high_rows = grid_ref.shape[0] // side
    tn = (((0,), (0,)), ((), ()))
    noise = noise_ref[...].astype(jnp.bfloat16)
    for h in range(out_ref.shape[0] // LOW):
        first = part * (high_rows // 2) + h
        high, low = split(grid_ref[pl.ds(first, side, stride=high_rows), :])
        block = lax.dot_general(
            high, noise, tn, preferred_element_type=jnp.float32
        ) + lax.dot_general(low, noise, tn, preferred_element_type=jnp.float32)
        out_ref[h * LOW : (h + 1) * LOW, :] = block[:LOW].astype(out_ref.dtype)


def gather_kernel(
    orient,
    own_ref,
    templates_ref,
    noise_ref,
    index_ref,
    interp_ref,
    gathered_ref,
    post_ref,
    mass_ref,
    places_ref,
    rows_ref,
    clash_ref,
    images_ref,
    wide,
    words,
    words_in,
    raw,
    weighted,
    whole,
    scores,
    norms,
    stats,
    landed,
    load_sem,
    store_sem,
    send_sem,
    recv_sem,
    stat_send,
    stat_recv,
    word_send,
    word_recv,
):
    lines, across = LINES, orient // (2 * LINES)
    group, place = lax.axis_index("dp"), lax.axis_index("orient")
    core = lax.rem(place, 2)
    chip = lax.div(place, 2)
    row, col = lax.div(chip, across), lax.rem(chip, across)
    mesh_ids = pl.DeviceIdType.MESH
    block_rows, width = images_ref.shape
    part = width // PARTS
    count = templates_ref.shape[0]
    fold = templates_ref.shape[1] // width
    line_images = 2 * across * block_rows // fold
    images = line_images * lines

    def at(r, q, c):
        return (r * across + q) * 2 + c

    barrier = pltpu.get_barrier_semaphore()

    @pl.loop(1, orient)
    def _(s):
        pl.semaphore_signal(
            barrier,
            inc=1,
            device_id=(group, lax.rem(place + s, orient)),
            device_id_type=mesh_ids,
        )

    def load_copy(k):
        cols = pl.ds(pl.multiple_of(k * width, width), width)
        return pltpu.make_async_copy(
            templates_ref.at[:, cols], weighted.at[:, cols], load_sem.at[k]
        )

    for k in range(fold):
        load_copy(k).start()

    own_rows = own_ref.shape[0]
    for k in range(fold):
        wide[k * own_rows : (k + 1) * own_rows, :] = own_ref[
            :, k * width : (k + 1) * width
        ].astype(jnp.float32)
    images_ref[...] = wide[...].astype(jnp.bfloat16)
    pl.semaphore_wait(barrier, orient - 1)

    def copy(source, r, q, s, way, target):
        cols = pl.ds(pl.multiple_of(s * part, part), part)
        slot = at(r, q, core)
        ref = images_ref if source is None else raw.at[slot]
        return pltpu.make_async_remote_copy(
            src_ref=ref.at[:, cols],
            dst_ref=raw.at[slot, :, cols],
            send_sem=send_sem.at[lax.div(slot, 2), s, way],
            recv_sem=recv_sem.at[slot, s],
            device_id=(group, target),
            device_id_type=mesh_ids,
        )

    def arrived(r, q, c, s):
        cols = pl.ds(pl.multiple_of(s * part, part), part)
        slot = at(r, q, c)
        pltpu.make_async_remote_copy(
            src_ref=raw.at[slot, :, cols],
            dst_ref=raw.at[slot, :, cols],
            send_sem=send_sem.at[0, 0, 0],
            recv_sem=recv_sem.at[slot, s],
            device_id=(group, place + 1 - 2 * core),
            device_id_type=mesh_ids,
        ).wait_recv()

    def each_send(r, q, s, act, source=raw):
        for way, step in ((0, 1), (1, -1)):
            onward = row + step
            if source is None:
                along = (onward >= 0) & (onward < lines)
            else:
                along = (q == col) & (onward >= 0) & (onward < lines) & ((row - r) * step > 0)

            @pl.when(along)
            def _(way=way, onward=onward):
                act(copy(source, r, q, s, way, at(onward, col, core)))

        for way, step in ((2, 1), (3, -1)):
            onward = col + step
            beside = (onward >= 0) & (onward < across) & ((col - q) * step >= 0)

            @pl.when(beside)
            def _(way=way, onward=onward):
                act(copy(source, r, q, s, way, at(row, onward, core)))

        act(copy(source, r, q, s, 4, place + 1 - 2 * core))

    @pl.loop(0, PARTS)
    def _(s):
        each_send(row, col, s, lambda c: c.start(), None)

    raw[place] = images_ref[...]
    scores[...] = jnp.zeros_like(scores)
    norms[...] = jnp.zeros_like(norms)

    index = index_ref[...]
    near = jnp.zeros(index.shape, jnp.int32)
    spot = lax.broadcasted_iota(jnp.int32, index.shape, 0) % SUB
    for d in range(1, SUB):
        same = (index == pltpu.roll(index, d, axis=0)) & (spot >= d)
        near = near | same.astype(jnp.int32)
    clash_ref[...] = jnp.zeros_like(clash_ref)
    for h in range(count // BATCH):
        clash_ref[h : h + 1, :] = jnp.max(
            near[h * BATCH : (h + 1) * BATCH, :], axis=0, keepdims=True
        )
    index_t = index.T
    for h in range(count // BATCH):
        rows_ref[pl.ds(h, index_t.shape[0], stride=count // BATCH), :] = index_t[
            :, h * BATCH : (h + 1) * BATCH
        ]
    level = (interp_ref[...] * LEVELS + 0.5).astype(jnp.int32)
    words[...] = (index * SHIFT + level).T

    bearer = lax.rem(group, 2) == core

    def word_copy(source, r, q, way, target):
        slot = r * across + q
        return pltpu.make_async_remote_copy(
            src_ref=words if source is None else words_in.at[slot],
            dst_ref=words_in.at[slot],
            send_sem=word_send.at[slot, way],
            recv_sem=word_recv.at[slot],
            device_id=(group, target),
            device_id_type=mesh_ids,
        )

    def word_arrived(r, q):
        word_copy(words_in, r, q, 0, place + 1 - 2 * core).wait_recv()

    def each_word(r, q, act, source=words_in):
        for way, step in ((0, 1), (1, -1)):
            onward = row + step
            along = (onward >= 0) & (onward < lines)
            if source is not None:
                along = (q == col) & along & ((row - r) * step > 0)

            @pl.when(along)
            def _(way=way, onward=onward):
                act(word_copy(source, r, q, way, at(onward, col, core)))

        for way, step in ((2, 1), (3, -1)):
            onward = col + step
            beside = (onward >= 0) & (onward < across) & ((col - q) * step >= 0)

            @pl.when(beside)
            def _(way=way, onward=onward):
                act(word_copy(source, r, q, way, at(row, onward, core)))

        act(word_copy(source, r, q, 4, place + 1 - 2 * core))

    def weigh(k):
        load_copy(k).wait()

        @pl.loop(0, width // NORM_COLS)
        def _(g):
            cols = pl.ds(pl.multiple_of(k * width + g * NORM_COLS, NORM_COLS), NORM_COLS)
            for h in range(0, count, 64):
                tpl = weighted[h : h + 64, cols].astype(jnp.float32)
                noise = noise_ref[:, cols]
                scaled = tpl * noise
                square = tpl * tpl * noise
                total = square[:, :LANES]
                for j in range(1, NORM_COLS // LANES):
                    total = total + square[:, j * LANES : (j + 1) * LANES]
                norms[h : h + 64, :] += total
                weighted[h : h + 64, cols] = scaled.astype(jnp.bfloat16)

    def score(r, s):
        for q in range(across):
            arrived(r, q, 1 - core, s)
        cols = pl.ds(pl.multiple_of(s * part, part), part)
        slots = pl.ds(pl.multiple_of(r * (2 * across), 2 * across), 2 * across)
        block = raw[slots, :, cols].reshape(2 * across * block_rows, part)
        total = 2 * across * block_rows
        out_row = lax.broadcasted_iota(jnp.int32, (total, total), 0)
        from_row = lax.broadcasted_iota(jnp.int32, (total, total), 1)
        image, piece = out_row % line_images, out_row // line_images
        wanted = (image // own_rows) * block_rows + piece * own_rows + image % own_rows
        pick = jnp.where(from_row == wanted, 1.0, 0.0).astype(jnp.bfloat16)
        sorted_ = jnp.dot(pick, block, preferred_element_type=jnp.float32)
        sorted_ = sorted_.astype(jnp.bfloat16)
        rows = pl.ds(pl.multiple_of(r * line_images, line_images), line_images)
        added = scores[rows, :]
        for k in range(fold):
            piece = sorted_[k * line_images : (k + 1) * line_images, :]
            span = pl.ds(pl.multiple_of(k * width + s * part, part), part)
            whole[rows, span] = piece
            added = added + lax.dot_general(
                piece,
                weighted[:, span],
                (((1,), (1,)), ((), ())),
                preferred_element_type=jnp.float32,
            )
        scores[rows, :] = added

    def store_copy(r):
        rows = pl.ds(pl.multiple_of(r * line_images, line_images), line_images)
        return pltpu.make_async_copy(whole.at[rows], gathered_ref.at[rows], store_sem.at[r])

    def score_store(r, s):
        score(r, s)

        @pl.when(s == PARTS - 1)
        def _():
            store_copy(r).start()

    @pl.loop(0, lines * PARTS + 1)
    def _(k):
        n, s = lax.div(k, PARTS) + 1, lax.rem(k, PARTS)
        for sign in (1, -1):
            r = row + sign * n

            @pl.when((r >= 0) & (r < lines) & (n < lines))
            def _(r=r):
                arrived(r, col, core, s)
                each_send(r, col, s, lambda c: c.start())

        for sign in (1, -1):
            r = row + sign * (n - 1)
            live = (r >= 0) & (r < lines) & (n <= lines)
            if sign < 0:
                live = live & (n > 1)
            for e in range(1, across):
                for side in (1, -1):
                    q = col + side * e

                    @pl.when(live & (q >= 0) & (q < across))
                    def _(r=r, q=q):
                        arrived(r, q, core, s)
                        each_send(r, q, s, lambda c: c.start())

        @pl.when(n == 1)
        def _():
            @pl.loop(0, fold // PARTS)
            def _(j):
                weigh(s * (fold // PARTS) + j)

        @pl.when(bearer & (n == lines) & (s == 0))
        def _():
            each_word(row, col, lambda c: c.start(), None)

        for sign in (1, -1):
            r = row + sign * s

            @pl.when(bearer & (n == lines) & (s > 0) & (r >= 0) & (r < lines))
            def _(r=r):
                word_arrived(r, col)
                each_word(r, col, lambda c: c.start())

        last = jnp.maximum(k - 1, 0)
        m, t = lax.div(last, PARTS) + 1, lax.rem(last, PARTS)

        @pl.when((m == 2) & (k > 0))
        def _():
            score_store(row, t)

        for sign in (1, -1):
            r = row + sign * (m - 1)

            @pl.when((m > 1) & (r >= 0) & (r < lines))
            def _(r=r):
                score_store(r, t)

    norm = 0.5 * jnp.sum(norms[...].T, axis=0, keepdims=True)
    value = (scores[...] - norm).T
    peak_own = jnp.max(value, axis=0, keepdims=True)
    expo = jnp.exp(value - peak_own)
    stats[...] = jnp.zeros_like(stats)
    stats[0:1, :] = peak_own
    stats[1:2, :] = jnp.sum(expo, axis=0, keepdims=True)

    def stat_copy(s):
        return pltpu.make_async_remote_copy(
            src_ref=stats,
            dst_ref=landed.at[s],
            send_sem=stat_send.at[s],
            recv_sem=stat_recv.at[s],
            device_id=(group, lax.rem(place + s, orient)),
            device_id_type=mesh_ids,
        )

    @pl.loop(1, orient)
    def _(s):
        stat_copy(s).start()

    landed[0] = stats[...]

    @pl.when(bearer)
    def _():
        for e in range(1, across):
            for side in (1, -1):
                for d in range(lines):
                    for sign in (1, -1) if d else (1,):
                        r, q = row + sign * d, col + side * e

                        @pl.when((r >= 0) & (r < lines) & (q >= 0) & (q < across))
                        def _(r=r, q=q):
                            word_arrived(r, q)
                            each_word(r, q, lambda c: c.start())

        words_in[row * across + col] = words[...]

    @pl.loop(1, orient)
    def _(s):
        stat_copy(s).wait()

    peak = peak_own
    for s in range(1, orient):
        peak = jnp.maximum(peak, landed[s, 0:1, :])
    total = jnp.zeros_like(peak)
    for s in range(orient):
        total = total + landed[s, 1:2, :] * jnp.exp(landed[s, 0:1, :] - peak)
    posterior = (expo * (jnp.exp(peak_own - peak) / total))[:, :images]
    post_ref[...] = posterior.astype(jnp.bfloat16)
    mass = jnp.sum(posterior, axis=1, keepdims=True)
    mass_t = jnp.broadcast_to(mass, (count, LANES)).T
    for h in range(count // LANES):
        mass_ref[h : h + 1, :] = mass_t[:1, h * LANES : (h + 1) * LANES]

    @pl.when(jnp.logical_not(bearer))
    def _():
        for r in range(lines):
            for q in range(across):
                word_arrived(r, q)

    places_ref[...] = words_in[...]

    @pl.when(bearer)
    def _():
        each_word(row, col, lambda c: c.wait_send(), None)
        for r in range(lines):
            for q in range(across):

                @pl.when((row != r) | (col != q))
                def _(r=r, q=q):
                    each_word(r, q, lambda c: c.wait_send())

    for r in range(lines):
        store_copy(r).wait()

    @pl.loop(0, PARTS)
    def _(s):
        each_send(row, col, s, lambda c: c.wait_send(), None)
        for r in range(lines):
            for q in range(across):

                @pl.when((row != r) | (col != q))
                def _(r=r, q=q):
                    each_send(r, q, s, lambda c: c.wait_send())


def gather_scores(images, templates, index, interp, noise_flat, orient):
    own, pixels = images.shape
    count, side = index.shape
    fold = PARTS
    while own * fold % 16:
        fold += PARTS
    width = pixels // fold
    total = own * orient
    padded = -(-total // LANES) * LANES
    vmem = pl.BlockSpec(memory_space=pltpu.VMEM)
    hbm = pl.BlockSpec(memory_space=pl.ANY)
    chips = orient // 2
    return pl.pallas_call(
        functools.partial(gather_kernel, orient),
        out_shape=(
            jax.ShapeDtypeStruct((total, pixels), jnp.bfloat16),
            jax.ShapeDtypeStruct((count, total), jnp.bfloat16),
            jax.ShapeDtypeStruct((count // LANES, LANES), jnp.float32),
            jax.ShapeDtypeStruct((chips, side, count), jnp.int32),
            jax.ShapeDtypeStruct((side * count // BATCH, BATCH), jnp.int32),
            jax.ShapeDtypeStruct((8, side), jnp.int32),
        ),
        in_specs=[vmem, hbm, vmem, vmem, vmem],
        out_specs=(hbm, vmem, vmem, vmem, vmem, vmem),
        scratch_shapes=[
            pltpu.VMEM((own * fold, width), jnp.bfloat16),
            pltpu.VMEM((own * fold, width), jnp.float32),
            pltpu.VMEM((side, count), jnp.int32),
            pltpu.VMEM((chips, side, count), jnp.int32),
            pltpu.VMEM((orient, own * fold, width), jnp.bfloat16),
            pltpu.VMEM((count, pixels), jnp.bfloat16),
            pltpu.VMEM((total, pixels), jnp.bfloat16),
            pltpu.VMEM((padded, count), jnp.float32),
            pltpu.VMEM((count, LANES), jnp.float32),
            pltpu.VMEM((8, padded), jnp.float32),
            pltpu.VMEM((orient, 8, padded), jnp.float32),
            pltpu.SemaphoreType.DMA((fold,)),
            pltpu.SemaphoreType.DMA((LINES,)),
            pltpu.SemaphoreType.DMA((chips, PARTS, 5)),
            pltpu.SemaphoreType.DMA((orient, PARTS)),
            pltpu.SemaphoreType.DMA((orient,)),
            pltpu.SemaphoreType.DMA((orient,)),
            pltpu.SemaphoreType.DMA((chips, 5)),
            pltpu.SemaphoreType.DMA((chips,)),
        ],
        compiler_params=pltpu.CompilerParams(
            collective_id=1, has_side_effects=True, vmem_limit_bytes=VMEM_LIMIT
        ),
    )(images, templates, noise_flat, index, interp)


def shards(groups, orient, images, templates, index, interp, inv_noise):
    side = inv_noise.shape[0]
    gathered, post, mass, places, voxels, clash = gather_scores(
        images, templates, index, interp, inv_noise.reshape(1, -1), orient
    )
    volume = insert_data(post, gathered, interp, voxels, clash, side * side)
    return reduce_rows(
        volume, mass, places, inv_noise, groups, orient
    )


def solution(mesh):
    placed = (
        P(("dp", "orient"), None),
        P("orient", None),
        P("orient", None),
        P("orient", None),
        P(),
    )
    return jax.shard_map(
        functools.partial(shards, mesh.shape["dp"], mesh.shape["orient"]),
        mesh=mesh,
        in_specs=placed,
        out_specs=(P(("dp", "orient"), None), P(("dp", "orient"), None)),
        check_vma=False,
    )
```

```python
import functools

import jax
import jax.numpy as jnp
from jax import lax
from jax.experimental import pallas as pl
from jax.experimental.pallas import tpu as pltpu
from jax.sharding import PartitionSpec as P

LANES = 128
ROWS_STEP = 8
ACCS = 4
SUB = 4
BATCH = 128
LINES = 4
PARTS = 4
NORM_COLS = 1024
LEVELS = 65535
SHIFT = 65536
LOW_BITS = 6
LOW = 1 << LOW_BITS
VMEM_LIMIT = 56 * 2**20


def data_kernel(post_ref, images_ref, interp_ref, idx_ref, clash_ref, out_ref, rows_ref, *more):
    accs = (out_ref,) + more
    step = pl.program_id(0)
    count, side = post_ref.shape[0], out_ref.shape[1]
    volume_rows = out_ref.shape[0]
    halves = count // BATCH

    @pl.when(step == 0)
    def _():
        @pl.loop(0, volume_rows // 64)
        def _(c):
            rows = pl.ds(pl.multiple_of(c * 64, 64), 64)
            for acc in accs:
                acc[rows, :] = jnp.zeros((64, side), jnp.float32)

    interp = pltpu.roll(interp_ref[...], lax.rem(side - step * ROWS_STEP, side), axis=1)
    for j in range(ROWS_STEP):
        block = jnp.dot(
            post_ref[...],
            images_ref[:, j * side : (j + 1) * side],
            preferred_element_type=jnp.float32,
        )
        rows_ref[j * count : (j + 1) * count, :] = block * interp[:, j : j + 1]

    @pl.loop(0, ROWS_STEP * halves)
    def _(g):
        base = pl.multiple_of(g * BATCH, BATCH)
        voxels = idx_ref.at[g]
        clash = clash_ref[lax.rem(g, halves), step * ROWS_STEP + lax.div(g, halves)]

        @pl.when(clash == 0)
        def _():
            pending = [None] * ACCS

            def flush(a):
                for voxel, value in pending[a] or ():
                    accs[a][pl.ds(voxel, 1), :] = value

            for n in range(BATCH // SUB):
                a = n % ACCS
                flush(a)
                pending[a] = []
                for k in range(n * SUB, (n + 1) * SUB):
                    voxel = voxels[k]
                    value = accs[a][pl.ds(voxel, 1), :] + rows_ref[pl.ds(base + k, 1), :]
                    pending[a].append((voxel, value))
            for a in range(ACCS):
                flush(a)

        @pl.when(clash != 0)
        def _():
            @pl.loop(0, BATCH // ACCS)
            def _(q):
                first = q * ACCS
                targets = [voxels[first + a] for a in range(ACCS)]
                summed = [
                    accs[a][pl.ds(targets[a], 1), :]
                    + rows_ref[pl.ds(base + first + a, 1), :]
                    for a in range(ACCS)
                ]
                for a in range(ACCS):
                    accs[a][pl.ds(targets[a], 1), :] = summed[a]

    @pl.when(step == pl.num_programs(0) - 1)
    def _():
        @pl.loop(0, volume_rows // 64)
        def _(c):
            rows = pl.ds(pl.multiple_of(c * 64, 64), 64)
            total = accs[0][rows, :]
            for acc in accs[1:]:
                total = total + acc[rows, :]
            out_ref[rows, :] = total


def insert_data(post, gathered, interp, voxels, clash, volume_rows):
    count, images = post.shape
    side = interp.shape[1]
    steps = side // ROWS_STEP
    batches = ROWS_STEP * count // BATCH
    return pl.pallas_call(
        data_kernel,
        grid=(steps,),
        out_shape=jax.ShapeDtypeStruct((volume_rows, side), jnp.float32),
        in_specs=[
            pl.BlockSpec((count, images), lambda i: (0, 0)),
            pl.BlockSpec((images, ROWS_STEP * side), lambda i: (0, i)),
            pl.BlockSpec((count, side), lambda i: (0, 0)),
            pl.BlockSpec((batches, BATCH), lambda i: (i, 0), memory_space=pltpu.SMEM),
            pl.BlockSpec(memory_space=pltpu.SMEM),
        ],
        out_specs=pl.BlockSpec(
            (volume_rows, side), lambda i: (0, 0), pipeline_mode=pl.Buffered(1)
        ),
        scratch_shapes=[pltpu.VMEM((ROWS_STEP * count, side), jnp.float32)]
        + [pltpu.VMEM((volume_rows, side), jnp.float32)] * (ACCS - 1),
        compiler_params=pltpu.CompilerParams(vmem_limit_bytes=VMEM_LIMIT),
        cost_estimate=pl.CostEstimate(
            flops=200_000_000_000, bytes_accessed=200_000_000, transcendentals=0
        ),
    )(post, gathered, interp, voxels, clash)


def reduce_kernel(
    groups,
    orient,
    blocks_ref,
    mass_ref,
    places_ref,
    noise_ref,
    out_ref,
    weight_ref,
    grid_ref,
    mass_row,
    mine,
    theirs,
    first_x,
    first_x_in,
    first_y,
    first_y_in,
    second_x,
    second_x_in,
    second_y,
    second_y_in,
    last,
    last_in,
    masses,
    twin,
    twin_in,
    own_sem,
    pair_send,
    pair_recv,
    fx_send,
    fx_recv,
    fy_send,
    fy_recv,
    sx_send,
    sx_recv,
    sy_send,
    sy_recv,
    last_send,
    last_recv,
    mass_send,
    mass_recv,
    twin_send,
    twin_recv,
):
    lines, across = LINES, orient // (2 * LINES)
    devices = groups * orient
    group, place = lax.axis_index("dp"), lax.axis_index("orient")
    core, chip = lax.rem(place, 2), lax.div(place, 2)
    row, col = lax.div(chip, across), lax.rem(chip, across)
    rank = group * orient + place
    half = out_ref.shape[0] // 2
    mesh_ids = pl.DeviceIdType.MESH

    def ranked(d):
        return (lax.div(d, orient), lax.rem(d, orient))

    def line(k):
        return lax.rem(row + k + 1, lines)

    def group_at(i):
        return lax.rem(group + i, groups)

    def col_at(j):
        return lax.rem(col + j, across)

    def block(x, r, q):
        return (x * lines + r) * across + q

    def remote(source, target, send, recv, x, r, q, c):
        return pltpu.make_async_remote_copy(
            src_ref=source,
            dst_ref=target,
            send_sem=send,
            recv_sem=recv,
            device_id=(x, (r * across + q) * 2 + c),
            device_id_type=mesh_ids,
        )

    barrier = pltpu.get_barrier_semaphore()

    @pl.loop(1, devices)
    def _(s):
        pl.semaphore_signal(
            barrier,
            inc=1,
            device_id=ranked(lax.rem(rank + s, devices)),
            device_id_type=mesh_ids,
        )

    def own_copy(k, i, j):
        p = block(group_at(i), line(k), col_at(j))
        return pltpu.make_async_copy(
            blocks_ref.at[p, core], mine.at[p], own_sem.at[k, i * across + j]
        )

    for i in reversed(range(groups)):
        for j in reversed(range(across)):

            @pl.loop(0, lines)
            def _(k, i=i, j=j):
                own_copy(k, i, j).start()

    pl.semaphore_wait(barrier, devices - 1)

    def mass_copy(s):
        return pltpu.make_async_remote_copy(
            src_ref=mass_ref,
            dst_ref=masses.at[s],
            send_sem=mass_send.at[s],
            recv_sem=mass_recv.at[s],
            device_id=ranked(lax.rem(rank + s, devices)),
            device_id_type=mesh_ids,
        )

    def pair_copy(k, i, j):
        p, n = block(group_at(i), line(k), col_at(j)), i * across + j
        return remote(
            blocks_ref.at[p, 1 - core],
            theirs.at[p],
            pair_send.at[k, n],
            pair_recv.at[k, n],
            group,
            row,
            col,
            1 - core,
        )

    def first_x_copy(k, i):
        return remote(
            first_x.at[i - 1, k],
            first_x_in.at[i - 1, k],
            fx_send.at[i - 1, k],
            fx_recv.at[i - 1, k],
            group_at(i),
            row,
            col,
            core,
        )

    def first_y_copy(k, j):
        return remote(
            first_y.at[j - 1, k],
            first_y_in.at[j - 1, k],
            fy_send.at[j - 1, k],
            fy_recv.at[j - 1, k],
            group,
            row,
            col_at(j),
            core,
        )

    def second_x_copy(k, i):
        return remote(
            second_x.at[i - 1, k],
            second_x_in.at[i - 1, k],
            sx_send.at[i - 1, k],
            sx_recv.at[i - 1, k],
            group_at(i),
            row,
            col,
            core,
        )

    def second_y_copy(k, j):
        return remote(
            second_y.at[j - 1, k],
            second_y_in.at[j - 1, k],
            sy_send.at[j - 1, k],
            sy_recv.at[j - 1, k],
            group,
            row,
            col_at(j),
            core,
        )

    def last_copy(k):
        return remote(
            last.at[k],
            last_in.at[k],
            last_send.at[k],
            last_recv.at[k],
            group,
            line(k),
            col,
            core,
        )

    @pl.loop(0, lines)
    def _(k):
        for i in reversed(range(groups)):
            for j in reversed(range(across)):
                pair_copy(k, i, j).start()

    twin_group = group + 1 - 2 * lax.rem(group, 2)

    def column(d):
        return lax.rem(lax.div(lax.rem(d, orient), 2), across)

    def mass_sent(s):
        target = lax.rem(rank + s, devices)
        return (lax.rem(lax.div(target, orient), 2) == core) & (column(target) == col)

    @pl.loop(1, devices)
    def _(s):
        @pl.when(mass_sent(s))
        def _():
            mass_copy(s).start()

    def narrow(value):
        return value.astype(jnp.bfloat16)

    def begin(k):
        for i in reversed(range(groups)):
            for j in reversed(range(across)):
                x, q = group_at(i), col_at(j)
                p = block(x, line(k), q)
                own_copy(k, i, j).wait()
                pair_copy(k, i, j).wait()
                if i == 0 or j == 0:
                    total = mine[p] + theirs[p]
                    mine[p] = total
                    if i:
                        first_x[i - 1, k, q] = narrow(total[:half])
                    if j:
                        first_y[j - 1, k, x] = narrow(total[half:])
                else:
                    first_x[i - 1, k, q] = narrow(mine[p, :half] + theirs[p, :half])
                    first_y[j - 1, k, x] = narrow(mine[p, half:] + theirs[p, half:])
            if i:
                first_x_copy(k, i).start()
        for j in range(1, across):
            first_y_copy(k, j).start()

    def middle(k):
        for i in range(1, groups):
            first_x_copy(k, i).wait()
        for j in reversed(range(across)):
            q = col_at(j)
            p = block(group, line(k), q)
            total = mine[p, :half]
            for i in range(1, groups):
                total = total + first_x_in[i - 1, k, q].astype(jnp.float32)
            if j:
                second_y[j - 1, k] = narrow(total)
                second_y_copy(k, j).start()
            else:
                mine[p, :half] = total
        for j in range(1, across):
            first_y_copy(k, j).wait()
        for i in reversed(range(groups)):
            x = group_at(i)
            p = block(x, line(k), col)
            total = mine[p, half:]
            for j in range(1, across):
                total = total + first_y_in[j - 1, k, x].astype(jnp.float32)
            if i:
                second_x[i - 1, k] = narrow(total)
                second_x_copy(k, i).start()
            else:
                mine[p, half:] = total

    def end(k):
        p = block(group, line(k), col)
        for j in range(1, across):
            second_y_copy(k, j).wait()
        top = mine[p, :half]
        for j in range(1, across):
            top = top + second_y_in[j - 1, k].astype(jnp.float32)
        for i in range(1, groups):
            second_x_copy(k, i).wait()
        low = mine[p, half:]
        for i in range(1, groups):
            low = low + second_x_in[i - 1, k].astype(jnp.float32)

        @pl.when(k < lines - 1)
        def _():
            last[k, :half] = narrow(top)
            last[k, half:] = narrow(low)
            last_copy(k).start()

        @pl.when(k == lines - 1)
        def _():
            out_ref[:half] = top
            out_ref[half:] = low

    mass_row[...] = jnp.zeros_like(mass_row)
    mass_rows = mass_ref.shape[0]

    def add_mass(d, ref):
        start = lax.div(lax.rem(d, orient), 2 * across) * (mass_rows * LANES)
        for k in range(mass_rows):
            lanes = pl.ds(pl.multiple_of(start + k * LANES, LANES), LANES)
            mass_row[:, lanes] += ref[k : k + 1, :]

    steps, slots = noise_ref.shape[0] // ROWS_STEP, 3 * (lines + 2)

    def weigh(w):
        rows = out_ref.shape[0]
        firsts = [
            (x * orient + (row * across + col_at(j)) * 2 + core) * rows
            for x in (group, twin_group)
            for j in range(across)
        ]
        weight_step(w, firsts, places_ref, mass_row, grid_ref)

    def twin_copy(n):
        return remote(
            twin.at[n - 1],
            twin_in.at[n - 1],
            twin_send.at[n - 1],
            twin_recv.at[n - 1],
            (group, twin_group)[n // across],
            row,
            col_at(n % across),
            core,
        )

    @pl.loop(0, slots)
    def _(slot):
        k, turn = lax.div(slot, 3), lax.rem(slot, 3)

        @pl.when((turn == 0) & (k < lines))
        def _():
            begin(k)

        @pl.when((turn == 1) & (k >= 1) & (k < lines + 1))
        def _():
            middle(k - 1)

        @pl.when((turn == 2) & (k >= 2))
        def _():
            end(k - 2)

        @pl.when(slot == 1)
        def _():
            @pl.when(core == lax.rem(group, 2))
            def _():
                add_mass(rank, mass_ref)

            @pl.loop(1, devices)
            def _(s):
                sender = lax.rem(rank + devices - s, devices)

                @pl.when((lax.rem(sender, 2) == lax.rem(group, 2)) & (column(sender) == col))
                def _():
                    mass_copy(s).wait_recv()
                    add_mass(sender, masses.at[s])

                @pl.when(mass_sent(s))
                def _():
                    mass_copy(s).wait_send()

        @pl.when((slot >= 2) & (slot < 2 + steps // 2))
        def _():
            weigh(2 * slot - 4)
            weigh(2 * slot - 3)

        @pl.when(slot == 2 + steps // 2)
        def _():
            for n in range(1, 2 * across):
                weight_rows(noise_ref, twin.at[n - 1], grid_ref, n, 2 * across)
                twin_copy(n).start()

    weight_rows(noise_ref, weight_ref, grid_ref, 0, 2 * across)
    for n in range(1, 2 * across):
        twin_copy(n).wait()
        weight_ref[...] += twin_in[n - 1].astype(jnp.float32)
    for k in range(lines - 1):
        last_copy(k).wait()
        out_ref[...] += last_in[k].astype(jnp.float32)


def reduce_rows(volume, mass_rows, places_t, inv_noise, groups, orient):
    chips = groups * orient // 2
    lines, across = LINES, orient // (2 * LINES)
    rows, side = volume.shape[0] // (2 * chips), volume.shape[1]
    half = rows // 2
    parts = (chips, rows, side)
    masses = (2 * chips,) + mass_rows.shape
    shapes = [
        (groups - 1, lines, across, half, side),
        (across - 1, lines, groups, half, side),
        (groups - 1, lines, half, side),
        (across - 1, lines, half, side),
        (lines - 1, rows, side),
    ]
    sems = [
        (groups - 1, lines),
        (across - 1, lines),
        (groups - 1, lines),
        (across - 1, lines),
        (lines - 1,),
        (2 * chips,),
    ]
    return pl.pallas_call(
        functools.partial(reduce_kernel, groups, orient),
        out_shape=(
            jax.ShapeDtypeStruct((rows, side), jnp.float32),
            jax.ShapeDtypeStruct((rows, side), jnp.float32),
        ),
        in_specs=[pl.BlockSpec(memory_space=pl.ANY)]
        + [pl.BlockSpec(memory_space=pltpu.VMEM)] * 3,
        out_specs=(
            pl.BlockSpec(memory_space=pltpu.VMEM),
            pl.BlockSpec(memory_space=pltpu.VMEM),
        ),
        scratch_shapes=[
            pltpu.VMEM((2 * across * side * max(8, rows // LOW), LANES), jnp.float32),
            pltpu.VMEM((1, places_t.shape[0] * places_t.shape[2]), jnp.float32),
        ]
        + [pltpu.VMEM(parts, jnp.float32)] * 2
        + [pltpu.VMEM(s, jnp.bfloat16) for s in shapes for _ in range(2)]
        + [pltpu.VMEM(masses, jnp.float32)]
        + [pltpu.VMEM((2 * across - 1, rows, side), jnp.bfloat16)] * 2
        + [pltpu.SemaphoreType.DMA((lines, groups * across))] * 3
        + [pltpu.SemaphoreType.DMA(s) for s in sems for _ in range(2)]
        + [pltpu.SemaphoreType.DMA((2 * across - 1,))] * 2,
        compiler_params=pltpu.CompilerParams(
            collective_id=0, has_side_effects=True, vmem_limit_bytes=VMEM_LIMIT
        ),
    )(volume.reshape(chips, 2, rows, side), mass_rows, places_t, inv_noise)


def weight_step(step, firsts, places_ref, mass_row, grid_ref):
    blocks, side, each = places_ref.shape
    count = blocks * each
    high_rows = grid_ref.shape[0] // side
    nt = (((1,), (1,)), ((), ()))
    one, zero = jnp.float32(1), jnp.float32(0)
    spot = lax.broadcasted_iota(jnp.int32, (high_rows, count), 0)
    each_high = high_rows // len(firsts)
    iota_high = spot
    for n, first in enumerate(firsts):
        shift = lax.div(first, LOW) - n * each_high
        iota_high = jnp.where(spot // each_high == n, spot + shift, iota_high)
    iota_low = lax.broadcasted_iota(jnp.int32, (LOW, count), 0)
    block = pl.ds(pl.multiple_of(step * ROWS_STEP, ROWS_STEP), ROWS_STEP)
    words = jnp.concatenate([places_ref[d, block, :] for d in range(blocks)], axis=1)
    voxels = words >> 16
    weights = (words & (SHIFT - 1)).astype(jnp.float32) * (1 / LEVELS) * mass_row[...]
    for j in range(ROWS_STEP):
        local = voxels[j : j + 1, :]
        hot = jnp.where(iota_high == (local >> LOW_BITS), one, zero)
        low = jnp.where(iota_low == (local & (LOW - 1)), weights[j : j + 1, :], zero)
        part = lax.dot_general(
            hot.astype(jnp.bfloat16),
            low.astype(jnp.bfloat16),
            nt,
            preferred_element_type=jnp.float32,
        )
        row = pl.multiple_of((step * ROWS_STEP + j) * high_rows, 8)
        grid_ref[pl.ds(row, high_rows), :LOW] = part


def weight_rows(noise_ref, out_ref, grid_ref, part, ranges):
    side = noise_ref.shape[0]
    high_rows = grid_ref.shape[0] // side
    noise = noise_ref[...].astype(jnp.bfloat16)
    for h in range(out_ref.shape[0] // LOW):
        first = part * (high_rows // ranges) + h
        block = lax.dot_general(
            grid_ref[pl.ds(first, side, stride=high_rows), :].astype(jnp.bfloat16),
            noise,
            (((0,), (0,)), ((), ())),
            preferred_element_type=jnp.float32,
        )
        out_ref[h * LOW : (h + 1) * LOW, :] = block[:LOW].astype(out_ref.dtype)


def gather_kernel(
    orient,
    own_ref,
    templates_ref,
    noise_ref,
    index_ref,
    interp_ref,
    gathered_ref,
    post_ref,
    mass_ref,
    places_ref,
    rows_ref,
    clash_ref,
    images_ref,
    wide,
    words,
    words_in,
    raw,
    weighted,
    whole,
    scores,
    norms,
    stats,
    landed,
    load_sem,
    store_sem,
    send_sem,
    recv_sem,
    stat_send,
    stat_recv,
    word_send,
    word_recv,
):
    lines, across = LINES, orient // (2 * LINES)
    group, place = lax.axis_index("dp"), lax.axis_index("orient")
    core = lax.rem(place, 2)
    chip = lax.div(place, 2)
    row, col = lax.div(chip, across), lax.rem(chip, across)
    mesh_ids = pl.DeviceIdType.MESH
    block_rows, width = images_ref.shape
    part = width // PARTS
    count = templates_ref.shape[0]
    fold = templates_ref.shape[1] // width
    line_images = 2 * across * block_rows // fold
    images = line_images * lines

    def at(r, q, c):
        return (r * across + q) * 2 + c

    barrier = pltpu.get_barrier_semaphore()

    @pl.loop(1, orient)
    def _(s):
        pl.semaphore_signal(
            barrier,
            inc=1,
            device_id=(group, lax.rem(place + s, orient)),
            device_id_type=mesh_ids,
        )

    def load_copy(k):
        cols = pl.ds(pl.multiple_of(k * width, width), width)
        return pltpu.make_async_copy(
            templates_ref.at[:, cols], weighted.at[:, cols], load_sem.at[k]
        )

    for k in range(fold):
        load_copy(k).start()

    own_rows = own_ref.shape[0]
    for k in range(fold):
        wide[k * own_rows : (k + 1) * own_rows, :] = own_ref[
            :, k * width : (k + 1) * width
        ].astype(jnp.float32)
    images_ref[...] = wide[...].astype(jnp.bfloat16)
    pl.semaphore_wait(barrier, orient - 1)

    def copy(source, r, q, s, way, target):
        cols = pl.ds(pl.multiple_of(s * part, part), part)
        slot = at(r, q, core)
        ref = images_ref if source is None else raw.at[slot]
        return pltpu.make_async_remote_copy(
            src_ref=ref.at[:, cols],
            dst_ref=raw.at[slot, :, cols],
            send_sem=send_sem.at[lax.div(slot, 2), s, way],
            recv_sem=recv_sem.at[slot, s],
            device_id=(group, target),
            device_id_type=mesh_ids,
        )

    def arrived(r, q, c, s):
        cols = pl.ds(pl.multiple_of(s * part, part), part)
        slot = at(r, q, c)
        pltpu.make_async_remote_copy(
            src_ref=raw.at[slot, :, cols],
            dst_ref=raw.at[slot, :, cols],
            send_sem=send_sem.at[0, 0, 0],
            recv_sem=recv_sem.at[slot, s],
            device_id=(group, place + 1 - 2 * core),
            device_id_type=mesh_ids,
        ).wait_recv()

    def each_send(r, q, s, act, source=raw):
        for way, step in ((0, 1), (1, -1)):
            onward = row + step
            if source is None:
                along = (onward >= 0) & (onward < lines)
            else:
                along = (q == col) & (onward >= 0) & (onward < lines) & ((row - r) * step > 0)

            @pl.when(along)
            def _(way=way, onward=onward):
                act(copy(source, r, q, s, way, at(onward, col, core)))

        for way, step in ((2, 1), (3, -1)):
            onward = col + step
            beside = (onward >= 0) & (onward < across) & ((col - q) * step >= 0)

            @pl.when(beside)
            def _(way=way, onward=onward):
                act(copy(source, r, q, s, way, at(row, onward, core)))

        act(copy(source, r, q, s, 4, place + 1 - 2 * core))

    @pl.loop(0, PARTS)
    def _(s):
        each_send(row, col, s, lambda c: c.start(), None)

    raw[place] = images_ref[...]
    scores[...] = jnp.zeros_like(scores)
    norms[...] = jnp.zeros_like(norms)

    index = index_ref[...]
    near = jnp.zeros(index.shape, jnp.int32)
    spot = lax.broadcasted_iota(jnp.int32, index.shape, 0) % SUB
    for d in range(1, SUB):
        same = (index == pltpu.roll(index, d, axis=0)) & (spot >= d)
        near = near | same.astype(jnp.int32)
    clash_ref[...] = jnp.zeros_like(clash_ref)
    for h in range(count // BATCH):
        clash_ref[h : h + 1, :] = jnp.max(
            near[h * BATCH : (h + 1) * BATCH, :], axis=0, keepdims=True
        )
    index_t = index.T
    for h in range(count // BATCH):
        rows_ref[pl.ds(h, index_t.shape[0], stride=count // BATCH), :] = index_t[
            :, h * BATCH : (h + 1) * BATCH
        ]
    level = (interp_ref[...] * LEVELS + 0.5).astype(jnp.int32)
    words[...] = (index * SHIFT + level).T

    bearer = lax.rem(group, 2) == core

    def word_copy(source, r, way, target):
        return pltpu.make_async_remote_copy(
            src_ref=words if source is None else words_in.at[r],
            dst_ref=words_in.at[r],
            send_sem=word_send.at[r, way],
            recv_sem=word_recv.at[r],
            device_id=(group, target),
            device_id_type=mesh_ids,
        )

    def word_arrived(r):
        word_copy(words_in, r, 2, place + 1 - 2 * core).wait_recv()

    def each_word(r, act, source=words_in):
        for way, step in ((0, 1), (1, -1)):
            onward = row + step
            along = (onward >= 0) & (onward < lines)
            if source is not None:
                along = along & ((row - r) * step > 0)

            @pl.when(along)
            def _(way=way, onward=onward):
                act(word_copy(source, r, way, at(onward, col, core)))

        act(word_copy(source, r, 2, place + 1 - 2 * core))

    def weigh(k):
        load_copy(k).wait()

        @pl.loop(0, width // NORM_COLS)
        def _(g):
            cols = pl.ds(pl.multiple_of(k * width + g * NORM_COLS, NORM_COLS), NORM_COLS)
            for h in range(0, count, 64):
                tpl = weighted[h : h + 64, cols].astype(jnp.float32)
                noise = noise_ref[:, cols]
                scaled = tpl * noise
                square = tpl * tpl * noise
                total = square[:, :LANES]
                for j in range(1, NORM_COLS // LANES):
                    total = total + square[:, j * LANES : (j + 1) * LANES]
                norms[h : h + 64, :] += total
                weighted[h : h + 64, cols] = scaled.astype(jnp.bfloat16)

    def score(r, s):
        for q in range(across):
            arrived(r, q, 1 - core, s)
        cols = pl.ds(pl.multiple_of(s * part, part), part)
        slots = pl.ds(pl.multiple_of(r * (2 * across), 2 * across), 2 * across)
        block = raw[slots, :, cols].reshape(2 * across * block_rows, part)
        total = 2 * across * block_rows
        out_row = lax.broadcasted_iota(jnp.int32, (total, total), 0)
        from_row = lax.broadcasted_iota(jnp.int32, (total, total), 1)
        image, piece = out_row % line_images, out_row // line_images
        wanted = (image // own_rows) * block_rows + piece * own_rows + image % own_rows
        pick = jnp.where(from_row == wanted, 1.0, 0.0).astype(jnp.bfloat16)
        sorted_ = jnp.dot(pick, block, preferred_element_type=jnp.float32)
        sorted_ = sorted_.astype(jnp.bfloat16)
        rows = pl.ds(pl.multiple_of(r * line_images, line_images), line_images)
        added = scores[rows, :]
        for k in range(fold):
            piece = sorted_[k * line_images : (k + 1) * line_images, :]
            span = pl.ds(pl.multiple_of(k * width + s * part, part), part)
            whole[rows, span] = piece
            added = added + lax.dot_general(
                piece,
                weighted[:, span],
                (((1,), (1,)), ((), ())),
                preferred_element_type=jnp.float32,
            )
        scores[rows, :] = added

    def store_copy(r):
        rows = pl.ds(pl.multiple_of(r * line_images, line_images), line_images)
        return pltpu.make_async_copy(whole.at[rows], gathered_ref.at[rows], store_sem.at[r])

    def score_store(r, s):
        score(r, s)

        @pl.when(s == PARTS - 1)
        def _():
            store_copy(r).start()

    @pl.loop(0, lines * PARTS + 1)
    def _(k):
        n, s = lax.div(k, PARTS) + 1, lax.rem(k, PARTS)
        for sign in (1, -1):
            r = row + sign * n

            @pl.when((r >= 0) & (r < lines) & (n < lines))
            def _(r=r):
                arrived(r, col, core, s)
                each_send(r, col, s, lambda c: c.start())

        for sign in (1, -1):
            r = row + sign * (n - 1)
            live = (r >= 0) & (r < lines) & (n <= lines)
            if sign < 0:
                live = live & (n > 1)
            for e in range(1, across):
                for side in (1, -1):
                    q = col + side * e

                    @pl.when(live & (q >= 0) & (q < across))
                    def _(r=r, q=q):
                        arrived(r, q, core, s)
                        each_send(r, q, s, lambda c: c.start())

        @pl.when(n == 1)
        def _():
            @pl.loop(0, fold // PARTS)
            def _(j):
                weigh(s * (fold // PARTS) + j)

        @pl.when(bearer & (n == lines) & (s == 0))
        def _():
            each_word(row, lambda c: c.start(), None)

        for sign in (1, -1):
            r = row + sign * s

            @pl.when(bearer & (n == lines) & (s > 0) & (r >= 0) & (r < lines))
            def _(r=r):
                word_arrived(r)
                each_word(r, lambda c: c.start())

        last = jnp.maximum(k - 1, 0)
        m, t = lax.div(last, PARTS) + 1, lax.rem(last, PARTS)

        @pl.when((m == 2) & (k > 0))
        def _():
            score_store(row, t)

        for sign in (1, -1):
            r = row + sign * (m - 1)

            @pl.when((m > 1) & (r >= 0) & (r < lines))
            def _(r=r):
                score_store(r, t)

    norm = 0.5 * jnp.sum(norms[...].T, axis=0, keepdims=True)
    value = (scores[...] - norm).T
    peak_own = jnp.max(value, axis=0, keepdims=True)
    expo = jnp.exp(value - peak_own)
    stats[...] = jnp.zeros_like(stats)
    stats[0:1, :] = peak_own
    stats[1:2, :] = jnp.sum(expo, axis=0, keepdims=True)

    def stat_copy(s):
        return pltpu.make_async_remote_copy(
            src_ref=stats,
            dst_ref=landed.at[s],
            send_sem=stat_send.at[s],
            recv_sem=stat_recv.at[s],
            device_id=(group, lax.rem(place + s, orient)),
            device_id_type=mesh_ids,
        )

    @pl.loop(1, orient)
    def _(s):
        stat_copy(s).start()

    landed[0] = stats[...]

    @pl.when(bearer)
    def _():
        words_in[row] = words[...]

    @pl.loop(1, orient)
    def _(s):
        stat_copy(s).wait()

    peak = peak_own
    for s in range(1, orient):
        peak = jnp.maximum(peak, landed[s, 0:1, :])
    total = jnp.zeros_like(peak)
    for s in range(orient):
        total = total + landed[s, 1:2, :] * jnp.exp(landed[s, 0:1, :] - peak)
    posterior = (expo * (jnp.exp(peak_own - peak) / total))[:, :images]
    post_ref[...] = posterior.astype(jnp.bfloat16)
    mass = jnp.sum(posterior, axis=1, keepdims=True)
    mass_t = jnp.broadcast_to(mass, (count, LANES)).T
    for h in range(count // LANES):
        mass_ref[h : h + 1, :] = mass_t[:1, h * LANES : (h + 1) * LANES]

    @pl.when(jnp.logical_not(bearer))
    def _():
        for r in range(lines):
            word_arrived(r)

    places_ref[...] = words_in[...]

    @pl.when(bearer)
    def _():
        each_word(row, lambda c: c.wait_send(), None)
        for r in range(lines):

            @pl.when(row != r)
            def _(r=r):
                each_word(r, lambda c: c.wait_send())

    for r in range(lines):
        store_copy(r).wait()

    @pl.loop(0, PARTS)
    def _(s):
        each_send(row, col, s, lambda c: c.wait_send(), None)
        for r in range(lines):
            for q in range(across):

                @pl.when((row != r) | (col != q))
                def _(r=r, q=q):
                    each_send(r, q, s, lambda c: c.wait_send())


def gather_scores(images, templates, index, interp, noise_flat, orient):
    own, pixels = images.shape
    count, side = index.shape
    fold = PARTS
    while own * fold % 16:
        fold += PARTS
    width = pixels // fold
    total = own * orient
    padded = -(-total // LANES) * LANES
    vmem = pl.BlockSpec(memory_space=pltpu.VMEM)
    hbm = pl.BlockSpec(memory_space=pl.ANY)
    chips = orient // 2
    return pl.pallas_call(
        functools.partial(gather_kernel, orient),
        out_shape=(
            jax.ShapeDtypeStruct((total, pixels), jnp.bfloat16),
            jax.ShapeDtypeStruct((count, total), jnp.bfloat16),
            jax.ShapeDtypeStruct((count // LANES, LANES), jnp.float32),
            jax.ShapeDtypeStruct((LINES, side, count), jnp.int32),
            jax.ShapeDtypeStruct((side * count // BATCH, BATCH), jnp.int32),
            jax.ShapeDtypeStruct((8, side), jnp.int32),
        ),
        in_specs=[vmem, hbm, vmem, vmem, vmem],
        out_specs=(hbm, vmem, vmem, vmem, vmem, vmem),
        scratch_shapes=[
            pltpu.VMEM((own * fold, width), jnp.bfloat16),
            pltpu.VMEM((own * fold, width), jnp.float32),
            pltpu.VMEM((side, count), jnp.int32),
            pltpu.VMEM((LINES, side, count), jnp.int32),
            pltpu.VMEM((orient, own * fold, width), jnp.bfloat16),
            pltpu.VMEM((count, pixels), jnp.bfloat16),
            pltpu.VMEM((total, pixels), jnp.bfloat16),
            pltpu.VMEM((padded, count), jnp.float32),
            pltpu.VMEM((count, LANES), jnp.float32),
            pltpu.VMEM((8, padded), jnp.float32),
            pltpu.VMEM((orient, 8, padded), jnp.float32),
            pltpu.SemaphoreType.DMA((fold,)),
            pltpu.SemaphoreType.DMA((LINES,)),
            pltpu.SemaphoreType.DMA((chips, PARTS, 5)),
            pltpu.SemaphoreType.DMA((orient, PARTS)),
            pltpu.SemaphoreType.DMA((orient,)),
            pltpu.SemaphoreType.DMA((orient,)),
            pltpu.SemaphoreType.DMA((LINES, 3)),
            pltpu.SemaphoreType.DMA((LINES,)),
        ],
        compiler_params=pltpu.CompilerParams(
            collective_id=1, has_side_effects=True, vmem_limit_bytes=VMEM_LIMIT
        ),
    )(images, templates, noise_flat, index, interp)


def shards(groups, orient, images, templates, index, interp, inv_noise):
    side = inv_noise.shape[0]
    gathered, post, mass, places, voxels, clash = gather_scores(
        images, templates, index, interp, inv_noise.reshape(1, -1), orient
    )
    volume = insert_data(post, gathered, interp, voxels, clash, side * side)
    return reduce_rows(
        volume, mass, places, inv_noise, groups, orient
    )


def solution(mesh):
    placed = (
        P(("dp", "orient"), None),
        P("orient", None),
        P("orient", None),
        P("orient", None),
        P(),
    )
    return jax.shard_map(
        functools.partial(shards, mesh.shape["dp"], mesh.shape["orient"]),
        mesh=mesh,
        in_specs=placed,
        out_specs=(P(("dp", "orient"), None), P(("dp", "orient"), None)),
        check_vma=False,
    )
```

```python
import functools

import jax
import jax.numpy as jnp
from jax import lax
from jax.experimental import pallas as pl
from jax.experimental.pallas import tpu as pltpu
from jax.sharding import PartitionSpec as P

LANES = 128
ROWS_STEP = 8
ACCS = 4
SUB = 4
BATCH = 128
LINES = 4
PARTS = 4
NORM_COLS = 1024
LEVELS = 65535
SHIFT = 65536
LOW_BITS = 6
LOW = 1 << LOW_BITS
VMEM_LIMIT = 56 * 2**20


def data_kernel(post_ref, images_ref, interp_ref, idx_ref, clash_ref, out_ref, rows_ref, *more):
    accs = (out_ref,) + more
    step = pl.program_id(0)
    count, side = post_ref.shape[0], out_ref.shape[1]
    volume_rows = out_ref.shape[0]
    halves = count // BATCH

    @pl.when(step == 0)
    def _():
        @pl.loop(0, volume_rows // 64)
        def _(c):
            rows = pl.ds(pl.multiple_of(c * 64, 64), 64)
            for acc in accs:
                acc[rows, :] = jnp.zeros((64, side), jnp.float32)

    interp = pltpu.roll(interp_ref[...], lax.rem(side - step * ROWS_STEP, side), axis=1)
    for j in range(ROWS_STEP):
        block = jnp.dot(
            post_ref[...],
            images_ref[:, j * side : (j + 1) * side],
            preferred_element_type=jnp.float32,
        )
        rows_ref[j * count : (j + 1) * count, :] = block * interp[:, j : j + 1]

    @pl.loop(0, ROWS_STEP * halves)
    def _(g):
        base = pl.multiple_of(g * BATCH, BATCH)
        voxels = idx_ref.at[g]
        clash = clash_ref[lax.rem(g, halves), step * ROWS_STEP + lax.div(g, halves)]

        @pl.when(clash == 0)
        def _():
            pending = [None] * ACCS

            def flush(a):
                for voxel, value in pending[a] or ():
                    accs[a][pl.ds(voxel, 1), :] = value

            for n in range(BATCH // SUB):
                a = n % ACCS
                flush(a)
                pending[a] = []
                for k in range(n * SUB, (n + 1) * SUB):
                    voxel = voxels[k]
                    value = accs[a][pl.ds(voxel, 1), :] + rows_ref[pl.ds(base + k, 1), :]
                    pending[a].append((voxel, value))
            for a in range(ACCS):
                flush(a)

        @pl.when(clash != 0)
        def _():
            @pl.loop(0, BATCH // ACCS)
            def _(q):
                first = q * ACCS
                targets = [voxels[first + a] for a in range(ACCS)]
                summed = [
                    accs[a][pl.ds(targets[a], 1), :]
                    + rows_ref[pl.ds(base + first + a, 1), :]
                    for a in range(ACCS)
                ]
                for a in range(ACCS):
                    accs[a][pl.ds(targets[a], 1), :] = summed[a]

    @pl.when(step == pl.num_programs(0) - 1)
    def _():
        @pl.loop(0, volume_rows // 64)
        def _(c):
            rows = pl.ds(pl.multiple_of(c * 64, 64), 64)
            total = accs[0][rows, :]
            for acc in accs[1:]:
                total = total + acc[rows, :]
            out_ref[rows, :] = total


def insert_data(post, gathered, interp, voxels, clash, volume_rows):
    count, images = post.shape
    side = interp.shape[1]
    steps = side // ROWS_STEP
    batches = ROWS_STEP * count // BATCH
    return pl.pallas_call(
        data_kernel,
        grid=(steps,),
        out_shape=jax.ShapeDtypeStruct((volume_rows, side), jnp.float32),
        in_specs=[
            pl.BlockSpec((count, images), lambda i: (0, 0)),
            pl.BlockSpec((images, ROWS_STEP * side), lambda i: (0, i)),
            pl.BlockSpec((count, side), lambda i: (0, 0)),
            pl.BlockSpec((batches, BATCH), lambda i: (i, 0), memory_space=pltpu.SMEM),
            pl.BlockSpec(memory_space=pltpu.SMEM),
        ],
        out_specs=pl.BlockSpec(
            (volume_rows, side), lambda i: (0, 0), pipeline_mode=pl.Buffered(1)
        ),
        scratch_shapes=[pltpu.VMEM((ROWS_STEP * count, side), jnp.float32)]
        + [pltpu.VMEM((volume_rows, side), jnp.float32)] * (ACCS - 1),
        compiler_params=pltpu.CompilerParams(vmem_limit_bytes=VMEM_LIMIT),
        cost_estimate=pl.CostEstimate(
            flops=200_000_000_000, bytes_accessed=200_000_000, transcendentals=0
        ),
    )(post, gathered, interp, voxels, clash)


def reduce_kernel(
    groups,
    orient,
    blocks_ref,
    mass_ref,
    places_ref,
    noise_ref,
    out_ref,
    weight_ref,
    grid_ref,
    mass_row,
    mine,
    theirs,
    first_x,
    first_x_in,
    first_y,
    first_y_in,
    second_x,
    second_x_in,
    second_y,
    second_y_in,
    last,
    last_in,
    masses,
    twin,
    twin_in,
    own_sem,
    pair_send,
    pair_recv,
    fx_send,
    fx_recv,
    fy_send,
    fy_recv,
    sx_send,
    sx_recv,
    sy_send,
    sy_recv,
    last_send,
    last_recv,
    mass_send,
    mass_recv,
    twin_send,
    twin_recv,
):
    lines, across = LINES, orient // (2 * LINES)
    devices = groups * orient
    group, place = lax.axis_index("dp"), lax.axis_index("orient")
    core, chip = lax.rem(place, 2), lax.div(place, 2)
    row, col = lax.div(chip, across), lax.rem(chip, across)
    rank = group * orient + place
    half = out_ref.shape[0] // 2
    mesh_ids = pl.DeviceIdType.MESH

    def ranked(d):
        return (lax.div(d, orient), lax.rem(d, orient))

    def line(k):
        return lax.rem(row + k + 1, lines)

    def group_at(i):
        return lax.rem(group + i, groups)

    def col_at(j):
        return lax.rem(col + j, across)

    def block(x, r, q):
        return (x * lines + r) * across + q

    def remote(source, target, send, recv, x, r, q, c):
        return pltpu.make_async_remote_copy(
            src_ref=source,
            dst_ref=target,
            send_sem=send,
            recv_sem=recv,
            device_id=(x, (r * across + q) * 2 + c),
            device_id_type=mesh_ids,
        )

    barrier = pltpu.get_barrier_semaphore()

    @pl.loop(1, devices)
    def _(s):
        pl.semaphore_signal(
            barrier,
            inc=1,
            device_id=ranked(lax.rem(rank + s, devices)),
            device_id_type=mesh_ids,
        )

    def own_copy(k, i, j):
        p = block(group_at(i), line(k), col_at(j))
        return pltpu.make_async_copy(
            blocks_ref.at[p, core], mine.at[p], own_sem.at[k, i * across + j]
        )

    for i in reversed(range(groups)):
        for j in reversed(range(across)):

            @pl.loop(0, lines)
            def _(k, i=i, j=j):
                own_copy(k, i, j).start()

    pl.semaphore_wait(barrier, devices - 1)

    def mass_copy(s):
        return pltpu.make_async_remote_copy(
            src_ref=mass_ref,
            dst_ref=masses.at[s],
            send_sem=mass_send.at[s],
            recv_sem=mass_recv.at[s],
            device_id=ranked(lax.rem(rank + s, devices)),
            device_id_type=mesh_ids,
        )

    def pair_copy(k, i, j):
        p, n = block(group_at(i), line(k), col_at(j)), i * across + j
        return remote(
            blocks_ref.at[p, 1 - core],
            theirs.at[p],
            pair_send.at[k, n],
            pair_recv.at[k, n],
            group,
            row,
            col,
            1 - core,
        )

    def first_x_copy(k, i):
        return remote(
            first_x.at[i - 1, k],
            first_x_in.at[i - 1, k],
            fx_send.at[i - 1, k],
            fx_recv.at[i - 1, k],
            group_at(i),
            row,
            col,
            core,
        )

    def first_y_copy(k, j):
        return remote(
            first_y.at[j - 1, k],
            first_y_in.at[j - 1, k],
            fy_send.at[j - 1, k],
            fy_recv.at[j - 1, k],
            group,
            row,
            col_at(j),
            core,
        )

    def second_x_copy(k, i):
        return remote(
            second_x.at[i - 1, k],
            second_x_in.at[i - 1, k],
            sx_send.at[i - 1, k],
            sx_recv.at[i - 1, k],
            group_at(i),
            row,
            col,
            core,
        )

    def second_y_copy(k, j):
        return remote(
            second_y.at[j - 1, k],
            second_y_in.at[j - 1, k],
            sy_send.at[j - 1, k],
            sy_recv.at[j - 1, k],
            group,
            row,
            col_at(j),
            core,
        )

    def last_copy(k):
        return remote(
            last.at[k],
            last_in.at[k],
            last_send.at[k],
            last_recv.at[k],
            group,
            line(k),
            col,
            core,
        )

    @pl.loop(0, lines)
    def _(k):
        for i in reversed(range(groups)):
            for j in reversed(range(across)):
                pair_copy(k, i, j).start()

    twin_group = group + 1 - 2 * lax.rem(group, 2)

    def column(d):
        return lax.rem(lax.div(lax.rem(d, orient), 2), across)

    def mass_sent(s):
        target = lax.rem(rank + s, devices)
        return (lax.rem(lax.div(target, orient), 2) == core) & (column(target) == col)

    @pl.loop(1, devices)
    def _(s):
        @pl.when(mass_sent(s))
        def _():
            mass_copy(s).start()

    def narrow(value):
        return value.astype(jnp.bfloat16)

    def begin(k):
        for i in reversed(range(groups)):
            for j in reversed(range(across)):
                x, q = group_at(i), col_at(j)
                p = block(x, line(k), q)
                own_copy(k, i, j).wait()
                pair_copy(k, i, j).wait()
                if i == 0 or j == 0:
                    total = mine[p] + theirs[p]
                    mine[p] = total
                    if i:
                        first_x[i - 1, k, q] = narrow(total[:half])
                    if j:
                        first_y[j - 1, k, x] = narrow(total[half:])
                else:
                    first_x[i - 1, k, q] = narrow(mine[p, :half] + theirs[p, :half])
                    first_y[j - 1, k, x] = narrow(mine[p, half:] + theirs[p, half:])
            if i:
                first_x_copy(k, i).start()
        for j in range(1, across):
            first_y_copy(k, j).start()

    def middle(k):
        for i in range(1, groups):
            first_x_copy(k, i).wait()
        for j in reversed(range(across)):
            q = col_at(j)
            p = block(group, line(k), q)
            total = mine[p, :half]
            for i in range(1, groups):
                total = total + first_x_in[i - 1, k, q].astype(jnp.float32)
            if j:
                second_y[j - 1, k] = narrow(total)
                second_y_copy(k, j).start()
            else:
                mine[p, :half] = total
        for j in range(1, across):
            first_y_copy(k, j).wait()
        for i in reversed(range(groups)):
            x = group_at(i)
            p = block(x, line(k), col)
            total = mine[p, half:]
            for j in range(1, across):
                total = total + first_y_in[j - 1, k, x].astype(jnp.float32)
            if i:
                second_x[i - 1, k] = narrow(total)
                second_x_copy(k, i).start()
            else:
                mine[p, half:] = total

    def end(k):
        p = block(group, line(k), col)
        for j in range(1, across):
            second_y_copy(k, j).wait()
        top = mine[p, :half]
        for j in range(1, across):
            top = top + second_y_in[j - 1, k].astype(jnp.float32)
        for i in range(1, groups):
            second_x_copy(k, i).wait()
        low = mine[p, half:]
        for i in range(1, groups):
            low = low + second_x_in[i - 1, k].astype(jnp.float32)

        @pl.when(k < lines - 1)
        def _():
            last[k, :half] = narrow(top)
            last[k, half:] = narrow(low)
            last_copy(k).start()

        @pl.when(k == lines - 1)
        def _():
            out_ref[:half] = top
            out_ref[half:] = low

    mass_row[...] = jnp.zeros_like(mass_row)
    mass_rows = mass_ref.shape[0]

    def add_mass(d, ref):
        start = lax.div(lax.rem(d, orient), 2 * across) * (mass_rows * LANES)
        for k in range(mass_rows):
            lanes = pl.ds(pl.multiple_of(start + k * LANES, LANES), LANES)
            mass_row[:, lanes] += ref[k : k + 1, :]

    steps, slots = noise_ref.shape[0] // ROWS_STEP, 3 * (lines + 2)

    def weigh(w):
        rows = out_ref.shape[0]
        firsts = [
            (x * orient + (row * across + col_at(j)) * 2 + core) * rows
            for x in (group, twin_group)
            for j in range(across)
        ]
        weight_step(w, firsts, places_ref, mass_row, grid_ref)

    def twin_copy(n):
        return remote(
            twin.at[n - 1],
            twin_in.at[n - 1],
            twin_send.at[n - 1],
            twin_recv.at[n - 1],
            (group, twin_group)[n // across],
            row,
            col_at(n % across),
            core,
        )

    @pl.loop(0, slots)
    def _(slot):
        k, turn = lax.div(slot, 3), lax.rem(slot, 3)

        @pl.when((turn == 0) & (k < lines))
        def _():
            begin(k)

        @pl.when((turn == 1) & (k >= 1) & (k < lines + 1))
        def _():
            middle(k - 1)

        @pl.when((turn == 2) & (k >= 2))
        def _():
            end(k - 2)

        @pl.when(slot == 1)
        def _():
            @pl.when(core == lax.rem(group, 2))
            def _():
                add_mass(rank, mass_ref)

            @pl.loop(1, devices)
            def _(s):
                sender = lax.rem(rank + devices - s, devices)

                @pl.when((lax.rem(sender, 2) == lax.rem(group, 2)) & (column(sender) == col))
                def _():
                    mass_copy(s).wait_recv()
                    add_mass(sender, masses.at[s])

                @pl.when(mass_sent(s))
                def _():
                    mass_copy(s).wait_send()

        @pl.when((slot >= 2) & (slot < 2 + steps // 2))
        def _():
            weigh(2 * slot - 4)
            weigh(2 * slot - 3)

        @pl.when(slot == 2 + steps // 2)
        def _():
            for n in range(1, 2 * across):
                weight_rows(noise_ref, twin.at[n - 1], grid_ref, n, 2 * across)
                twin_copy(n).start()

    weight_rows(noise_ref, weight_ref, grid_ref, 0, 2 * across)
    for n in range(1, 2 * across):
        twin_copy(n).wait()
        weight_ref[...] += twin_in[n - 1].astype(jnp.float32)
    for k in range(lines - 1):
        last_copy(k).wait()
        out_ref[...] += last_in[k].astype(jnp.float32)


def reduce_rows(volume, mass_rows, places_t, inv_noise, groups, orient):
    chips = groups * orient // 2
    lines, across = LINES, orient // (2 * LINES)
    rows, side = volume.shape[0] // (2 * chips), volume.shape[1]
    half = rows // 2
    parts = (chips, rows, side)
    masses = (2 * chips,) + mass_rows.shape
    shapes = [
        (groups - 1, lines, across, half, side),
        (across - 1, lines, groups, half, side),
        (groups - 1, lines, half, side),
        (across - 1, lines, half, side),
        (lines - 1, rows, side),
    ]
    sems = [
        (groups - 1, lines),
        (across - 1, lines),
        (groups - 1, lines),
        (across - 1, lines),
        (lines - 1,),
        (2 * chips,),
    ]
    return pl.pallas_call(
        functools.partial(reduce_kernel, groups, orient),
        out_shape=(
            jax.ShapeDtypeStruct((rows, side), jnp.float32),
            jax.ShapeDtypeStruct((rows, side), jnp.float32),
        ),
        in_specs=[pl.BlockSpec(memory_space=pl.ANY)]
        + [pl.BlockSpec(memory_space=pltpu.VMEM)] * 3,
        out_specs=(
            pl.BlockSpec(memory_space=pltpu.VMEM),
            pl.BlockSpec(memory_space=pltpu.VMEM),
        ),
        scratch_shapes=[
            pltpu.VMEM((2 * across * side * max(8, rows // LOW), LANES), jnp.float32),
            pltpu.VMEM((1, places_t.shape[0] * places_t.shape[2]), jnp.float32),
        ]
        + [pltpu.VMEM(parts, jnp.float32)] * 2
        + [pltpu.VMEM(s, jnp.bfloat16) for s in shapes for _ in range(2)]
        + [pltpu.VMEM(masses, jnp.float32)]
        + [pltpu.VMEM((2 * across - 1, rows, side), jnp.bfloat16)] * 2
        + [pltpu.SemaphoreType.DMA((lines, groups * across))] * 3
        + [pltpu.SemaphoreType.DMA(s) for s in sems for _ in range(2)]
        + [pltpu.SemaphoreType.DMA((2 * across - 1,))] * 2,
        compiler_params=pltpu.CompilerParams(
            collective_id=0, has_side_effects=True, vmem_limit_bytes=VMEM_LIMIT
        ),
    )(volume.reshape(chips, 2, rows, side), mass_rows, places_t, inv_noise)


def weight_step(step, firsts, places_ref, mass_row, grid_ref):
    blocks, side, each = places_ref.shape
    count = blocks * each
    high_rows = grid_ref.shape[0] // side
    nt = (((1,), (1,)), ((), ()))
    one, zero = jnp.float32(1), jnp.float32(0)
    spot = lax.broadcasted_iota(jnp.int32, (high_rows, count), 0)
    each_high = high_rows // len(firsts)
    iota_high = spot
    for n, first in enumerate(firsts):
        shift = lax.div(first, LOW) - n * each_high
        iota_high = jnp.where(spot // each_high == n, spot + shift, iota_high)
    iota_low = lax.broadcasted_iota(jnp.int32, (LOW, count), 0)
    block = pl.ds(pl.multiple_of(step * ROWS_STEP, ROWS_STEP), ROWS_STEP)
    words = jnp.concatenate([places_ref[d, block, :] for d in range(blocks)], axis=1)
    voxels = words >> 16
    weights = (words & (SHIFT - 1)).astype(jnp.float32) * (1 / LEVELS) * mass_row[...]
    for j in range(ROWS_STEP):
        local = voxels[j : j + 1, :]
        hot = jnp.where(iota_high == (local >> LOW_BITS), one, zero)
        low = jnp.where(iota_low == (local & (LOW - 1)), weights[j : j + 1, :], zero)
        part = lax.dot_general(
            hot.astype(jnp.bfloat16),
            low.astype(jnp.bfloat16),
            nt,
            preferred_element_type=jnp.float32,
        )
        row = pl.multiple_of((step * ROWS_STEP + j) * high_rows, 8)
        grid_ref[pl.ds(row, high_rows), :LOW] = part


def weight_rows(noise_ref, out_ref, grid_ref, part, ranges):
    side = noise_ref.shape[0]
    high_rows = grid_ref.shape[0] // side
    noise = noise_ref[...].astype(jnp.bfloat16)
    for h in range(out_ref.shape[0] // LOW):
        first = part * (high_rows // ranges) + h
        block = lax.dot_general(
            grid_ref[pl.ds(first, side, stride=high_rows), :].astype(jnp.bfloat16),
            noise,
            (((0,), (0,)), ((), ())),
            preferred_element_type=jnp.float32,
        )
        out_ref[h * LOW : (h + 1) * LOW, :] = block[:LOW].astype(out_ref.dtype)


def gather_kernel(
    orient,
    own_ref,
    templates_ref,
    noise_ref,
    index_ref,
    interp_ref,
    gathered_ref,
    post_ref,
    mass_ref,
    places_ref,
    rows_ref,
    clash_ref,
    images_ref,
    wide,
    words,
    words_in,
    raw,
    weighted,
    whole,
    scores,
    norms,
    stats,
    landed,
    load_sem,
    store_sem,
    send_sem,
    recv_sem,
    stat_send,
    stat_recv,
    word_send,
    word_recv,
):
    lines, across = LINES, orient // (2 * LINES)
    group, place = lax.axis_index("dp"), lax.axis_index("orient")
    core = lax.rem(place, 2)
    chip = lax.div(place, 2)
    row, col = lax.div(chip, across), lax.rem(chip, across)
    mesh_ids = pl.DeviceIdType.MESH
    block_rows, width = images_ref.shape
    part = width // PARTS
    count = templates_ref.shape[0]
    fold = templates_ref.shape[1] // width
    line_images = 2 * across * block_rows // fold
    images = line_images * lines

    def at(r, q, c):
        return (r * across + q) * 2 + c

    barrier = pltpu.get_barrier_semaphore()

    @pl.loop(1, orient)
    def _(s):
        pl.semaphore_signal(
            barrier,
            inc=1,
            device_id=(group, lax.rem(place + s, orient)),
            device_id_type=mesh_ids,
        )

    def load_copy(k):
        cols = pl.ds(pl.multiple_of(k * width, width), width)
        return pltpu.make_async_copy(
            templates_ref.at[:, cols], weighted.at[:, cols], load_sem.at[k]
        )

    for k in range(fold):
        load_copy(k).start()

    own_rows = own_ref.shape[0]
    for k in range(fold):
        wide[k * own_rows : (k + 1) * own_rows, :] = own_ref[
            :, k * width : (k + 1) * width
        ].astype(jnp.float32)
    images_ref[...] = wide[...].astype(jnp.bfloat16)
    index = index_ref[...]
    near = jnp.zeros(index.shape, jnp.int32)
    spot = lax.broadcasted_iota(jnp.int32, index.shape, 0) % SUB
    for d in range(1, SUB):
        same = (index == pltpu.roll(index, d, axis=0)) & (spot >= d)
        near = near | same.astype(jnp.int32)
    clash_ref[...] = jnp.zeros_like(clash_ref)
    for h in range(count // BATCH):
        clash_ref[h : h + 1, :] = jnp.max(
            near[h * BATCH : (h + 1) * BATCH, :], axis=0, keepdims=True
        )
    index_t = index.T
    for h in range(count // BATCH):
        rows_ref[pl.ds(h, index_t.shape[0], stride=count // BATCH), :] = index_t[
            :, h * BATCH : (h + 1) * BATCH
        ]
    level = (interp_ref[...] * LEVELS + 0.5).astype(jnp.int32)
    words[...] = (index * SHIFT + level).T
    pl.semaphore_wait(barrier, orient - 1)

    bearer = lax.rem(group, 2) == core

    def word_copy(source, r, way, target):
        return pltpu.make_async_remote_copy(
            src_ref=words if source is None else words_in.at[r],
            dst_ref=words_in.at[r],
            send_sem=word_send.at[r, way],
            recv_sem=word_recv.at[r],
            device_id=(group, target),
            device_id_type=mesh_ids,
        )

    def word_arrived(r):
        word_copy(words_in, r, 2, place + 1 - 2 * core).wait_recv()

    def each_word(r, act, source=words_in):
        for way, step in ((0, 1), (1, -1)):
            onward = row + step
            along = (onward >= 0) & (onward < lines)
            if source is not None:
                along = along & ((row - r) * step > 0)

            @pl.when(along)
            def _(way=way, onward=onward):
                act(word_copy(source, r, way, at(onward, col, core)))

        act(word_copy(source, r, 2, place + 1 - 2 * core))

    @pl.when(bearer)
    def _():
        each_word(row, lambda c: c.start(), None)

    def copy(source, r, q, s, way, target):
        cols = pl.ds(pl.multiple_of(s * part, part), part)
        slot = at(r, q, core)
        ref = images_ref if source is None else raw.at[slot]
        return pltpu.make_async_remote_copy(
            src_ref=ref.at[:, cols],
            dst_ref=raw.at[slot, :, cols],
            send_sem=send_sem.at[lax.div(slot, 2), s, way],
            recv_sem=recv_sem.at[slot, s],
            device_id=(group, target),
            device_id_type=mesh_ids,
        )

    def arrived(r, q, c, s):
        cols = pl.ds(pl.multiple_of(s * part, part), part)
        slot = at(r, q, c)
        pltpu.make_async_remote_copy(
            src_ref=raw.at[slot, :, cols],
            dst_ref=raw.at[slot, :, cols],
            send_sem=send_sem.at[0, 0, 0],
            recv_sem=recv_sem.at[slot, s],
            device_id=(group, place + 1 - 2 * core),
            device_id_type=mesh_ids,
        ).wait_recv()

    def each_send(r, q, s, act, source=raw):
        for way, step in ((0, 1), (1, -1)):
            onward = row + step
            if source is None:
                along = (onward >= 0) & (onward < lines)
            else:
                along = (q == col) & (onward >= 0) & (onward < lines) & ((row - r) * step > 0)

            @pl.when(along)
            def _(way=way, onward=onward):
                act(copy(source, r, q, s, way, at(onward, col, core)))

        for way, step in ((2, 1), (3, -1)):
            onward = col + step
            beside = (onward >= 0) & (onward < across) & ((col - q) * step >= 0)

            @pl.when(beside)
            def _(way=way, onward=onward):
                act(copy(source, r, q, s, way, at(row, onward, core)))

        act(copy(source, r, q, s, 4, place + 1 - 2 * core))

    @pl.loop(0, PARTS)
    def _(s):
        each_send(row, col, s, lambda c: c.start(), None)

    raw[place] = images_ref[...]
    scores[...] = jnp.zeros_like(scores)
    norms[...] = jnp.zeros_like(norms)

    def weigh(k):
        load_copy(k).wait()

        @pl.loop(0, width // NORM_COLS)
        def _(g):
            cols = pl.ds(pl.multiple_of(k * width + g * NORM_COLS, NORM_COLS), NORM_COLS)
            for h in range(0, count, 64):
                tpl = weighted[h : h + 64, cols].astype(jnp.float32)
                noise = noise_ref[:, cols]
                scaled = tpl * noise
                square = tpl * tpl * noise
                total = square[:, :LANES]
                for j in range(1, NORM_COLS // LANES):
                    total = total + square[:, j * LANES : (j + 1) * LANES]
                norms[h : h + 64, :] += total
                weighted[h : h + 64, cols] = scaled.astype(jnp.bfloat16)

    def score(r, s):
        for q in range(across):
            arrived(r, q, 1 - core, s)
        cols = pl.ds(pl.multiple_of(s * part, part), part)
        slots = pl.ds(pl.multiple_of(r * (2 * across), 2 * across), 2 * across)
        block = raw[slots, :, cols].reshape(2 * across * block_rows, part)
        total = 2 * across * block_rows
        out_row = lax.broadcasted_iota(jnp.int32, (total, total), 0)
        from_row = lax.broadcasted_iota(jnp.int32, (total, total), 1)
        image, piece = out_row % line_images, out_row // line_images
        wanted = (image // own_rows) * block_rows + piece * own_rows + image % own_rows
        pick = jnp.where(from_row == wanted, 1.0, 0.0).astype(jnp.bfloat16)
        sorted_ = jnp.dot(pick, block, preferred_element_type=jnp.float32)
        sorted_ = sorted_.astype(jnp.bfloat16)
        rows = pl.ds(pl.multiple_of(r * line_images, line_images), line_images)
        added = scores[rows, :]
        for k in range(fold):
            piece = sorted_[k * line_images : (k + 1) * line_images, :]
            span = pl.ds(pl.multiple_of(k * width + s * part, part), part)
            whole[rows, span] = piece
            added = added + lax.dot_general(
                piece,
                weighted[:, span],
                (((1,), (1,)), ((), ())),
                preferred_element_type=jnp.float32,
            )
        scores[rows, :] = added

    def store_copy(r):
        rows = pl.ds(pl.multiple_of(r * line_images, line_images), line_images)
        return pltpu.make_async_copy(whole.at[rows], gathered_ref.at[rows], store_sem.at[r])

    def score_store(r, s):
        score(r, s)

        @pl.when(s == PARTS - 1)
        def _():
            store_copy(r).start()

    @pl.loop(0, lines * PARTS + 1)
    def _(k):
        n, s = lax.div(k, PARTS) + 1, lax.rem(k, PARTS)
        for sign in (1, -1):
            r = row + sign * n

            @pl.when((r >= 0) & (r < lines) & (n < lines))
            def _(r=r):
                arrived(r, col, core, s)
                each_send(r, col, s, lambda c: c.start())

        for sign in (1, -1):
            r = row + sign * (n - 1)
            live = (r >= 0) & (r < lines) & (n <= lines)
            if sign < 0:
                live = live & (n > 1)
            for e in range(1, across):
                for side in (1, -1):
                    q = col + side * e

                    @pl.when(live & (q >= 0) & (q < across))
                    def _(r=r, q=q):
                        arrived(r, q, core, s)
                        each_send(r, q, s, lambda c: c.start())

        @pl.when(n == 1)
        def _():
            @pl.loop(0, fold // PARTS)
            def _(j):
                weigh(s * (fold // PARTS) + j)

        for sign in (1, -1):
            r = row + sign * s

            @pl.when(bearer & (n == 1) & (s > 0) & (r >= 0) & (r < lines))
            def _(r=r):
                word_arrived(r)
                each_word(r, lambda c: c.start())

        last = jnp.maximum(k - 1, 0)
        m, t = lax.div(last, PARTS) + 1, lax.rem(last, PARTS)

        @pl.when((m == 2) & (k > 0))
        def _():
            score_store(row, t)

        for sign in (1, -1):
            r = row + sign * (m - 1)

            @pl.when((m > 1) & (r >= 0) & (r < lines))
            def _(r=r):
                score_store(r, t)

    norm = 0.5 * jnp.sum(norms[...].T, axis=0, keepdims=True)
    value = (scores[...] - norm).T
    peak_own = jnp.max(value, axis=0, keepdims=True)
    expo = jnp.exp(value - peak_own)
    stats[...] = jnp.zeros_like(stats)
    stats[0:1, :] = peak_own
    stats[1:2, :] = jnp.sum(expo, axis=0, keepdims=True)

    def stat_copy(s):
        return pltpu.make_async_remote_copy(
            src_ref=stats,
            dst_ref=landed.at[s],
            send_sem=stat_send.at[s],
            recv_sem=stat_recv.at[s],
            device_id=(group, lax.rem(place + s, orient)),
            device_id_type=mesh_ids,
        )

    @pl.loop(1, orient)
    def _(s):
        stat_copy(s).start()

    landed[0] = stats[...]

    @pl.when(bearer)
    def _():
        words_in[row] = words[...]

    @pl.loop(1, orient)
    def _(s):
        stat_copy(s).wait()

    peak = peak_own
    for s in range(1, orient):
        peak = jnp.maximum(peak, landed[s, 0:1, :])
    total = jnp.zeros_like(peak)
    for s in range(orient):
        total = total + landed[s, 1:2, :] * jnp.exp(landed[s, 0:1, :] - peak)
    posterior = (expo * (jnp.exp(peak_own - peak) / total))[:, :images]
    post_ref[...] = posterior.astype(jnp.bfloat16)
    mass = jnp.sum(posterior, axis=1, keepdims=True)
    mass_t = jnp.broadcast_to(mass, (count, LANES)).T
    for h in range(count // LANES):
        mass_ref[h : h + 1, :] = mass_t[:1, h * LANES : (h + 1) * LANES]

    @pl.when(jnp.logical_not(bearer))
    def _():
        for r in range(lines):
            word_arrived(r)

    places_ref[...] = words_in[...]

    @pl.when(bearer)
    def _():
        each_word(row, lambda c: c.wait_send(), None)
        for r in range(lines):

            @pl.when(row != r)
            def _(r=r):
                each_word(r, lambda c: c.wait_send())

    for r in range(lines):
        store_copy(r).wait()

    @pl.loop(0, PARTS)
    def _(s):
        each_send(row, col, s, lambda c: c.wait_send(), None)
        for r in range(lines):
            for q in range(across):

                @pl.when((row != r) | (col != q))
                def _(r=r, q=q):
                    each_send(r, q, s, lambda c: c.wait_send())


def gather_scores(images, templates, index, interp, noise_flat, orient):
    own, pixels = images.shape
    count, side = index.shape
    fold = PARTS
    while own * fold % 16:
        fold += PARTS
    width = pixels // fold
    total = own * orient
    padded = -(-total // LANES) * LANES
    vmem = pl.BlockSpec(memory_space=pltpu.VMEM)
    hbm = pl.BlockSpec(memory_space=pl.ANY)
    chips = orient // 2
    return pl.pallas_call(
        functools.partial(gather_kernel, orient),
        out_shape=(
            jax.ShapeDtypeStruct((total, pixels), jnp.bfloat16),
            jax.ShapeDtypeStruct((count, total), jnp.bfloat16),
            jax.ShapeDtypeStruct((count // LANES, LANES), jnp.float32),
            jax.ShapeDtypeStruct((LINES, side, count), jnp.int32),
            jax.ShapeDtypeStruct((side * count // BATCH, BATCH), jnp.int32),
            jax.ShapeDtypeStruct((8, side), jnp.int32),
        ),
        in_specs=[vmem, hbm, vmem, vmem, vmem],
        out_specs=(hbm, vmem, vmem, vmem, vmem, vmem),
        scratch_shapes=[
            pltpu.VMEM((own * fold, width), jnp.bfloat16),
            pltpu.VMEM((own * fold, width), jnp.float32),
            pltpu.VMEM((side, count), jnp.int32),
            pltpu.VMEM((LINES, side, count), jnp.int32),
            pltpu.VMEM((orient, own * fold, width), jnp.bfloat16),
            pltpu.VMEM((count, pixels), jnp.bfloat16),
            pltpu.VMEM((total, pixels), jnp.bfloat16),
            pltpu.VMEM((padded, count), jnp.float32),
            pltpu.VMEM((count, LANES), jnp.float32),
            pltpu.VMEM((8, padded), jnp.float32),
            pltpu.VMEM((orient, 8, padded), jnp.float32),
            pltpu.SemaphoreType.DMA((fold,)),
            pltpu.SemaphoreType.DMA((LINES,)),
            pltpu.SemaphoreType.DMA((chips, PARTS, 5)),
            pltpu.SemaphoreType.DMA((orient, PARTS)),
            pltpu.SemaphoreType.DMA((orient,)),
            pltpu.SemaphoreType.DMA((orient,)),
            pltpu.SemaphoreType.DMA((LINES, 3)),
            pltpu.SemaphoreType.DMA((LINES,)),
        ],
        compiler_params=pltpu.CompilerParams(
            collective_id=1, has_side_effects=True, vmem_limit_bytes=VMEM_LIMIT
        ),
    )(images, templates, noise_flat, index, interp)


def shards(groups, orient, images, templates, index, interp, inv_noise):
    side = inv_noise.shape[0]
    gathered, post, mass, places, voxels, clash = gather_scores(
        images, templates, index, interp, inv_noise.reshape(1, -1), orient
    )
    volume = insert_data(post, gathered, interp, voxels, clash, side * side)
    return reduce_rows(
        volume, mass, places, inv_noise, groups, orient
    )


def solution(mesh):
    placed = (
        P(("dp", "orient"), None),
        P("orient", None),
        P("orient", None),
        P("orient", None),
        P(),
    )
    return jax.shard_map(
        functools.partial(shards, mesh.shape["dp"], mesh.shape["orient"]),
        mesh=mesh,
        in_specs=placed,
        out_specs=(P(("dp", "orient"), None), P(("dp", "orient"), None)),
        check_vma=False,
    )
```

```python
import functools

import jax
import jax.numpy as jnp
from jax import lax
from jax.experimental import pallas as pl
from jax.experimental.pallas import tpu as pltpu
from jax.sharding import PartitionSpec as P

LANES = 128
ROWS_STEP = 8
ACCS = 4
SUB = 4
BATCH = 128
SLOT = 512
COLS = 2
CHUNKS = 16
LINES = 4
PARTS = 4
NORM_COLS = 1024
LEVELS = 65535
SHIFT = 65536
LOW_BITS = 6
LOW = 1 << LOW_BITS
VMEM_LIMIT = 56 * 2**20


def data_kernel(
    post_ref,
    images_ref,
    interp_ref,
    idx_ref,
    clash_ref,
    out_ref,
    rows_ref,
    idx,
    idx_sem,
    out_sem,
    *accs,
):
    step, steps = pl.program_id(0), pl.num_programs(0)
    count, side = post_ref.shape[0], out_ref.shape[1]
    volume_rows = out_ref.shape[0]
    halves = count // BATCH
    slots = ROWS_STEP * count // SLOT
    each = SLOT // BATCH

    def fetch(at, u):
        return pltpu.make_async_copy(
            idx_ref.at[pl.ds((at * slots + u) * each, each)], idx.at[u], idx_sem.at[u]
        )

    @pl.when(step == 0)
    def _():
        for u in range(slots):
            fetch(step, u).start()

        @pl.loop(0, volume_rows // 64)
        def _(c):
            rows = pl.ds(pl.multiple_of(c * 64, 64), 64)
            for acc in accs:
                acc[rows, :] = jnp.zeros((64, side), jnp.float32)

    interp = pltpu.roll(interp_ref[...], lax.rem(side - step * ROWS_STEP, side), axis=1)
    for j in range(0, ROWS_STEP, COLS):
        block = jnp.dot(
            post_ref[...],
            images_ref[:, j * side : (j + COLS) * side],
            preferred_element_type=jnp.float32,
        )
        for i in range(COLS):
            rows_ref[(j + i) * count : (j + i + 1) * count, :] = (
                block[:, i * side : (i + 1) * side] * interp[:, j + i : j + i + 1]
            )

    for u in range(slots):
        fetch(step, u).wait()
        for b in range(each):
            base = (u * each + b) * BATCH
            clash = clash_ref[b % halves, step * ROWS_STEP + base // count]

            @pl.when(clash == 0)
            def _(u=u, b=b, base=base):
                pending = [()] * ACCS

                def flush(a):
                    for voxel, value in pending[a]:
                        accs[a][pl.ds(voxel, 1), :] = value

                for n in range(BATCH // SUB):
                    a = n % ACCS
                    flush(a)
                    pending[a] = []
                    for k in range(n * SUB, (n + 1) * SUB):
                        voxel = idx[u, b, k]
                        value = accs[a][pl.ds(voxel, 1), :] + rows_ref[base + k : base + k + 1, :]
                        pending[a].append((voxel, value))
                for a in range(ACCS):
                    flush(a)

            @pl.when(clash != 0)
            def _(u=u, b=b, base=base):
                @pl.loop(0, BATCH // ACCS)
                def _(q):
                    first = q * ACCS
                    targets = [idx[u, b, first + a] for a in range(ACCS)]
                    summed = [
                        accs[a][pl.ds(targets[a], 1), :]
                        + rows_ref[pl.ds(base + first + a, 1), :]
                        for a in range(ACCS)
                    ]
                    for a in range(ACCS):
                        accs[a][pl.ds(targets[a], 1), :] = summed[a]

        @pl.when(step < steps - 1)
        def _(u=u):
            fetch(step + 1, u).start()

    @pl.when(step == steps - 1)
    def _():
        chunk = volume_rows // CHUNKS

        def write(p):
            rows = pl.ds(pl.multiple_of(p * chunk, chunk), chunk)
            return pltpu.make_async_copy(accs[0].at[rows], out_ref.at[rows], out_sem.at[p])

        @pl.loop(0, CHUNKS)
        def _(p):
            @pl.loop(0, chunk // 64)
            def _(c):
                rows = pl.ds(pl.multiple_of(p * chunk + c * 64, 64), 64)
                total = accs[0][rows, :]
                for acc in accs[1:]:
                    total = total + acc[rows, :]
                accs[0][rows, :] = total

            write(p).start()

        @pl.loop(0, CHUNKS)
        def _(p):
            write(p).wait()


def insert_data(post, gathered, interp, voxels, clash, volume_rows):
    count, images = post.shape
    side = interp.shape[1]
    slots = ROWS_STEP * count // SLOT
    return pl.pallas_call(
        data_kernel,
        grid=(side // ROWS_STEP,),
        out_shape=jax.ShapeDtypeStruct((volume_rows, side), jnp.float32),
        in_specs=[
            pl.BlockSpec((count, images), lambda i: (0, 0)),
            pl.BlockSpec((images, ROWS_STEP * side), lambda i: (0, i)),
            pl.BlockSpec((count, side), lambda i: (0, 0)),
            pl.BlockSpec(memory_space=pl.ANY),
            pl.BlockSpec(memory_space=pltpu.SMEM),
        ],
        out_specs=pl.BlockSpec(memory_space=pl.ANY),
        scratch_shapes=[
            pltpu.VMEM((ROWS_STEP * count, side), jnp.float32),
            pltpu.SMEM((slots, SLOT // BATCH, BATCH), jnp.int32),
            pltpu.SemaphoreType.DMA((slots,)),
            pltpu.SemaphoreType.DMA((CHUNKS,)),
        ]
        + [pltpu.VMEM((volume_rows, side), jnp.float32)] * ACCS,
        compiler_params=pltpu.CompilerParams(vmem_limit_bytes=VMEM_LIMIT),
        cost_estimate=pl.CostEstimate(
            flops=200_000_000_000, bytes_accessed=200_000_000, transcendentals=0
        ),
    )(post, gathered, interp, voxels, clash)


def reduce_kernel(
    groups,
    orient,
    blocks_ref,
    mass_ref,
    places_ref,
    noise_ref,
    out_ref,
    weight_ref,
    grid_ref,
    mass_row,
    mine,
    theirs,
    first_x,
    first_x_in,
    first_y,
    first_y_in,
    second_x,
    second_x_in,
    second_y,
    second_y_in,
    last,
    last_in,
    masses,
    twin,
    twin_in,
    own_sem,
    pair_send,
    pair_recv,
    fx_send,
    fx_recv,
    fy_send,
    fy_recv,
    sx_send,
    sx_recv,
    sy_send,
    sy_recv,
    last_send,
    last_recv,
    mass_send,
    mass_recv,
    twin_send,
    twin_recv,
):
    lines, across = LINES, orient // (2 * LINES)
    devices = groups * orient
    group, place = lax.axis_index("dp"), lax.axis_index("orient")
    core, chip = lax.rem(place, 2), lax.div(place, 2)
    row, col = lax.div(chip, across), lax.rem(chip, across)
    rank = group * orient + place
    half = out_ref.shape[0] // 2
    mesh_ids = pl.DeviceIdType.MESH

    def ranked(d):
        return (lax.div(d, orient), lax.rem(d, orient))

    def line(k):
        return lax.rem(row + k + 1, lines)

    def group_at(i):
        return lax.rem(group + i, groups)

    def col_at(j):
        return lax.rem(col + j, across)

    def block(x, r, q):
        return (x * lines + r) * across + q

    def remote(source, target, send, recv, x, r, q, c):
        return pltpu.make_async_remote_copy(
            src_ref=source,
            dst_ref=target,
            send_sem=send,
            recv_sem=recv,
            device_id=(x, (r * across + q) * 2 + c),
            device_id_type=mesh_ids,
        )

    barrier = pltpu.get_barrier_semaphore()

    @pl.loop(1, devices)
    def _(s):
        pl.semaphore_signal(
            barrier,
            inc=1,
            device_id=ranked(lax.rem(rank + s, devices)),
            device_id_type=mesh_ids,
        )

    def own_copy(k, i, j):
        p = block(group_at(i), line(k), col_at(j))
        return pltpu.make_async_copy(
            blocks_ref.at[p, core], mine.at[p], own_sem.at[k, i * across + j]
        )

    for i in reversed(range(groups)):
        for j in reversed(range(across)):

            @pl.loop(0, lines)
            def _(k, i=i, j=j):
                own_copy(k, i, j).start()

    pl.semaphore_wait(barrier, devices - 1)

    def mass_copy(s):
        return pltpu.make_async_remote_copy(
            src_ref=mass_ref,
            dst_ref=masses.at[s],
            send_sem=mass_send.at[s],
            recv_sem=mass_recv.at[s],
            device_id=ranked(lax.rem(rank + s, devices)),
            device_id_type=mesh_ids,
        )

    def pair_copy(k, i, j):
        p, n = block(group_at(i), line(k), col_at(j)), i * across + j
        return remote(
            blocks_ref.at[p, 1 - core],
            theirs.at[p],
            pair_send.at[k, n],
            pair_recv.at[k, n],
            group,
            row,
            col,
            1 - core,
        )

    def first_x_copy(k, i):
        return remote(
            first_x.at[i - 1, k],
            first_x_in.at[i - 1, k],
            fx_send.at[i - 1, k],
            fx_recv.at[i - 1, k],
            group_at(i),
            row,
            col,
            core,
        )

    def first_y_copy(k, j):
        return remote(
            first_y.at[j - 1, k],
            first_y_in.at[j - 1, k],
            fy_send.at[j - 1, k],
            fy_recv.at[j - 1, k],
            group,
            row,
            col_at(j),
            core,
        )

    def second_x_copy(k, i):
        return remote(
            second_x.at[i - 1, k],
            second_x_in.at[i - 1, k],
            sx_send.at[i - 1, k],
            sx_recv.at[i - 1, k],
            group_at(i),
            row,
            col,
            core,
        )

    def second_y_copy(k, j):
        return remote(
            second_y.at[j - 1, k],
            second_y_in.at[j - 1, k],
            sy_send.at[j - 1, k],
            sy_recv.at[j - 1, k],
            group,
            row,
            col_at(j),
            core,
        )

    def last_copy(k):
        return remote(
            last.at[k],
            last_in.at[k],
            last_send.at[k],
            last_recv.at[k],
            group,
            line(k),
            col,
            core,
        )

    @pl.loop(0, lines)
    def _(k):
        for i in reversed(range(groups)):
            for j in reversed(range(across)):
                pair_copy(k, i, j).start()

    twin_group = group + 1 - 2 * lax.rem(group, 2)

    def column(d):
        return lax.rem(lax.div(lax.rem(d, orient), 2), across)

    def mass_sent(s):
        target = lax.rem(rank + s, devices)
        return (lax.rem(lax.div(target, orient), 2) == core) & (column(target) == col)

    @pl.loop(1, devices)
    def _(s):
        @pl.when(mass_sent(s))
        def _():
            mass_copy(s).start()

    def narrow(value):
        return value.astype(jnp.bfloat16)

    def begin(k):
        for i in reversed(range(groups)):
            for j in reversed(range(across)):
                x, q = group_at(i), col_at(j)
                p = block(x, line(k), q)
                own_copy(k, i, j).wait()
                pair_copy(k, i, j).wait()
                if i == 0 or j == 0:
                    total = mine[p] + theirs[p]
                    mine[p] = total
                    if i:
                        first_x[i - 1, k, q] = narrow(total[:half])
                    if j:
                        first_y[j - 1, k, x] = narrow(total[half:])
                else:
                    first_x[i - 1, k, q] = narrow(mine[p, :half] + theirs[p, :half])
                    first_y[j - 1, k, x] = narrow(mine[p, half:] + theirs[p, half:])
            if i:
                first_x_copy(k, i).start()
        for j in range(1, across):
            first_y_copy(k, j).start()

    def middle(k):
        for i in range(1, groups):
            first_x_copy(k, i).wait()
        for j in reversed(range(across)):
            q = col_at(j)
            p = block(group, line(k), q)
            total = mine[p, :half]
            for i in range(1, groups):
                total = total + first_x_in[i - 1, k, q].astype(jnp.float32)
            if j:
                second_y[j - 1, k] = narrow(total)
                second_y_copy(k, j).start()
            else:
                mine[p, :half] = total
        for j in range(1, across):
            first_y_copy(k, j).wait()
        for i in reversed(range(groups)):
            x = group_at(i)
            p = block(x, line(k), col)
            total = mine[p, half:]
            for j in range(1, across):
                total = total + first_y_in[j - 1, k, x].astype(jnp.float32)
            if i:
                second_x[i - 1, k] = narrow(total)
                second_x_copy(k, i).start()
            else:
                mine[p, half:] = total

    def end(k):
        p = block(group, line(k), col)
        for j in range(1, across):
            second_y_copy(k, j).wait()
        top = mine[p, :half]
        for j in range(1, across):
            top = top + second_y_in[j - 1, k].astype(jnp.float32)
        for i in range(1, groups):
            second_x_copy(k, i).wait()
        low = mine[p, half:]
        for i in range(1, groups):
            low = low + second_x_in[i - 1, k].astype(jnp.float32)

        @pl.when(k < lines - 1)
        def _():
            last[k, :half] = narrow(top)
            last[k, half:] = narrow(low)
            last_copy(k).start()

        @pl.when(k == lines - 1)
        def _():
            out_ref[:half] = top
            out_ref[half:] = low

    mass_row[...] = jnp.zeros_like(mass_row)
    mass_rows = mass_ref.shape[0]

    def add_mass(d, ref):
        start = lax.div(lax.rem(d, orient), 2 * across) * (mass_rows * LANES)
        for k in range(mass_rows):
            lanes = pl.ds(pl.multiple_of(start + k * LANES, LANES), LANES)
            mass_row[:, lanes] += ref[k : k + 1, :]

    steps, slots = noise_ref.shape[0] // ROWS_STEP, 3 * (lines + 2)

    def weigh(w):
        rows = out_ref.shape[0]
        firsts = [
            (x * orient + (row * across + col_at(j)) * 2 + core) * rows
            for x in (group, twin_group)
            for j in range(across)
        ]
        weight_step(w, firsts, places_ref, mass_row, grid_ref)

    def twin_copy(n):
        return remote(
            twin.at[n - 1],
            twin_in.at[n - 1],
            twin_send.at[n - 1],
            twin_recv.at[n - 1],
            (group, twin_group)[n // across],
            row,
            col_at(n % across),
            core,
        )

    @pl.loop(0, slots)
    def _(slot):
        k, turn = lax.div(slot, 3), lax.rem(slot, 3)

        @pl.when((turn == 0) & (k < lines))
        def _():
            begin(k)

        @pl.when((turn == 1) & (k >= 1) & (k < lines + 1))
        def _():
            middle(k - 1)

        @pl.when((turn == 2) & (k >= 2))
        def _():
            end(k - 2)

        @pl.when(slot == 1)
        def _():
            @pl.when(core == lax.rem(group, 2))
            def _():
                add_mass(rank, mass_ref)

            @pl.loop(1, devices)
            def _(s):
                sender = lax.rem(rank + devices - s, devices)

                @pl.when((lax.rem(sender, 2) == lax.rem(group, 2)) & (column(sender) == col))
                def _():
                    mass_copy(s).wait_recv()
                    add_mass(sender, masses.at[s])

                @pl.when(mass_sent(s))
                def _():
                    mass_copy(s).wait_send()

        @pl.when((slot >= 2) & (slot < 2 + steps // 2))
        def _():
            weigh(2 * slot - 4)
            weigh(2 * slot - 3)

        @pl.when(slot == 2 + steps // 2)
        def _():
            for n in range(1, 2 * across):
                weight_rows(noise_ref, twin.at[n - 1], grid_ref, n, 2 * across)
                twin_copy(n).start()

    weight_rows(noise_ref, weight_ref, grid_ref, 0, 2 * across)
    for n in range(1, 2 * across):
        twin_copy(n).wait()
        weight_ref[...] += twin_in[n - 1].astype(jnp.float32)
    for k in range(lines - 1):
        last_copy(k).wait()
        out_ref[...] += last_in[k].astype(jnp.float32)


def reduce_rows(volume, mass_rows, places_t, inv_noise, groups, orient):
    chips = groups * orient // 2
    lines, across = LINES, orient // (2 * LINES)
    rows, side = volume.shape[0] // (2 * chips), volume.shape[1]
    half = rows // 2
    parts = (chips, rows, side)
    masses = (2 * chips,) + mass_rows.shape
    shapes = [
        (groups - 1, lines, across, half, side),
        (across - 1, lines, groups, half, side),
        (groups - 1, lines, half, side),
        (across - 1, lines, half, side),
        (lines - 1, rows, side),
    ]
    sems = [
        (groups - 1, lines),
        (across - 1, lines),
        (groups - 1, lines),
        (across - 1, lines),
        (lines - 1,),
        (2 * chips,),
    ]
    return pl.pallas_call(
        functools.partial(reduce_kernel, groups, orient),
        out_shape=(
            jax.ShapeDtypeStruct((rows, side), jnp.float32),
            jax.ShapeDtypeStruct((rows, side), jnp.float32),
        ),
        in_specs=[pl.BlockSpec(memory_space=pl.ANY)]
        + [pl.BlockSpec(memory_space=pltpu.VMEM)] * 3,
        out_specs=(
            pl.BlockSpec(memory_space=pltpu.VMEM),
            pl.BlockSpec(memory_space=pltpu.VMEM),
        ),
        scratch_shapes=[
            pltpu.VMEM((2 * across * side * max(8, rows // LOW), LANES), jnp.float32),
            pltpu.VMEM((1, places_t.shape[0] * places_t.shape[2]), jnp.float32),
        ]
        + [pltpu.VMEM(parts, jnp.float32)] * 2
        + [pltpu.VMEM(s, jnp.bfloat16) for s in shapes for _ in range(2)]
        + [pltpu.VMEM(masses, jnp.float32)]
        + [pltpu.VMEM((2 * across - 1, rows, side), jnp.bfloat16)] * 2
        + [pltpu.SemaphoreType.DMA((lines, groups * across))] * 3
        + [pltpu.SemaphoreType.DMA(s) for s in sems for _ in range(2)]
        + [pltpu.SemaphoreType.DMA((2 * across - 1,))] * 2,
        compiler_params=pltpu.CompilerParams(
            collective_id=0, has_side_effects=True, vmem_limit_bytes=VMEM_LIMIT
        ),
    )(volume.reshape(chips, 2, rows, side), mass_rows, places_t, inv_noise)


def weight_step(step, firsts, places_ref, mass_row, grid_ref):
    blocks, side, each = places_ref.shape
    count = blocks * each
    high_rows = grid_ref.shape[0] // side
    nt = (((1,), (1,)), ((), ()))
    one, zero = jnp.float32(1), jnp.float32(0)
    spot = lax.broadcasted_iota(jnp.int32, (high_rows, count), 0)
    each_high = high_rows // len(firsts)
    iota_high = spot
    for n, first in enumerate(firsts):
        shift = lax.div(first, LOW) - n * each_high
        iota_high = jnp.where(spot // each_high == n, spot + shift, iota_high)
    iota_low = lax.broadcasted_iota(jnp.int32, (LOW, count), 0)
    block = pl.ds(pl.multiple_of(step * ROWS_STEP, ROWS_STEP), ROWS_STEP)
    words = jnp.concatenate([places_ref[d, block, :] for d in range(blocks)], axis=1)
    voxels = words >> 16
    weights = (words & (SHIFT - 1)).astype(jnp.float32) * (1 / LEVELS) * mass_row[...]
    for j in range(ROWS_STEP):
        local = voxels[j : j + 1, :]
        hot = jnp.where(iota_high == (local >> LOW_BITS), one, zero)
        low = jnp.where(iota_low == (local & (LOW - 1)), weights[j : j + 1, :], zero)
        part = lax.dot_general(
            hot.astype(jnp.bfloat16),
            low.astype(jnp.bfloat16),
            nt,
            preferred_element_type=jnp.float32,
        )
        row = pl.multiple_of((step * ROWS_STEP + j) * high_rows, 8)
        grid_ref[pl.ds(row, high_rows), :LOW] = part


def weight_rows(noise_ref, out_ref, grid_ref, part, ranges):
    side = noise_ref.shape[0]
    high_rows = grid_ref.shape[0] // side
    noise = noise_ref[...].astype(jnp.bfloat16)
    for h in range(out_ref.shape[0] // LOW):
        first = part * (high_rows // ranges) + h
        block = lax.dot_general(
            grid_ref[pl.ds(first, side, stride=high_rows), :].astype(jnp.bfloat16),
            noise,
            (((0,), (0,)), ((), ())),
            preferred_element_type=jnp.float32,
        )
        out_ref[h * LOW : (h + 1) * LOW, :] = block[:LOW].astype(out_ref.dtype)


def gather_kernel(
    orient,
    own_ref,
    templates_ref,
    noise_ref,
    index_ref,
    interp_ref,
    gathered_ref,
    post_ref,
    mass_ref,
    places_ref,
    rows_ref,
    clash_ref,
    images_ref,
    wide,
    words,
    words_in,
    raw,
    weighted,
    whole,
    scores,
    norms,
    stats,
    landed,
    load_sem,
    store_sem,
    send_sem,
    recv_sem,
    stat_send,
    stat_recv,
    word_send,
    word_recv,
):
    lines, across = LINES, orient // (2 * LINES)
    group, place = lax.axis_index("dp"), lax.axis_index("orient")
    core = lax.rem(place, 2)
    chip = lax.div(place, 2)
    row, col = lax.div(chip, across), lax.rem(chip, across)
    mesh_ids = pl.DeviceIdType.MESH
    block_rows, width = images_ref.shape
    part = width // PARTS
    count = templates_ref.shape[0]
    fold = templates_ref.shape[1] // width
    line_images = 2 * across * block_rows // fold
    images = line_images * lines

    def at(r, q, c):
        return (r * across + q) * 2 + c

    barrier = pltpu.get_barrier_semaphore()

    @pl.loop(1, orient)
    def _(s):
        pl.semaphore_signal(
            barrier,
            inc=1,
            device_id=(group, lax.rem(place + s, orient)),
            device_id_type=mesh_ids,
        )

    def load_copy(k):
        cols = pl.ds(pl.multiple_of(k * width, width), width)
        return pltpu.make_async_copy(
            templates_ref.at[:, cols], weighted.at[:, cols], load_sem.at[k]
        )

    for k in range(fold):
        load_copy(k).start()

    own_rows = own_ref.shape[0]
    for k in range(fold):
        wide[k * own_rows : (k + 1) * own_rows, :] = own_ref[
            :, k * width : (k + 1) * width
        ].astype(jnp.float32)
    images_ref[...] = wide[...].astype(jnp.bfloat16)
    index = index_ref[...]
    near = jnp.zeros(index.shape, jnp.int32)
    spot = lax.broadcasted_iota(jnp.int32, index.shape, 0) % SUB
    for d in range(1, SUB):
        same = (index == pltpu.roll(index, d, axis=0)) & (spot >= d)
        near = near | same.astype(jnp.int32)
    clash_ref[...] = jnp.zeros_like(clash_ref)
    for h in range(count // BATCH):
        clash_ref[h : h + 1, :] = jnp.max(
            near[h * BATCH : (h + 1) * BATCH, :], axis=0, keepdims=True
        )
    index_t = index.T
    for h in range(count // BATCH):
        rows_ref[pl.ds(h, index_t.shape[0], stride=count // BATCH), :] = index_t[
            :, h * BATCH : (h + 1) * BATCH
        ]
    level = (interp_ref[...] * LEVELS + 0.5).astype(jnp.int32)
    words[...] = (index * SHIFT + level).T
    pl.semaphore_wait(barrier, orient - 1)

    bearer = lax.rem(group, 2) == core

    def word_copy(source, r, way, target):
        return pltpu.make_async_remote_copy(
            src_ref=words if source is None else words_in.at[r],
            dst_ref=words_in.at[r],
            send_sem=word_send.at[r, way],
            recv_sem=word_recv.at[r],
            device_id=(group, target),
            device_id_type=mesh_ids,
        )

    def word_arrived(r):
        word_copy(words_in, r, 2, place + 1 - 2 * core).wait_recv()

    def each_word(r, act, source=words_in):
        for way, step in ((0, 1), (1, -1)):
            onward = row + step
            along = (onward >= 0) & (onward < lines)
            if source is not None:
                along = along & ((row - r) * step > 0)

            @pl.when(along)
            def _(way=way, onward=onward):
                act(word_copy(source, r, way, at(onward, col, core)))

        act(word_copy(source, r, 2, place + 1 - 2 * core))

    @pl.when(bearer)
    def _():
        each_word(row, lambda c: c.start(), None)

    def copy(source, r, q, s, way, target):
        cols = pl.ds(pl.multiple_of(s * part, part), part)
        slot = at(r, q, core)
        ref = images_ref if source is None else raw.at[slot]
        return pltpu.make_async_remote_copy(
            src_ref=ref.at[:, cols],
            dst_ref=raw.at[slot, :, cols],
            send_sem=send_sem.at[lax.div(slot, 2), s, way],
            recv_sem=recv_sem.at[slot, s],
            device_id=(group, target),
            device_id_type=mesh_ids,
        )

    def arrived(r, q, c, s):
        cols = pl.ds(pl.multiple_of(s * part, part), part)
        slot = at(r, q, c)
        pltpu.make_async_remote_copy(
            src_ref=raw.at[slot, :, cols],
            dst_ref=raw.at[slot, :, cols],
            send_sem=send_sem.at[0, 0, 0],
            recv_sem=recv_sem.at[slot, s],
            device_id=(group, place + 1 - 2 * core),
            device_id_type=mesh_ids,
        ).wait_recv()

    def each_send(r, q, s, act, source=raw):
        for way, step in ((0, 1), (1, -1)):
            onward = row + step
            if source is None:
                along = (onward >= 0) & (onward < lines)
            else:
                along = (q == col) & (onward >= 0) & (onward < lines) & ((row - r) * step > 0)

            @pl.when(along)
            def _(way=way, onward=onward):
                act(copy(source, r, q, s, way, at(onward, col, core)))

        for way, step in ((2, 1), (3, -1)):
            onward = col + step
            beside = (onward >= 0) & (onward < across) & ((col - q) * step >= 0)

            @pl.when(beside)
            def _(way=way, onward=onward):
                act(copy(source, r, q, s, way, at(row, onward, core)))

        act(copy(source, r, q, s, 4, place + 1 - 2 * core))

    @pl.loop(0, PARTS)
    def _(s):
        each_send(row, col, s, lambda c: c.start(), None)

    raw[place] = images_ref[...]
    scores[...] = jnp.zeros_like(scores)
    norms[...] = jnp.zeros_like(norms)

    def weigh(k):
        load_copy(k).wait()

        @pl.loop(0, width // NORM_COLS)
        def _(g):
            cols = pl.ds(pl.multiple_of(k * width + g * NORM_COLS, NORM_COLS), NORM_COLS)
            for h in range(0, count, 64):
                tpl = weighted[h : h + 64, cols].astype(jnp.float32)
                noise = noise_ref[:, cols]
                scaled = tpl * noise
                square = tpl * tpl * noise
                total = square[:, :LANES]
                for j in range(1, NORM_COLS // LANES):
                    total = total + square[:, j * LANES : (j + 1) * LANES]
                norms[h : h + 64, :] += total
                weighted[h : h + 64, cols] = scaled.astype(jnp.bfloat16)

    def score(r, s):
        for q in range(across):
            arrived(r, q, 1 - core, s)
        cols = pl.ds(pl.multiple_of(s * part, part), part)
        slots = pl.ds(pl.multiple_of(r * (2 * across), 2 * across), 2 * across)
        block = raw[slots, :, cols].reshape(2 * across * block_rows, part)
        total = 2 * across * block_rows
        out_row = lax.broadcasted_iota(jnp.int32, (total, total), 0)
        from_row = lax.broadcasted_iota(jnp.int32, (total, total), 1)
        image, piece = out_row % line_images, out_row // line_images
        wanted = (image // own_rows) * block_rows + piece * own_rows + image % own_rows
        pick = jnp.where(from_row == wanted, 1.0, 0.0).astype(jnp.bfloat16)
        sorted_ = jnp.dot(pick, block, preferred_element_type=jnp.float32)
        sorted_ = sorted_.astype(jnp.bfloat16)
        rows = pl.ds(pl.multiple_of(r * line_images, line_images), line_images)
        added = scores[rows, :]
        for k in range(fold):
            piece = sorted_[k * line_images : (k + 1) * line_images, :]
            span = pl.ds(pl.multiple_of(k * width + s * part, part), part)
            whole[rows, span] = piece
            added = added + lax.dot_general(
                piece,
                weighted[:, span],
                (((1,), (1,)), ((), ())),
                preferred_element_type=jnp.float32,
            )
        scores[rows, :] = added

    def store_copy(r):
        rows = pl.ds(pl.multiple_of(r * line_images, line_images), line_images)
        return pltpu.make_async_copy(whole.at[rows], gathered_ref.at[rows], store_sem.at[r])

    def score_store(r, s):
        score(r, s)

        @pl.when(s == PARTS - 1)
        def _():
            store_copy(r).start()

    @pl.loop(0, lines * PARTS + 1)
    def _(k):
        n, s = lax.div(k, PARTS) + 1, lax.rem(k, PARTS)
        for sign in (1, -1):
            r = row + sign * n

            @pl.when((r >= 0) & (r < lines) & (n < lines))
            def _(r=r):
                arrived(r, col, core, s)
                each_send(r, col, s, lambda c: c.start())

        for sign in (1, -1):
            r = row + sign * (n - 1)
            live = (r >= 0) & (r < lines) & (n <= lines)
            if sign < 0:
                live = live & (n > 1)
            for e in range(1, across):
                for side in (1, -1):
                    q = col + side * e

                    @pl.when(live & (q >= 0) & (q < across))
                    def _(r=r, q=q):
                        arrived(r, q, core, s)
                        each_send(r, q, s, lambda c: c.start())

        @pl.when(n == 1)
        def _():
            @pl.loop(0, fold // PARTS)
            def _(j):
                weigh(s * (fold // PARTS) + j)

        for sign in (1, -1):
            r = row + sign * s

            @pl.when(bearer & (n == 1) & (s > 0) & (r >= 0) & (r < lines))
            def _(r=r):
                word_arrived(r)
                each_word(r, lambda c: c.start())

        last = jnp.maximum(k - 1, 0)
        m, t = lax.div(last, PARTS) + 1, lax.rem(last, PARTS)

        @pl.when((m == 2) & (k > 0))
        def _():
            score_store(row, t)

        for sign in (1, -1):
            r = row + sign * (m - 1)

            @pl.when((m > 1) & (r >= 0) & (r < lines))
            def _(r=r):
                score_store(r, t)

    norm = 0.5 * jnp.sum(norms[...].T, axis=0, keepdims=True)
    value = (scores[...] - norm).T
    peak_own = jnp.max(value, axis=0, keepdims=True)
    expo = jnp.exp(value - peak_own)
    stats[...] = jnp.zeros_like(stats)
    stats[0:1, :] = peak_own
    stats[1:2, :] = jnp.sum(expo, axis=0, keepdims=True)

    def stat_copy(s):
        return pltpu.make_async_remote_copy(
            src_ref=stats,
            dst_ref=landed.at[s],
            send_sem=stat_send.at[s],
            recv_sem=stat_recv.at[s],
            device_id=(group, lax.rem(place + s, orient)),
            device_id_type=mesh_ids,
        )

    @pl.loop(1, orient)
    def _(s):
        stat_copy(s).start()

    landed[0] = stats[...]

    @pl.when(bearer)
    def _():
        words_in[row] = words[...]

    @pl.loop(1, orient)
    def _(s):
        stat_copy(s).wait()

    peak = peak_own
    for s in range(1, orient):
        peak = jnp.maximum(peak, landed[s, 0:1, :])
    total = jnp.zeros_like(peak)
    for s in range(orient):
        total = total + landed[s, 1:2, :] * jnp.exp(landed[s, 0:1, :] - peak)
    posterior = (expo * (jnp.exp(peak_own - peak) / total))[:, :images]
    post_ref[...] = posterior.astype(jnp.bfloat16)
    mass = jnp.sum(posterior, axis=1, keepdims=True)
    mass_t = jnp.broadcast_to(mass, (count, LANES)).T
    for h in range(count // LANES):
        mass_ref[h : h + 1, :] = mass_t[:1, h * LANES : (h + 1) * LANES]

    @pl.when(jnp.logical_not(bearer))
    def _():
        for r in range(lines):
            word_arrived(r)

    places_ref[...] = words_in[...]

    @pl.when(bearer)
    def _():
        each_word(row, lambda c: c.wait_send(), None)
        for r in range(lines):

            @pl.when(row != r)
            def _(r=r):
                each_word(r, lambda c: c.wait_send())

    for r in range(lines):
        store_copy(r).wait()

    @pl.loop(0, PARTS)
    def _(s):
        each_send(row, col, s, lambda c: c.wait_send(), None)
        for r in range(lines):
            for q in range(across):

                @pl.when((row != r) | (col != q))
                def _(r=r, q=q):
                    each_send(r, q, s, lambda c: c.wait_send())


def gather_scores(images, templates, index, interp, noise_flat, orient):
    own, pixels = images.shape
    count, side = index.shape
    fold = PARTS
    while own * fold % 16:
        fold += PARTS
    width = pixels // fold
    total = own * orient
    padded = -(-total // LANES) * LANES
    vmem = pl.BlockSpec(memory_space=pltpu.VMEM)
    hbm = pl.BlockSpec(memory_space=pl.ANY)
    chips = orient // 2
    return pl.pallas_call(
        functools.partial(gather_kernel, orient),
        out_shape=(
            jax.ShapeDtypeStruct((total, pixels), jnp.bfloat16),
            jax.ShapeDtypeStruct((count, total), jnp.bfloat16),
            jax.ShapeDtypeStruct((count // LANES, LANES), jnp.float32),
            jax.ShapeDtypeStruct((LINES, side, count), jnp.int32),
            jax.ShapeDtypeStruct((side * count // BATCH, BATCH), jnp.int32),
            jax.ShapeDtypeStruct((8, side), jnp.int32),
        ),
        in_specs=[vmem, hbm, vmem, vmem, vmem],
        out_specs=(hbm, vmem, vmem, vmem, vmem, vmem),
        scratch_shapes=[
            pltpu.VMEM((own * fold, width), jnp.bfloat16),
            pltpu.VMEM((own * fold, width), jnp.float32),
            pltpu.VMEM((side, count), jnp.int32),
            pltpu.VMEM((LINES, side, count), jnp.int32),
            pltpu.VMEM((orient, own * fold, width), jnp.bfloat16),
            pltpu.VMEM((count, pixels), jnp.bfloat16),
            pltpu.VMEM((total, pixels), jnp.bfloat16),
            pltpu.VMEM((padded, count), jnp.float32),
            pltpu.VMEM((count, LANES), jnp.float32),
            pltpu.VMEM((8, padded), jnp.float32),
            pltpu.VMEM((orient, 8, padded), jnp.float32),
            pltpu.SemaphoreType.DMA((fold,)),
            pltpu.SemaphoreType.DMA((LINES,)),
            pltpu.SemaphoreType.DMA((chips, PARTS, 5)),
            pltpu.SemaphoreType.DMA((orient, PARTS)),
            pltpu.SemaphoreType.DMA((orient,)),
            pltpu.SemaphoreType.DMA((orient,)),
            pltpu.SemaphoreType.DMA((LINES, 3)),
            pltpu.SemaphoreType.DMA((LINES,)),
        ],
        compiler_params=pltpu.CompilerParams(
            collective_id=1, has_side_effects=True, vmem_limit_bytes=VMEM_LIMIT
        ),
    )(images, templates, noise_flat, index, interp)


def shards(groups, orient, images, templates, index, interp, inv_noise):
    side = inv_noise.shape[0]
    gathered, post, mass, places, voxels, clash = gather_scores(
        images, templates, index, interp, inv_noise.reshape(1, -1), orient
    )
    volume = insert_data(post, gathered, interp, voxels, clash, side * side)
    return reduce_rows(
        volume, mass, places, inv_noise, groups, orient
    )


def solution(mesh):
    placed = (
        P(("dp", "orient"), None),
        P("orient", None),
        P("orient", None),
        P("orient", None),
        P(),
    )
    return jax.shard_map(
        functools.partial(shards, mesh.shape["dp"], mesh.shape["orient"]),
        mesh=mesh,
        in_specs=placed,
        out_specs=(P(("dp", "orient"), None), P(("dp", "orient"), None)),
        check_vma=False,
    )
```

```python
import functools

import jax
import jax.numpy as jnp
from jax import lax
from jax.experimental import pallas as pl
from jax.experimental.pallas import tpu as pltpu
from jax.sharding import PartitionSpec as P

LANES = 128
ROWS_STEP = 8
ACCS = 4
SUB = 4
BATCH = 128
SLOT = 512
COLS = 2
CHUNKS = 16
WORD_STEPS = 3
LINES = 4
PARTS = 4
NORM_COLS = 1024
LEVELS = 65535
SHIFT = 65536
LOW_BITS = 6
LOW = 1 << LOW_BITS
VMEM_LIMIT = 56 * 2**20


def data_kernel(
    post_ref,
    images_ref,
    interp_ref,
    idx_ref,
    clash_ref,
    out_ref,
    rows_ref,
    idx,
    idx_sem,
    out_sem,
    *accs,
):
    step, steps = pl.program_id(0), pl.num_programs(0)
    count, side = post_ref.shape[0], out_ref.shape[1]
    volume_rows = out_ref.shape[0]
    halves = count // BATCH
    slots = ROWS_STEP * count // SLOT
    each = SLOT // BATCH

    def fetch(at, u):
        return pltpu.make_async_copy(
            idx_ref.at[pl.ds((at * slots + u) * each, each)], idx.at[u], idx_sem.at[u]
        )

    @pl.when(step == 0)
    def _():
        for u in range(slots):
            fetch(step, u).start()

        @pl.loop(0, volume_rows // 64)
        def _(c):
            rows = pl.ds(pl.multiple_of(c * 64, 64), 64)
            for acc in accs:
                acc[rows, :] = jnp.zeros((64, side), jnp.float32)

    interp = pltpu.roll(interp_ref[...], lax.rem(side - step * ROWS_STEP, side), axis=1)
    for j in range(0, ROWS_STEP, COLS):
        block = jnp.dot(
            post_ref[...],
            images_ref[:, j * side : (j + COLS) * side],
            preferred_element_type=jnp.float32,
        )
        for i in range(COLS):
            rows_ref[(j + i) * count : (j + i + 1) * count, :] = (
                block[:, i * side : (i + 1) * side] * interp[:, j + i : j + i + 1]
            )

    for u in range(slots):
        fetch(step, u).wait()
        for b in range(each):
            base = (u * each + b) * BATCH
            clash = clash_ref[b % halves, step * ROWS_STEP + base // count]

            @pl.when(clash == 0)
            def _(u=u, b=b, base=base):
                pending = [()] * ACCS

                def flush(a):
                    for voxel, value in pending[a]:
                        accs[a][pl.ds(voxel, 1), :] = value

                for n in range(BATCH // SUB):
                    a = n % ACCS
                    flush(a)
                    pending[a] = []
                    for k in range(n * SUB, (n + 1) * SUB):
                        voxel = idx[u, b, k]
                        value = accs[a][pl.ds(voxel, 1), :] + rows_ref[base + k : base + k + 1, :]
                        pending[a].append((voxel, value))
                for a in range(ACCS):
                    flush(a)

            @pl.when(clash != 0)
            def _(u=u, b=b, base=base):
                @pl.loop(0, BATCH // ACCS)
                def _(q):
                    first = q * ACCS
                    targets = [idx[u, b, first + a] for a in range(ACCS)]
                    summed = [
                        accs[a][pl.ds(targets[a], 1), :]
                        + rows_ref[pl.ds(base + first + a, 1), :]
                        for a in range(ACCS)
                    ]
                    for a in range(ACCS):
                        accs[a][pl.ds(targets[a], 1), :] = summed[a]

        @pl.when(step < steps - 1)
        def _(u=u):
            fetch(step + 1, u).start()

    @pl.when(step == steps - 1)
    def _():
        chunk = volume_rows // CHUNKS

        def write(p):
            rows = pl.ds(pl.multiple_of(p * chunk, chunk), chunk)
            return pltpu.make_async_copy(accs[0].at[rows], out_ref.at[rows], out_sem.at[p])

        @pl.loop(0, CHUNKS)
        def _(p):
            @pl.loop(0, chunk // 64)
            def _(c):
                rows = pl.ds(pl.multiple_of(p * chunk + c * 64, 64), 64)
                total = accs[0][rows, :]
                for acc in accs[1:]:
                    total = total + acc[rows, :]
                accs[0][rows, :] = total

            write(p).start()

        @pl.loop(0, CHUNKS)
        def _(p):
            write(p).wait()


def insert_data(post, gathered, interp, voxels, clash, volume_rows):
    count, images = post.shape
    side = interp.shape[1]
    slots = ROWS_STEP * count // SLOT
    return pl.pallas_call(
        data_kernel,
        grid=(side // ROWS_STEP,),
        out_shape=jax.ShapeDtypeStruct((volume_rows, side), jnp.float32),
        in_specs=[
            pl.BlockSpec((count, images), lambda i: (0, 0)),
            pl.BlockSpec((images, ROWS_STEP * side), lambda i: (0, i)),
            pl.BlockSpec((count, side), lambda i: (0, 0)),
            pl.BlockSpec(memory_space=pl.ANY),
            pl.BlockSpec(memory_space=pltpu.SMEM),
        ],
        out_specs=pl.BlockSpec(memory_space=pl.ANY),
        scratch_shapes=[
            pltpu.VMEM((ROWS_STEP * count, side), jnp.float32),
            pltpu.SMEM((slots, SLOT // BATCH, BATCH), jnp.int32),
            pltpu.SemaphoreType.DMA((slots,)),
            pltpu.SemaphoreType.DMA((CHUNKS,)),
        ]
        + [pltpu.VMEM((volume_rows, side), jnp.float32)] * ACCS,
        compiler_params=pltpu.CompilerParams(vmem_limit_bytes=VMEM_LIMIT),
        cost_estimate=pl.CostEstimate(
            flops=200_000_000_000, bytes_accessed=200_000_000, transcendentals=0
        ),
    )(post, gathered, interp, voxels, clash)


def reduce_kernel(
    groups,
    orient,
    blocks_ref,
    mass_ref,
    places_ref,
    noise_ref,
    out_ref,
    weight_ref,
    grid_ref,
    mass_row,
    mine,
    theirs,
    first_x,
    first_x_in,
    first_y,
    first_y_in,
    second_x,
    second_x_in,
    second_y,
    second_y_in,
    last,
    last_in,
    masses,
    twin,
    twin_in,
    own_sem,
    pair_send,
    pair_recv,
    fx_send,
    fx_recv,
    fy_send,
    fy_recv,
    sx_send,
    sx_recv,
    sy_send,
    sy_recv,
    last_send,
    last_recv,
    mass_send,
    mass_recv,
    twin_send,
    twin_recv,
):
    lines, across = LINES, orient // (2 * LINES)
    devices = groups * orient
    group, place = lax.axis_index("dp"), lax.axis_index("orient")
    core, chip = lax.rem(place, 2), lax.div(place, 2)
    row, col = lax.div(chip, across), lax.rem(chip, across)
    rank = group * orient + place
    half = out_ref.shape[0] // 2
    mesh_ids = pl.DeviceIdType.MESH

    def ranked(d):
        return (lax.div(d, orient), lax.rem(d, orient))

    def line(k):
        return lax.rem(row + k + 1, lines)

    def group_at(i):
        return lax.rem(group + i, groups)

    def col_at(j):
        return lax.rem(col + j, across)

    def block(x, r, q):
        return (x * lines + r) * across + q

    def remote(source, target, send, recv, x, r, q, c):
        return pltpu.make_async_remote_copy(
            src_ref=source,
            dst_ref=target,
            send_sem=send,
            recv_sem=recv,
            device_id=(x, (r * across + q) * 2 + c),
            device_id_type=mesh_ids,
        )

    barrier = pltpu.get_barrier_semaphore()

    @pl.loop(1, devices)
    def _(s):
        pl.semaphore_signal(
            barrier,
            inc=1,
            device_id=ranked(lax.rem(rank + s, devices)),
            device_id_type=mesh_ids,
        )

    def own_copy(k, i, j):
        p = block(group_at(i), line(k), col_at(j))
        return pltpu.make_async_copy(
            blocks_ref.at[p, core], mine.at[p], own_sem.at[k, i * across + j]
        )

    for i in reversed(range(groups)):
        for j in reversed(range(across)):

            @pl.loop(0, lines)
            def _(k, i=i, j=j):
                own_copy(k, i, j).start()

    pl.semaphore_wait(barrier, devices - 1)

    def mass_copy(s):
        return pltpu.make_async_remote_copy(
            src_ref=mass_ref,
            dst_ref=masses.at[s],
            send_sem=mass_send.at[s],
            recv_sem=mass_recv.at[s],
            device_id=ranked(lax.rem(rank + s, devices)),
            device_id_type=mesh_ids,
        )

    def pair_copy(k, i, j):
        p, n = block(group_at(i), line(k), col_at(j)), i * across + j
        return remote(
            blocks_ref.at[p, 1 - core],
            theirs.at[p],
            pair_send.at[k, n],
            pair_recv.at[k, n],
            group,
            row,
            col,
            1 - core,
        )

    def first_x_copy(k, i):
        return remote(
            first_x.at[i - 1, k],
            first_x_in.at[i - 1, k],
            fx_send.at[i - 1, k],
            fx_recv.at[i - 1, k],
            group_at(i),
            row,
            col,
            core,
        )

    def first_y_copy(k, j):
        return remote(
            first_y.at[j - 1, k],
            first_y_in.at[j - 1, k],
            fy_send.at[j - 1, k],
            fy_recv.at[j - 1, k],
            group,
            row,
            col_at(j),
            core,
        )

    def second_x_copy(k, i):
        return remote(
            second_x.at[i - 1, k],
            second_x_in.at[i - 1, k],
            sx_send.at[i - 1, k],
            sx_recv.at[i - 1, k],
            group_at(i),
            row,
            col,
            core,
        )

    def second_y_copy(k, j):
        return remote(
            second_y.at[j - 1, k],
            second_y_in.at[j - 1, k],
            sy_send.at[j - 1, k],
            sy_recv.at[j - 1, k],
            group,
            row,
            col_at(j),
            core,
        )

    def last_copy(k):
        return remote(
            last.at[k],
            last_in.at[k],
            last_send.at[k],
            last_recv.at[k],
            group,
            line(k),
            col,
            core,
        )

    @pl.loop(0, lines)
    def _(k):
        for i in reversed(range(groups)):
            for j in reversed(range(across)):
                pair_copy(k, i, j).start()

    twin_group = group + 1 - 2 * lax.rem(group, 2)

    def column(d):
        return lax.rem(lax.div(lax.rem(d, orient), 2), across)

    def mass_sent(s):
        target = lax.rem(rank + s, devices)
        return (lax.rem(lax.div(target, orient), 2) == core) & (column(target) == col)

    @pl.loop(1, devices)
    def _(s):
        @pl.when(mass_sent(s))
        def _():
            mass_copy(s).start()

    def narrow(value):
        return value.astype(jnp.bfloat16)

    def begin(k):
        for i in reversed(range(groups)):
            for j in reversed(range(across)):
                x, q = group_at(i), col_at(j)
                p = block(x, line(k), q)
                own_copy(k, i, j).wait()
                pair_copy(k, i, j).wait()
                if i == 0 or j == 0:
                    total = mine[p] + theirs[p]
                    mine[p] = total
                    if i:
                        first_x[i - 1, k, q] = narrow(total[:half])
                    if j:
                        first_y[j - 1, k, x] = narrow(total[half:])
                else:
                    first_x[i - 1, k, q] = narrow(mine[p, :half] + theirs[p, :half])
                    first_y[j - 1, k, x] = narrow(mine[p, half:] + theirs[p, half:])
            if i:
                first_x_copy(k, i).start()
        for j in range(1, across):
            first_y_copy(k, j).start()

    def middle(k):
        for i in range(1, groups):
            first_x_copy(k, i).wait()
        for j in reversed(range(across)):
            q = col_at(j)
            p = block(group, line(k), q)
            total = mine[p, :half]
            for i in range(1, groups):
                total = total + first_x_in[i - 1, k, q].astype(jnp.float32)
            if j:
                second_y[j - 1, k] = narrow(total)
                second_y_copy(k, j).start()
            else:
                mine[p, :half] = total
        for j in range(1, across):
            first_y_copy(k, j).wait()
        for i in reversed(range(groups)):
            x = group_at(i)
            p = block(x, line(k), col)
            total = mine[p, half:]
            for j in range(1, across):
                total = total + first_y_in[j - 1, k, x].astype(jnp.float32)
            if i:
                second_x[i - 1, k] = narrow(total)
                second_x_copy(k, i).start()
            else:
                mine[p, half:] = total

    def end(k):
        p = block(group, line(k), col)
        for j in range(1, across):
            second_y_copy(k, j).wait()
        top = mine[p, :half]
        for j in range(1, across):
            top = top + second_y_in[j - 1, k].astype(jnp.float32)
        for i in range(1, groups):
            second_x_copy(k, i).wait()
        low = mine[p, half:]
        for i in range(1, groups):
            low = low + second_x_in[i - 1, k].astype(jnp.float32)

        @pl.when(k < lines - 1)
        def _():
            last[k, :half] = narrow(top)
            last[k, half:] = narrow(low)
            last_copy(k).start()

        @pl.when(k == lines - 1)
        def _():
            out_ref[:half] = top
            out_ref[half:] = low

    mass_row[...] = jnp.zeros_like(mass_row)
    mass_rows = mass_ref.shape[0]

    def add_mass(d, ref):
        start = lax.div(lax.rem(d, orient), 2 * across) * (mass_rows * LANES)
        for k in range(mass_rows):
            lanes = pl.ds(pl.multiple_of(start + k * LANES, LANES), LANES)
            mass_row[:, lanes] += ref[k : k + 1, :]

    steps, slots = noise_ref.shape[0] // ROWS_STEP, 3 * (lines + 2)

    def weigh(w):
        rows = out_ref.shape[0]
        firsts = [
            (x * orient + (row * across + col_at(j)) * 2 + core) * rows
            for x in (group, twin_group)
            for j in range(across)
        ]
        weight_step(w, firsts, places_ref, mass_row, grid_ref)

    def twin_copy(n):
        return remote(
            twin.at[n - 1],
            twin_in.at[n - 1],
            twin_send.at[n - 1],
            twin_recv.at[n - 1],
            (group, twin_group)[n // across],
            row,
            col_at(n % across),
            core,
        )

    @pl.loop(0, slots)
    def _(slot):
        k, turn = lax.div(slot, 3), lax.rem(slot, 3)

        @pl.when((turn == 0) & (k < lines))
        def _():
            begin(k)

        @pl.when((turn == 1) & (k >= 1) & (k < lines + 1))
        def _():
            middle(k - 1)

        @pl.when((turn == 2) & (k >= 2))
        def _():
            end(k - 2)

        @pl.when(slot == 1)
        def _():
            @pl.when(core == lax.rem(group, 2))
            def _():
                add_mass(rank, mass_ref)

            @pl.loop(1, devices)
            def _(s):
                sender = lax.rem(rank + devices - s, devices)

                @pl.when((lax.rem(sender, 2) == lax.rem(group, 2)) & (column(sender) == col))
                def _():
                    mass_copy(s).wait_recv()
                    add_mass(sender, masses.at[s])

                @pl.when(mass_sent(s))
                def _():
                    mass_copy(s).wait_send()

        @pl.when((slot >= 2) & (slot < 2 + steps // 2))
        def _():
            weigh(2 * slot - 4)
            weigh(2 * slot - 3)

        @pl.when(slot == 2 + steps // 2)
        def _():
            for n in range(1, 2 * across):
                weight_rows(noise_ref, twin.at[n - 1], grid_ref, n, 2 * across)
                twin_copy(n).start()

    weight_rows(noise_ref, weight_ref, grid_ref, 0, 2 * across)
    for n in range(1, 2 * across):
        twin_copy(n).wait()
        weight_ref[...] += twin_in[n - 1].astype(jnp.float32)
    for k in range(lines - 1):
        last_copy(k).wait()
        out_ref[...] += last_in[k].astype(jnp.float32)


def reduce_rows(volume, mass_rows, places_t, inv_noise, groups, orient):
    chips = groups * orient // 2
    lines, across = LINES, orient // (2 * LINES)
    rows, side = volume.shape[0] // (2 * chips), volume.shape[1]
    half = rows // 2
    parts = (chips, rows, side)
    masses = (2 * chips,) + mass_rows.shape
    shapes = [
        (groups - 1, lines, across, half, side),
        (across - 1, lines, groups, half, side),
        (groups - 1, lines, half, side),
        (across - 1, lines, half, side),
        (lines - 1, rows, side),
    ]
    sems = [
        (groups - 1, lines),
        (across - 1, lines),
        (groups - 1, lines),
        (across - 1, lines),
        (lines - 1,),
        (2 * chips,),
    ]
    return pl.pallas_call(
        functools.partial(reduce_kernel, groups, orient),
        out_shape=(
            jax.ShapeDtypeStruct((rows, side), jnp.float32),
            jax.ShapeDtypeStruct((rows, side), jnp.float32),
        ),
        in_specs=[pl.BlockSpec(memory_space=pl.ANY)]
        + [pl.BlockSpec(memory_space=pltpu.VMEM)] * 3,
        out_specs=(
            pl.BlockSpec(memory_space=pltpu.VMEM),
            pl.BlockSpec(memory_space=pltpu.VMEM),
        ),
        scratch_shapes=[
            pltpu.VMEM((2 * across * side * max(8, rows // LOW), LANES), jnp.float32),
            pltpu.VMEM((1, places_t.shape[0] * places_t.shape[2]), jnp.float32),
        ]
        + [pltpu.VMEM(parts, jnp.float32)] * 2
        + [pltpu.VMEM(s, jnp.bfloat16) for s in shapes for _ in range(2)]
        + [pltpu.VMEM(masses, jnp.float32)]
        + [pltpu.VMEM((2 * across - 1, rows, side), jnp.bfloat16)] * 2
        + [pltpu.SemaphoreType.DMA((lines, groups * across))] * 3
        + [pltpu.SemaphoreType.DMA(s) for s in sems for _ in range(2)]
        + [pltpu.SemaphoreType.DMA((2 * across - 1,))] * 2,
        compiler_params=pltpu.CompilerParams(
            collective_id=0, has_side_effects=True, vmem_limit_bytes=VMEM_LIMIT
        ),
    )(volume.reshape(chips, 2, rows, side), mass_rows, places_t, inv_noise)


def weight_step(step, firsts, places_ref, mass_row, grid_ref):
    blocks, side, each = places_ref.shape
    count = blocks * each
    high_rows = grid_ref.shape[0] // side
    nt = (((1,), (1,)), ((), ()))
    one, zero = jnp.float32(1), jnp.float32(0)
    spot = lax.broadcasted_iota(jnp.int32, (high_rows, count), 0)
    each_high = high_rows // len(firsts)
    iota_high = spot
    for n, first in enumerate(firsts):
        shift = lax.div(first, LOW) - n * each_high
        iota_high = jnp.where(spot // each_high == n, spot + shift, iota_high)
    iota_low = lax.broadcasted_iota(jnp.int32, (LOW, count), 0)
    block = pl.ds(pl.multiple_of(step * ROWS_STEP, ROWS_STEP), ROWS_STEP)
    words = jnp.concatenate([places_ref[d, block, :] for d in range(blocks)], axis=1)
    voxels = words >> 16
    weights = (words & (SHIFT - 1)).astype(jnp.float32) * (1 / LEVELS) * mass_row[...]
    for j in range(ROWS_STEP):
        local = voxels[j : j + 1, :]
        hot = jnp.where(iota_high == (local >> LOW_BITS), one, zero)
        low = jnp.where(iota_low == (local & (LOW - 1)), weights[j : j + 1, :], zero)
        part = lax.dot_general(
            hot.astype(jnp.bfloat16),
            low.astype(jnp.bfloat16),
            nt,
            preferred_element_type=jnp.float32,
        )
        row = pl.multiple_of((step * ROWS_STEP + j) * high_rows, 8)
        grid_ref[pl.ds(row, high_rows), :LOW] = part


def weight_rows(noise_ref, out_ref, grid_ref, part, ranges):
    side = noise_ref.shape[0]
    high_rows = grid_ref.shape[0] // side
    noise = noise_ref[...].astype(jnp.bfloat16)
    for h in range(out_ref.shape[0] // LOW):
        first = part * (high_rows // ranges) + h
        block = lax.dot_general(
            grid_ref[pl.ds(first, side, stride=high_rows), :].astype(jnp.bfloat16),
            noise,
            (((0,), (0,)), ((), ())),
            preferred_element_type=jnp.float32,
        )
        out_ref[h * LOW : (h + 1) * LOW, :] = block[:LOW].astype(out_ref.dtype)


def gather_kernel(
    orient,
    own_ref,
    templates_ref,
    noise_ref,
    index_ref,
    interp_ref,
    gathered_ref,
    post_ref,
    mass_ref,
    places_ref,
    rows_ref,
    clash_ref,
    images_ref,
    wide,
    words,
    words_in,
    raw,
    weighted,
    whole,
    scores,
    norms,
    stats,
    landed,
    load_sem,
    store_sem,
    send_sem,
    recv_sem,
    stat_send,
    stat_recv,
    word_send,
    word_recv,
):
    lines, across = LINES, orient // (2 * LINES)
    group, place = lax.axis_index("dp"), lax.axis_index("orient")
    core = lax.rem(place, 2)
    chip = lax.div(place, 2)
    row, col = lax.div(chip, across), lax.rem(chip, across)
    mesh_ids = pl.DeviceIdType.MESH
    block_rows, width = images_ref.shape
    part = width // PARTS
    count = templates_ref.shape[0]
    fold = templates_ref.shape[1] // width
    line_images = 2 * across * block_rows // fold
    images = line_images * lines

    def at(r, q, c):
        return (r * across + q) * 2 + c

    barrier = pltpu.get_barrier_semaphore()

    @pl.loop(1, orient)
    def _(s):
        pl.semaphore_signal(
            barrier,
            inc=1,
            device_id=(group, lax.rem(place + s, orient)),
            device_id_type=mesh_ids,
        )

    def load_copy(k):
        cols = pl.ds(pl.multiple_of(k * width, width), width)
        return pltpu.make_async_copy(
            templates_ref.at[:, cols], weighted.at[:, cols], load_sem.at[k]
        )

    for k in range(fold):
        load_copy(k).start()

    own_rows = own_ref.shape[0]
    for k in range(fold):
        wide[k * own_rows : (k + 1) * own_rows, :] = own_ref[
            :, k * width : (k + 1) * width
        ].astype(jnp.float32)
    images_ref[...] = wide[...].astype(jnp.bfloat16)
    index = index_ref[...]
    near = jnp.zeros(index.shape, jnp.int32)
    spot = lax.broadcasted_iota(jnp.int32, index.shape, 0) % SUB
    for d in range(1, SUB):
        same = (index == pltpu.roll(index, d, axis=0)) & (spot >= d)
        near = near | same.astype(jnp.int32)
    clash_ref[...] = jnp.zeros_like(clash_ref)
    for h in range(count // BATCH):
        clash_ref[h : h + 1, :] = jnp.max(
            near[h * BATCH : (h + 1) * BATCH, :], axis=0, keepdims=True
        )
    index_t = index.T
    for h in range(count // BATCH):
        rows_ref[pl.ds(h, index_t.shape[0], stride=count // BATCH), :] = index_t[
            :, h * BATCH : (h + 1) * BATCH
        ]
    level = (interp_ref[...] * LEVELS + 0.5).astype(jnp.int32)
    words[...] = (index * SHIFT + level).T
    pl.semaphore_wait(barrier, orient - 1)

    bearer = lax.rem(group, 2) == core

    def word_copy(source, r, way, target):
        return pltpu.make_async_remote_copy(
            src_ref=words if source is None else words_in.at[r],
            dst_ref=words_in.at[r],
            send_sem=word_send.at[r, way],
            recv_sem=word_recv.at[r],
            device_id=(group, target),
            device_id_type=mesh_ids,
        )

    def word_arrived(r):
        word_copy(words_in, r, 2, place + 1 - 2 * core).wait_recv()

    def each_word(r, act, source=words_in):
        for way, step in ((0, 1), (1, -1)):
            onward = row + step
            along = (onward >= 0) & (onward < lines)
            if source is not None:
                along = along & ((row - r) * step > 0)

            @pl.when(along)
            def _(way=way, onward=onward):
                act(word_copy(source, r, way, at(onward, col, core)))

        act(word_copy(source, r, 2, place + 1 - 2 * core))

    @pl.when(bearer)
    def _():
        each_word(row, lambda c: c.start(), None)

    def copy(source, r, q, s, way, target):
        cols = pl.ds(pl.multiple_of(s * part, part), part)
        slot = at(r, q, core)
        ref = images_ref if source is None else raw.at[slot]
        return pltpu.make_async_remote_copy(
            src_ref=ref.at[:, cols],
            dst_ref=raw.at[slot, :, cols],
            send_sem=send_sem.at[lax.div(slot, 2), s, way],
            recv_sem=recv_sem.at[slot, s],
            device_id=(group, target),
            device_id_type=mesh_ids,
        )

    def arrived(r, q, c, s):
        cols = pl.ds(pl.multiple_of(s * part, part), part)
        slot = at(r, q, c)
        pltpu.make_async_remote_copy(
            src_ref=raw.at[slot, :, cols],
            dst_ref=raw.at[slot, :, cols],
            send_sem=send_sem.at[0, 0, 0],
            recv_sem=recv_sem.at[slot, s],
            device_id=(group, place + 1 - 2 * core),
            device_id_type=mesh_ids,
        ).wait_recv()

    def each_send(r, q, s, act, source=raw):
        for way, step in ((0, 1), (1, -1)):
            onward = row + step
            if source is None:
                along = (onward >= 0) & (onward < lines)
            else:
                along = (q == col) & (onward >= 0) & (onward < lines) & ((row - r) * step > 0)

            @pl.when(along)
            def _(way=way, onward=onward):
                act(copy(source, r, q, s, way, at(onward, col, core)))

        for way, step in ((2, 1), (3, -1)):
            onward = col + step
            beside = (onward >= 0) & (onward < across) & ((col - q) * step >= 0)

            @pl.when(beside)
            def _(way=way, onward=onward):
                act(copy(source, r, q, s, way, at(row, onward, core)))

        act(copy(source, r, q, s, 4, place + 1 - 2 * core))

    @pl.loop(0, PARTS)
    def _(s):
        each_send(row, col, s, lambda c: c.start(), None)

    raw[place] = images_ref[...]
    scores[...] = jnp.zeros_like(scores)
    norms[...] = jnp.zeros_like(norms)

    def weigh(k):
        load_copy(k).wait()

        @pl.loop(0, width // NORM_COLS)
        def _(g):
            cols = pl.ds(pl.multiple_of(k * width + g * NORM_COLS, NORM_COLS), NORM_COLS)
            for h in range(0, count, 64):
                tpl = weighted[h : h + 64, cols].astype(jnp.float32)
                noise = noise_ref[:, cols]
                scaled = tpl * noise
                square = tpl * tpl * noise
                total = square[:, :LANES]
                for j in range(1, NORM_COLS // LANES):
                    total = total + square[:, j * LANES : (j + 1) * LANES]
                norms[h : h + 64, :] += total
                weighted[h : h + 64, cols] = scaled.astype(jnp.bfloat16)

    def score(r, s):
        for q in range(across):
            arrived(r, q, 1 - core, s)
        cols = pl.ds(pl.multiple_of(s * part, part), part)
        slots = pl.ds(pl.multiple_of(r * (2 * across), 2 * across), 2 * across)
        block = raw[slots, :, cols].reshape(2 * across * block_rows, part)
        total = 2 * across * block_rows
        out_row = lax.broadcasted_iota(jnp.int32, (total, total), 0)
        from_row = lax.broadcasted_iota(jnp.int32, (total, total), 1)
        image, piece = out_row % line_images, out_row // line_images
        wanted = (image // own_rows) * block_rows + piece * own_rows + image % own_rows
        pick = jnp.where(from_row == wanted, 1.0, 0.0).astype(jnp.bfloat16)
        sorted_ = jnp.dot(pick, block, preferred_element_type=jnp.float32)
        sorted_ = sorted_.astype(jnp.bfloat16)
        rows = pl.ds(pl.multiple_of(r * line_images, line_images), line_images)
        added = scores[rows, :]
        for k in range(fold):
            piece = sorted_[k * line_images : (k + 1) * line_images, :]
            span = pl.ds(pl.multiple_of(k * width + s * part, part), part)
            whole[rows, span] = piece
            added = added + lax.dot_general(
                piece,
                weighted[:, span],
                (((1,), (1,)), ((), ())),
                preferred_element_type=jnp.float32,
            )
        scores[rows, :] = added

    def store_copy(r):
        rows = pl.ds(pl.multiple_of(r * line_images, line_images), line_images)
        return pltpu.make_async_copy(whole.at[rows], gathered_ref.at[rows], store_sem.at[r])

    def score_store(r, s):
        score(r, s)

        @pl.when(s == PARTS - 1)
        def _():
            store_copy(r).start()

    @pl.loop(0, lines * PARTS + 1)
    def _(k):
        n, s = lax.div(k, PARTS) + 1, lax.rem(k, PARTS)
        for sign in (1, -1):
            r = row + sign * n

            @pl.when((r >= 0) & (r < lines) & (n < lines))
            def _(r=r):
                arrived(r, col, core, s)
                each_send(r, col, s, lambda c: c.start())

        for sign in (1, -1):
            r = row + sign * (n - 1)
            live = (r >= 0) & (r < lines) & (n <= lines)
            if sign < 0:
                live = live & (n > 1)
            for e in range(1, across):
                for side in (1, -1):
                    q = col + side * e

                    @pl.when(live & (q >= 0) & (q < across))
                    def _(r=r, q=q):
                        arrived(r, q, core, s)
                        each_send(r, q, s, lambda c: c.start())

        @pl.when(n == 1)
        def _():
            @pl.loop(0, fold // PARTS)
            def _(j):
                weigh(s * (fold // PARTS) + j)

        hop, early = lax.div(k, WORD_STEPS), lax.rem(k, WORD_STEPS)
        for sign in (1, -1):
            r = row + sign * hop

            @pl.when(bearer & (early == 0) & (hop > 0) & (hop < lines) & (r >= 0) & (r < lines))
            def _(r=r):
                word_arrived(r)
                each_word(r, lambda c: c.start())

        last = jnp.maximum(k - 1, 0)
        m, t = lax.div(last, PARTS) + 1, lax.rem(last, PARTS)

        @pl.when((m == 2) & (k > 0))
        def _():
            score_store(row, t)

        for sign in (1, -1):
            r = row + sign * (m - 1)

            @pl.when((m > 1) & (r >= 0) & (r < lines))
            def _(r=r):
                score_store(r, t)

    norm = 0.5 * jnp.sum(norms[...].T, axis=0, keepdims=True)
    value = (scores[...] - norm).T
    peak_own = jnp.max(value, axis=0, keepdims=True)
    expo = jnp.exp(value - peak_own)
    stats[...] = jnp.zeros_like(stats)
    stats[0:1, :] = peak_own
    stats[1:2, :] = jnp.sum(expo, axis=0, keepdims=True)

    def stat_copy(s):
        return pltpu.make_async_remote_copy(
            src_ref=stats,
            dst_ref=landed.at[s],
            send_sem=stat_send.at[s],
            recv_sem=stat_recv.at[s],
            device_id=(group, lax.rem(place + s, orient)),
            device_id_type=mesh_ids,
        )

    @pl.loop(1, orient)
    def _(s):
        stat_copy(s).start()

    landed[0] = stats[...]

    @pl.when(bearer)
    def _():
        words_in[row] = words[...]

    @pl.loop(1, orient)
    def _(s):
        stat_copy(s).wait()

    peak = peak_own
    for s in range(1, orient):
        peak = jnp.maximum(peak, landed[s, 0:1, :])
    total = jnp.zeros_like(peak)
    for s in range(orient):
        total = total + landed[s, 1:2, :] * jnp.exp(landed[s, 0:1, :] - peak)
    posterior = (expo * (jnp.exp(peak_own - peak) / total))[:, :images]
    post_ref[...] = posterior.astype(jnp.bfloat16)
    mass = jnp.sum(posterior, axis=1, keepdims=True)
    mass_t = jnp.broadcast_to(mass, (count, LANES)).T
    for h in range(count // LANES):
        mass_ref[h : h + 1, :] = mass_t[:1, h * LANES : (h + 1) * LANES]

    @pl.when(jnp.logical_not(bearer))
    def _():
        for r in range(lines):
            word_arrived(r)

    places_ref[...] = words_in[...]

    @pl.when(bearer)
    def _():
        each_word(row, lambda c: c.wait_send(), None)
        for r in range(lines):

            @pl.when(row != r)
            def _(r=r):
                each_word(r, lambda c: c.wait_send())

    for r in range(lines):
        store_copy(r).wait()

    @pl.loop(0, PARTS)
    def _(s):
        each_send(row, col, s, lambda c: c.wait_send(), None)
        for r in range(lines):
            for q in range(across):

                @pl.when((row != r) | (col != q))
                def _(r=r, q=q):
                    each_send(r, q, s, lambda c: c.wait_send())


def gather_scores(images, templates, index, interp, noise_flat, orient):
    own, pixels = images.shape
    count, side = index.shape
    fold = PARTS
    while own * fold % 16:
        fold += PARTS
    width = pixels // fold
    total = own * orient
    padded = -(-total // LANES) * LANES
    vmem = pl.BlockSpec(memory_space=pltpu.VMEM)
    hbm = pl.BlockSpec(memory_space=pl.ANY)
    chips = orient // 2
    return pl.pallas_call(
        functools.partial(gather_kernel, orient),
        out_shape=(
            jax.ShapeDtypeStruct((total, pixels), jnp.bfloat16),
            jax.ShapeDtypeStruct((count, total), jnp.bfloat16),
            jax.ShapeDtypeStruct((count // LANES, LANES), jnp.float32),
            jax.ShapeDtypeStruct((LINES, side, count), jnp.int32),
            jax.ShapeDtypeStruct((side * count // BATCH, BATCH), jnp.int32),
            jax.ShapeDtypeStruct((8, side), jnp.int32),
        ),
        in_specs=[vmem, hbm, vmem, vmem, vmem],
        out_specs=(hbm, vmem, vmem, vmem, vmem, vmem),
        scratch_shapes=[
            pltpu.VMEM((own * fold, width), jnp.bfloat16),
            pltpu.VMEM((own * fold, width), jnp.float32),
            pltpu.VMEM((side, count), jnp.int32),
            pltpu.VMEM((LINES, side, count), jnp.int32),
            pltpu.VMEM((orient, own * fold, width), jnp.bfloat16),
            pltpu.VMEM((count, pixels), jnp.bfloat16),
            pltpu.VMEM((total, pixels), jnp.bfloat16),
            pltpu.VMEM((padded, count), jnp.float32),
            pltpu.VMEM((count, LANES), jnp.float32),
            pltpu.VMEM((8, padded), jnp.float32),
            pltpu.VMEM((orient, 8, padded), jnp.float32),
            pltpu.SemaphoreType.DMA((fold,)),
            pltpu.SemaphoreType.DMA((LINES,)),
            pltpu.SemaphoreType.DMA((chips, PARTS, 5)),
            pltpu.SemaphoreType.DMA((orient, PARTS)),
            pltpu.SemaphoreType.DMA((orient,)),
            pltpu.SemaphoreType.DMA((orient,)),
            pltpu.SemaphoreType.DMA((LINES, 3)),
            pltpu.SemaphoreType.DMA((LINES,)),
        ],
        compiler_params=pltpu.CompilerParams(
            collective_id=1, has_side_effects=True, vmem_limit_bytes=VMEM_LIMIT
        ),
    )(images, templates, noise_flat, index, interp)


def finish_kernel(data_ref, weight_ref, data_out, weight_out):
    data_out[...] = data_ref[...]
    weight_out[...] = weight_ref[...]


def finish(data, weight):
    shape = jax.ShapeDtypeStruct(data.shape, data.dtype)
    return pl.pallas_call(finish_kernel, out_shape=(shape, shape))(data, weight)


def shards(groups, orient, images, templates, index, interp, inv_noise):
    side = inv_noise.shape[0]
    gathered, post, mass, places, voxels, clash = gather_scores(
        images, templates, index, interp, inv_noise.reshape(1, -1), orient
    )
    volume = insert_data(post, gathered, interp, voxels, clash, side * side)
    return finish(*reduce_rows(volume, mass, places, inv_noise, groups, orient))


def solution(mesh):
    placed = (
        P(("dp", "orient"), None),
        P("orient", None),
        P("orient", None),
        P("orient", None),
        P(),
    )
    return jax.shard_map(
        functools.partial(shards, mesh.shape["dp"], mesh.shape["orient"]),
        mesh=mesh,
        in_specs=placed,
        out_specs=(P(("dp", "orient"), None), P(("dp", "orient"), None)),
        check_vma=False,
    )
```

```python
import functools

import jax
import jax.numpy as jnp
from jax import lax
from jax.experimental import pallas as pl
from jax.experimental.pallas import tpu as pltpu
from jax.sharding import PartitionSpec as P

LANES = 128
ROWS_STEP = 8
ACCS = 4
SUB = 4
BATCH = 128
SLOT = 512
COLS = 2
CHUNKS = 16
WORD_STEPS = 3
LINES = 4
PARTS = 4
NORM_COLS = 1024
LEVELS = 65535
SHIFT = 65536
LOW_BITS = 6
LOW = 1 << LOW_BITS
VMEM_LIMIT = 56 * 2**20


def data_kernel(
    post_hbm,
    images_hbm,
    interp_hbm,
    idx_ref,
    clash_ref,
    out_ref,
    rows_ref,
    post_ref,
    images_two,
    interp_ref,
    idx,
    idx_sem,
    image_sem,
    once_sem,
    out_sem,
    *accs,
):
    step, steps = pl.program_id(0), pl.num_programs(0)
    count, side = post_ref.shape[0], out_ref.shape[1]
    volume_rows = out_ref.shape[0]
    wide = ROWS_STEP * side
    halves = count // BATCH
    slots = ROWS_STEP * count // SLOT
    each = SLOT // BATCH

    def fetch(at, u):
        return pltpu.make_async_copy(
            idx_ref.at[pl.ds((at * slots + u) * each, each)], idx.at[u], idx_sem.at[u]
        )

    def load(at):
        cols = pl.ds(pl.multiple_of(at * wide, wide), wide)
        two = lax.rem(at, 2)
        return pltpu.make_async_copy(
            images_hbm.at[:, cols], images_two.at[two], image_sem.at[two]
        )

    post_copy = pltpu.make_async_copy(post_hbm, post_ref, once_sem.at[0])
    interp_copy = pltpu.make_async_copy(interp_hbm, interp_ref, once_sem.at[1])

    @pl.when(step == 0)
    def _():
        post_copy.start()
        interp_copy.start()
        load(step).start()
        for u in range(slots):
            fetch(step, u).start()

        @pl.loop(0, volume_rows // 64)
        def _(c):
            rows = pl.ds(pl.multiple_of(c * 64, 64), 64)
            for acc in accs:
                acc[rows, :] = jnp.zeros((64, side), jnp.float32)

        post_copy.wait()
        interp_copy.wait()

    load(step).wait()

    @pl.when(step < steps - 1)
    def _():
        load(step + 1).start()

    images_ref = images_two.at[lax.rem(step, 2)]
    interp = pltpu.roll(interp_ref[...], lax.rem(side - step * ROWS_STEP, side), axis=1)
    for j in range(0, ROWS_STEP, COLS):
        block = jnp.dot(
            post_ref[...],
            images_ref[:, j * side : (j + COLS) * side],
            preferred_element_type=jnp.float32,
        )
        for i in range(COLS):
            rows_ref[(j + i) * count : (j + i + 1) * count, :] = (
                block[:, i * side : (i + 1) * side] * interp[:, j + i : j + i + 1]
            )

    for u in range(slots):
        fetch(step, u).wait()
        for b in range(each):
            base = (u * each + b) * BATCH
            clash = clash_ref[b % halves, step * ROWS_STEP + base // count]

            @pl.when(clash == 0)
            def _(u=u, b=b, base=base):
                pending = [()] * ACCS

                def flush(a):
                    for voxel, value in pending[a]:
                        accs[a][pl.ds(voxel, 1), :] = value

                for n in range(BATCH // SUB):
                    a = n % ACCS
                    flush(a)
                    pending[a] = []
                    for k in range(n * SUB, (n + 1) * SUB):
                        voxel = idx[u, b, k]
                        value = accs[a][pl.ds(voxel, 1), :] + rows_ref[base + k : base + k + 1, :]
                        pending[a].append((voxel, value))
                for a in range(ACCS):
                    flush(a)

            @pl.when(clash != 0)
            def _(u=u, b=b, base=base):
                @pl.loop(0, BATCH // ACCS)
                def _(q):
                    first = q * ACCS
                    targets = [idx[u, b, first + a] for a in range(ACCS)]
                    summed = [
                        accs[a][pl.ds(targets[a], 1), :]
                        + rows_ref[pl.ds(base + first + a, 1), :]
                        for a in range(ACCS)
                    ]
                    for a in range(ACCS):
                        accs[a][pl.ds(targets[a], 1), :] = summed[a]

        @pl.when(step < steps - 1)
        def _(u=u):
            fetch(step + 1, u).start()

    @pl.when(step == steps - 1)
    def _():
        chunk = volume_rows // CHUNKS

        def write(p):
            rows = pl.ds(pl.multiple_of(p * chunk, chunk), chunk)
            return pltpu.make_async_copy(accs[0].at[rows], out_ref.at[rows], out_sem.at[p])

        @pl.loop(0, CHUNKS)
        def _(p):
            @pl.loop(0, chunk // 64)
            def _(c):
                rows = pl.ds(pl.multiple_of(p * chunk + c * 64, 64), 64)
                total = accs[0][rows, :]
                for acc in accs[1:]:
                    total = total + acc[rows, :]
                accs[0][rows, :] = total

            write(p).start()

        @pl.loop(0, CHUNKS)
        def _(p):
            write(p).wait()


def insert_data(post, gathered, interp, voxels, clash, volume_rows):
    count, images = post.shape
    side = interp.shape[1]
    slots = ROWS_STEP * count // SLOT
    return pl.pallas_call(
        data_kernel,
        grid=(side // ROWS_STEP,),
        out_shape=jax.ShapeDtypeStruct((volume_rows, side), jnp.float32),
        in_specs=[
            pl.BlockSpec(memory_space=pl.ANY),
            pl.BlockSpec(memory_space=pl.ANY),
            pl.BlockSpec(memory_space=pl.ANY),
            pl.BlockSpec(memory_space=pl.ANY),
            pl.BlockSpec(memory_space=pltpu.SMEM),
        ],
        out_specs=pl.BlockSpec(memory_space=pl.ANY),
        scratch_shapes=[
            pltpu.VMEM((ROWS_STEP * count, side), jnp.float32),
            pltpu.VMEM((count, images), jnp.bfloat16),
            pltpu.VMEM((2, images, ROWS_STEP * side), jnp.bfloat16),
            pltpu.VMEM((count, side), jnp.float32),
            pltpu.SMEM((slots, SLOT // BATCH, BATCH), jnp.int32),
            pltpu.SemaphoreType.DMA((slots,)),
            pltpu.SemaphoreType.DMA((2,)),
            pltpu.SemaphoreType.DMA((2,)),
            pltpu.SemaphoreType.DMA((CHUNKS,)),
        ]
        + [pltpu.VMEM((volume_rows, side), jnp.float32)] * ACCS,
        compiler_params=pltpu.CompilerParams(vmem_limit_bytes=VMEM_LIMIT),
        cost_estimate=pl.CostEstimate(
            flops=200_000_000_000, bytes_accessed=200_000_000, transcendentals=0
        ),
    )(post, gathered, interp, voxels, clash)


def reduce_kernel(
    groups,
    orient,
    blocks_ref,
    mass_ref,
    places_ref,
    noise_ref,
    out_ref,
    weight_ref,
    grid_ref,
    mass_row,
    mine,
    theirs,
    first_x,
    first_x_in,
    first_y,
    first_y_in,
    second_x,
    second_x_in,
    second_y,
    second_y_in,
    last,
    last_in,
    masses,
    twin,
    twin_in,
    own_sem,
    pair_send,
    pair_recv,
    fx_send,
    fx_recv,
    fy_send,
    fy_recv,
    sx_send,
    sx_recv,
    sy_send,
    sy_recv,
    last_send,
    last_recv,
    mass_send,
    mass_recv,
    twin_send,
    twin_recv,
):
    lines, across = LINES, orient // (2 * LINES)
    devices = groups * orient
    group, place = lax.axis_index("dp"), lax.axis_index("orient")
    core, chip = lax.rem(place, 2), lax.div(place, 2)
    row, col = lax.div(chip, across), lax.rem(chip, across)
    rank = group * orient + place
    half = out_ref.shape[0] // 2
    mesh_ids = pl.DeviceIdType.MESH

    def ranked(d):
        return (lax.div(d, orient), lax.rem(d, orient))

    def line(k):
        return lax.rem(row + k + 1, lines)

    def group_at(i):
        return lax.rem(group + i, groups)

    def col_at(j):
        return lax.rem(col + j, across)

    def block(x, r, q):
        return (x * lines + r) * across + q

    def remote(source, target, send, recv, x, r, q, c):
        return pltpu.make_async_remote_copy(
            src_ref=source,
            dst_ref=target,
            send_sem=send,
            recv_sem=recv,
            device_id=(x, (r * across + q) * 2 + c),
            device_id_type=mesh_ids,
        )

    barrier = pltpu.get_barrier_semaphore()

    @pl.loop(1, devices)
    def _(s):
        pl.semaphore_signal(
            barrier,
            inc=1,
            device_id=ranked(lax.rem(rank + s, devices)),
            device_id_type=mesh_ids,
        )

    def own_copy(k, i, j):
        p = block(group_at(i), line(k), col_at(j))
        return pltpu.make_async_copy(
            blocks_ref.at[p, core], mine.at[p], own_sem.at[k, i * across + j]
        )

    for i in reversed(range(groups)):
        for j in reversed(range(across)):

            @pl.loop(0, lines)
            def _(k, i=i, j=j):
                own_copy(k, i, j).start()

    pl.semaphore_wait(barrier, devices - 1)

    def mass_copy(s):
        return pltpu.make_async_remote_copy(
            src_ref=mass_ref,
            dst_ref=masses.at[s],
            send_sem=mass_send.at[s],
            recv_sem=mass_recv.at[s],
            device_id=ranked(lax.rem(rank + s, devices)),
            device_id_type=mesh_ids,
        )

    def pair_copy(k, i, j):
        p, n = block(group_at(i), line(k), col_at(j)), i * across + j
        return remote(
            blocks_ref.at[p, 1 - core],
            theirs.at[p],
            pair_send.at[k, n],
            pair_recv.at[k, n],
            group,
            row,
            col,
            1 - core,
        )

    def first_x_copy(k, i):
        return remote(
            first_x.at[i - 1, k],
            first_x_in.at[i - 1, k],
            fx_send.at[i - 1, k],
            fx_recv.at[i - 1, k],
            group_at(i),
            row,
            col,
            core,
        )

    def first_y_copy(k, j):
        return remote(
            first_y.at[j - 1, k],
            first_y_in.at[j - 1, k],
            fy_send.at[j - 1, k],
            fy_recv.at[j - 1, k],
            group,
            row,
            col_at(j),
            core,
        )

    def second_x_copy(k, i):
        return remote(
            second_x.at[i - 1, k],
            second_x_in.at[i - 1, k],
            sx_send.at[i - 1, k],
            sx_recv.at[i - 1, k],
            group_at(i),
            row,
            col,
            core,
        )

    def second_y_copy(k, j):
        return remote(
            second_y.at[j - 1, k],
            second_y_in.at[j - 1, k],
            sy_send.at[j - 1, k],
            sy_recv.at[j - 1, k],
            group,
            row,
            col_at(j),
            core,
        )

    def last_copy(k):
        return remote(
            last.at[k],
            last_in.at[k],
            last_send.at[k],
            last_recv.at[k],
            group,
            line(k),
            col,
            core,
        )

    @pl.loop(0, lines)
    def _(k):
        for i in reversed(range(groups)):
            for j in reversed(range(across)):
                pair_copy(k, i, j).start()

    twin_group = group + 1 - 2 * lax.rem(group, 2)

    def column(d):
        return lax.rem(lax.div(lax.rem(d, orient), 2), across)

    def mass_sent(s):
        target = lax.rem(rank + s, devices)
        return (lax.rem(lax.div(target, orient), 2) == core) & (column(target) == col)

    @pl.loop(1, devices)
    def _(s):
        @pl.when(mass_sent(s))
        def _():
            mass_copy(s).start()

    def narrow(value):
        return value.astype(jnp.bfloat16)

    def begin(k):
        for i in reversed(range(groups)):
            for j in reversed(range(across)):
                x, q = group_at(i), col_at(j)
                p = block(x, line(k), q)
                own_copy(k, i, j).wait()
                pair_copy(k, i, j).wait()
                if i == 0 or j == 0:
                    total = mine[p] + theirs[p]
                    mine[p] = total
                    if i:
                        first_x[i - 1, k, q] = narrow(total[:half])
                    if j:
                        first_y[j - 1, k, x] = narrow(total[half:])
                else:
                    first_x[i - 1, k, q] = narrow(mine[p, :half] + theirs[p, :half])
                    first_y[j - 1, k, x] = narrow(mine[p, half:] + theirs[p, half:])
            if i:
                first_x_copy(k, i).start()
        for j in range(1, across):
            first_y_copy(k, j).start()

    def middle(k):
        for i in range(1, groups):
            first_x_copy(k, i).wait()
        for j in reversed(range(across)):
            q = col_at(j)
            p = block(group, line(k), q)
            total = mine[p, :half]
            for i in range(1, groups):
                total = total + first_x_in[i - 1, k, q].astype(jnp.float32)
            if j:
                second_y[j - 1, k] = narrow(total)
                second_y_copy(k, j).start()
            else:
                mine[p, :half] = total
        for j in range(1, across):
            first_y_copy(k, j).wait()
        for i in reversed(range(groups)):
            x = group_at(i)
            p = block(x, line(k), col)
            total = mine[p, half:]
            for j in range(1, across):
                total = total + first_y_in[j - 1, k, x].astype(jnp.float32)
            if i:
                second_x[i - 1, k] = narrow(total)
                second_x_copy(k, i).start()
            else:
                mine[p, half:] = total

    def end(k):
        p = block(group, line(k), col)
        for j in range(1, across):
            second_y_copy(k, j).wait()
        top = mine[p, :half]
        for j in range(1, across):
            top = top + second_y_in[j - 1, k].astype(jnp.float32)
        for i in range(1, groups):
            second_x_copy(k, i).wait()
        low = mine[p, half:]
        for i in range(1, groups):
            low = low + second_x_in[i - 1, k].astype(jnp.float32)

        @pl.when(k < lines - 1)
        def _():
            last[k, :half] = narrow(top)
            last[k, half:] = narrow(low)
            last_copy(k).start()

        @pl.when(k == lines - 1)
        def _():
            out_ref[:half] = top
            out_ref[half:] = low

    mass_row[...] = jnp.zeros_like(mass_row)
    mass_rows = mass_ref.shape[0]

    def add_mass(d, ref):
        start = lax.div(lax.rem(d, orient), 2 * across) * (mass_rows * LANES)
        for k in range(mass_rows):
            lanes = pl.ds(pl.multiple_of(start + k * LANES, LANES), LANES)
            mass_row[:, lanes] += ref[k : k + 1, :]

    steps, slots = noise_ref.shape[0] // ROWS_STEP, 3 * (lines + 2)

    def weigh(w):
        rows = out_ref.shape[0]
        firsts = [
            (x * orient + (row * across + col_at(j)) * 2 + core) * rows
            for x in (group, twin_group)
            for j in range(across)
        ]
        weight_step(w, firsts, places_ref, mass_row, grid_ref)

    def twin_copy(n):
        return remote(
            twin.at[n - 1],
            twin_in.at[n - 1],
            twin_send.at[n - 1],
            twin_recv.at[n - 1],
            (group, twin_group)[n // across],
            row,
            col_at(n % across),
            core,
        )

    @pl.loop(0, slots)
    def _(slot):
        k, turn = lax.div(slot, 3), lax.rem(slot, 3)

        @pl.when((turn == 0) & (k < lines))
        def _():
            begin(k)

        @pl.when((turn == 1) & (k >= 1) & (k < lines + 1))
        def _():
            middle(k - 1)

        @pl.when((turn == 2) & (k >= 2))
        def _():
            end(k - 2)

        @pl.when(slot == 1)
        def _():
            @pl.when(core == lax.rem(group, 2))
            def _():
                add_mass(rank, mass_ref)

            @pl.loop(1, devices)
            def _(s):
                sender = lax.rem(rank + devices - s, devices)

                @pl.when((lax.rem(sender, 2) == lax.rem(group, 2)) & (column(sender) == col))
                def _():
                    mass_copy(s).wait_recv()
                    add_mass(sender, masses.at[s])

                @pl.when(mass_sent(s))
                def _():
                    mass_copy(s).wait_send()

        @pl.when((slot >= 2) & (slot < 2 + steps // 2))
        def _():
            weigh(2 * slot - 4)
            weigh(2 * slot - 3)

        @pl.when(slot == 2 + steps // 2)
        def _():
            for n in range(1, 2 * across):
                weight_rows(noise_ref, twin.at[n - 1], grid_ref, n, 2 * across)
                twin_copy(n).start()

    weight_rows(noise_ref, weight_ref, grid_ref, 0, 2 * across)
    for n in range(1, 2 * across):
        twin_copy(n).wait()
        weight_ref[...] += twin_in[n - 1].astype(jnp.float32)
    for k in range(lines - 1):
        last_copy(k).wait()
        out_ref[...] += last_in[k].astype(jnp.float32)


def reduce_rows(volume, mass_rows, places_t, inv_noise, groups, orient):
    chips = groups * orient // 2
    lines, across = LINES, orient // (2 * LINES)
    rows, side = volume.shape[0] // (2 * chips), volume.shape[1]
    half = rows // 2
    parts = (chips, rows, side)
    masses = (2 * chips,) + mass_rows.shape
    shapes = [
        (groups - 1, lines, across, half, side),
        (across - 1, lines, groups, half, side),
        (groups - 1, lines, half, side),
        (across - 1, lines, half, side),
        (lines - 1, rows, side),
    ]
    sems = [
        (groups - 1, lines),
        (across - 1, lines),
        (groups - 1, lines),
        (across - 1, lines),
        (lines - 1,),
        (2 * chips,),
    ]
    return pl.pallas_call(
        functools.partial(reduce_kernel, groups, orient),
        out_shape=(
            jax.ShapeDtypeStruct((rows, side), jnp.float32),
            jax.ShapeDtypeStruct((rows, side), jnp.float32),
        ),
        in_specs=[pl.BlockSpec(memory_space=pl.ANY)]
        + [pl.BlockSpec(memory_space=pltpu.VMEM)] * 3,
        out_specs=(
            pl.BlockSpec(memory_space=pltpu.VMEM),
            pl.BlockSpec(memory_space=pltpu.VMEM),
        ),
        scratch_shapes=[
            pltpu.VMEM((2 * across * side * max(8, rows // LOW), LANES), jnp.float32),
            pltpu.VMEM((1, places_t.shape[0] * places_t.shape[2]), jnp.float32),
        ]
        + [pltpu.VMEM(parts, jnp.float32)] * 2
        + [pltpu.VMEM(s, jnp.bfloat16) for s in shapes for _ in range(2)]
        + [pltpu.VMEM(masses, jnp.float32)]
        + [pltpu.VMEM((2 * across - 1, rows, side), jnp.bfloat16)] * 2
        + [pltpu.SemaphoreType.DMA((lines, groups * across))] * 3
        + [pltpu.SemaphoreType.DMA(s) for s in sems for _ in range(2)]
        + [pltpu.SemaphoreType.DMA((2 * across - 1,))] * 2,
        compiler_params=pltpu.CompilerParams(
            collective_id=0, has_side_effects=True, vmem_limit_bytes=VMEM_LIMIT
        ),
    )(volume.reshape(chips, 2, rows, side), mass_rows, places_t, inv_noise)


def weight_step(step, firsts, places_ref, mass_row, grid_ref):
    blocks, side, each = places_ref.shape
    count = blocks * each
    high_rows = grid_ref.shape[0] // side
    nt = (((1,), (1,)), ((), ()))
    one, zero = jnp.float32(1), jnp.float32(0)
    spot = lax.broadcasted_iota(jnp.int32, (high_rows, count), 0)
    each_high = high_rows // len(firsts)
    iota_high = spot
    for n, first in enumerate(firsts):
        shift = lax.div(first, LOW) - n * each_high
        iota_high = jnp.where(spot // each_high == n, spot + shift, iota_high)
    iota_low = lax.broadcasted_iota(jnp.int32, (LOW, count), 0)
    block = pl.ds(pl.multiple_of(step * ROWS_STEP, ROWS_STEP), ROWS_STEP)
    words = jnp.concatenate([places_ref[d, block, :] for d in range(blocks)], axis=1)
    voxels = words >> 16
    weights = (words & (SHIFT - 1)).astype(jnp.float32) * (1 / LEVELS) * mass_row[...]
    for j in range(ROWS_STEP):
        local = voxels[j : j + 1, :]
        hot = jnp.where(iota_high == (local >> LOW_BITS), one, zero)
        low = jnp.where(iota_low == (local & (LOW - 1)), weights[j : j + 1, :], zero)
        part = lax.dot_general(
            hot.astype(jnp.bfloat16),
            low.astype(jnp.bfloat16),
            nt,
            preferred_element_type=jnp.float32,
        )
        row = pl.multiple_of((step * ROWS_STEP + j) * high_rows, 8)
        grid_ref[pl.ds(row, high_rows), :LOW] = part


def weight_rows(noise_ref, out_ref, grid_ref, part, ranges):
    side = noise_ref.shape[0]
    high_rows = grid_ref.shape[0] // side
    noise = noise_ref[...].astype(jnp.bfloat16)
    for h in range(out_ref.shape[0] // LOW):
        first = part * (high_rows // ranges) + h
        block = lax.dot_general(
            grid_ref[pl.ds(first, side, stride=high_rows), :].astype(jnp.bfloat16),
            noise,
            (((0,), (0,)), ((), ())),
            preferred_element_type=jnp.float32,
        )
        out_ref[h * LOW : (h + 1) * LOW, :] = block[:LOW].astype(out_ref.dtype)


def gather_kernel(
    orient,
    own_ref,
    templates_ref,
    noise_ref,
    index_ref,
    interp_ref,
    gathered_ref,
    post_ref,
    mass_ref,
    places_ref,
    rows_ref,
    clash_ref,
    images_ref,
    wide,
    words,
    words_in,
    raw,
    weighted,
    whole,
    scores,
    norms,
    stats,
    landed,
    load_sem,
    store_sem,
    send_sem,
    recv_sem,
    stat_send,
    stat_recv,
    word_send,
    word_recv,
):
    lines, across = LINES, orient // (2 * LINES)
    group, place = lax.axis_index("dp"), lax.axis_index("orient")
    core = lax.rem(place, 2)
    chip = lax.div(place, 2)
    row, col = lax.div(chip, across), lax.rem(chip, across)
    mesh_ids = pl.DeviceIdType.MESH
    block_rows, width = images_ref.shape
    part = width // PARTS
    count = templates_ref.shape[0]
    fold = templates_ref.shape[1] // width
    line_images = 2 * across * block_rows // fold
    images = line_images * lines

    def at(r, q, c):
        return (r * across + q) * 2 + c

    barrier = pltpu.get_barrier_semaphore()

    @pl.loop(1, orient)
    def _(s):
        pl.semaphore_signal(
            barrier,
            inc=1,
            device_id=(group, lax.rem(place + s, orient)),
            device_id_type=mesh_ids,
        )

    def load_copy(k):
        cols = pl.ds(pl.multiple_of(k * width, width), width)
        return pltpu.make_async_copy(
            templates_ref.at[:, cols], weighted.at[:, cols], load_sem.at[k]
        )

    for k in range(fold):
        load_copy(k).start()

    own_rows = own_ref.shape[0]
    for k in range(fold):
        wide[k * own_rows : (k + 1) * own_rows, :] = own_ref[
            :, k * width : (k + 1) * width
        ].astype(jnp.float32)
    images_ref[...] = wide[...].astype(jnp.bfloat16)
    index = index_ref[...]
    near = jnp.zeros(index.shape, jnp.int32)
    spot = lax.broadcasted_iota(jnp.int32, index.shape, 0) % SUB
    for d in range(1, SUB):
        same = (index == pltpu.roll(index, d, axis=0)) & (spot >= d)
        near = near | same.astype(jnp.int32)
    clash_ref[...] = jnp.zeros_like(clash_ref)
    for h in range(count // BATCH):
        clash_ref[h : h + 1, :] = jnp.max(
            near[h * BATCH : (h + 1) * BATCH, :], axis=0, keepdims=True
        )
    index_t = index.T
    for h in range(count // BATCH):
        rows_ref[pl.ds(h, index_t.shape[0], stride=count // BATCH), :] = index_t[
            :, h * BATCH : (h + 1) * BATCH
        ]
    level = (interp_ref[...] * LEVELS + 0.5).astype(jnp.int32)
    words[...] = (index * SHIFT + level).T
    pl.semaphore_wait(barrier, orient - 1)

    bearer = lax.rem(group, 2) == core

    def word_copy(source, r, way, target):
        return pltpu.make_async_remote_copy(
            src_ref=words if source is None else words_in.at[r],
            dst_ref=words_in.at[r],
            send_sem=word_send.at[r, way],
            recv_sem=word_recv.at[r],
            device_id=(group, target),
            device_id_type=mesh_ids,
        )

    def word_arrived(r):
        word_copy(words_in, r, 2, place + 1 - 2 * core).wait_recv()

    def each_word(r, act, source=words_in):
        for way, step in ((0, 1), (1, -1)):
            onward = row + step
            along = (onward >= 0) & (onward < lines)
            if source is not None:
                along = along & ((row - r) * step > 0)

            @pl.when(along)
            def _(way=way, onward=onward):
                act(word_copy(source, r, way, at(onward, col, core)))

        act(word_copy(source, r, 2, place + 1 - 2 * core))

    @pl.when(bearer)
    def _():
        each_word(row, lambda c: c.start(), None)

    def copy(source, r, q, s, way, target):
        cols = pl.ds(pl.multiple_of(s * part, part), part)
        slot = at(r, q, core)
        ref = images_ref if source is None else raw.at[slot]
        return pltpu.make_async_remote_copy(
            src_ref=ref.at[:, cols],
            dst_ref=raw.at[slot, :, cols],
            send_sem=send_sem.at[lax.div(slot, 2), s, way],
            recv_sem=recv_sem.at[slot, s],
            device_id=(group, target),
            device_id_type=mesh_ids,
        )

    def arrived(r, q, c, s):
        cols = pl.ds(pl.multiple_of(s * part, part), part)
        slot = at(r, q, c)
        pltpu.make_async_remote_copy(
            src_ref=raw.at[slot, :, cols],
            dst_ref=raw.at[slot, :, cols],
            send_sem=send_sem.at[0, 0, 0],
            recv_sem=recv_sem.at[slot, s],
            device_id=(group, place + 1 - 2 * core),
            device_id_type=mesh_ids,
        ).wait_recv()

    def each_send(r, q, s, act, source=raw):
        for way, step in ((0, 1), (1, -1)):
            onward = row + step
            if source is None:
                along = (onward >= 0) & (onward < lines)
            else:
                along = (q == col) & (onward >= 0) & (onward < lines) & ((row - r) * step > 0)

            @pl.when(along)
            def _(way=way, onward=onward):
                act(copy(source, r, q, s, way, at(onward, col, core)))

        for way, step in ((2, 1), (3, -1)):
            onward = col + step
            beside = (onward >= 0) & (onward < across) & ((col - q) * step >= 0)

            @pl.when(beside)
            def _(way=way, onward=onward):
                act(copy(source, r, q, s, way, at(row, onward, core)))

        act(copy(source, r, q, s, 4, place + 1 - 2 * core))

    @pl.loop(0, PARTS)
    def _(s):
        each_send(row, col, s, lambda c: c.start(), None)

    raw[place] = images_ref[...]
    scores[...] = jnp.zeros_like(scores)
    norms[...] = jnp.zeros_like(norms)

    def weigh(k):
        load_copy(k).wait()

        @pl.loop(0, width // NORM_COLS)
        def _(g):
            cols = pl.ds(pl.multiple_of(k * width + g * NORM_COLS, NORM_COLS), NORM_COLS)
            for h in range(0, count, 64):
                tpl = weighted[h : h + 64, cols].astype(jnp.float32)
                noise = noise_ref[:, cols]
                scaled = tpl * noise
                square = tpl * tpl * noise
                total = square[:, :LANES]
                for j in range(1, NORM_COLS // LANES):
                    total = total + square[:, j * LANES : (j + 1) * LANES]
                norms[h : h + 64, :] += total
                weighted[h : h + 64, cols] = scaled.astype(jnp.bfloat16)

    def score(r, s):
        for q in range(across):
            arrived(r, q, 1 - core, s)
        cols = pl.ds(pl.multiple_of(s * part, part), part)
        slots = pl.ds(pl.multiple_of(r * (2 * across), 2 * across), 2 * across)
        block = raw[slots, :, cols].reshape(2 * across * block_rows, part)
        total = 2 * across * block_rows
        out_row = lax.broadcasted_iota(jnp.int32, (total, total), 0)
        from_row = lax.broadcasted_iota(jnp.int32, (total, total), 1)
        image, piece = out_row % line_images, out_row // line_images
        wanted = (image // own_rows) * block_rows + piece * own_rows + image % own_rows
        pick = jnp.where(from_row == wanted, 1.0, 0.0).astype(jnp.bfloat16)
        sorted_ = jnp.dot(pick, block, preferred_element_type=jnp.float32)
        sorted_ = sorted_.astype(jnp.bfloat16)
        rows = pl.ds(pl.multiple_of(r * line_images, line_images), line_images)
        added = scores[rows, :]
        for k in range(fold):
            piece = sorted_[k * line_images : (k + 1) * line_images, :]
            span = pl.ds(pl.multiple_of(k * width + s * part, part), part)
            whole[rows, span] = piece
            added = added + lax.dot_general(
                piece,
                weighted[:, span],
                (((1,), (1,)), ((), ())),
                preferred_element_type=jnp.float32,
            )
        scores[rows, :] = added

    def store_copy(r):
        rows = pl.ds(pl.multiple_of(r * line_images, line_images), line_images)
        return pltpu.make_async_copy(whole.at[rows], gathered_ref.at[rows], store_sem.at[r])

    def score_store(r, s):
        score(r, s)

        @pl.when(s == PARTS - 1)
        def _():
            store_copy(r).start()

    @pl.loop(0, lines * PARTS + 1)
    def _(k):
        n, s = lax.div(k, PARTS) + 1, lax.rem(k, PARTS)
        for sign in (1, -1):
            r = row + sign * n

            @pl.when((r >= 0) & (r < lines) & (n < lines))
            def _(r=r):
                arrived(r, col, core, s)
                each_send(r, col, s, lambda c: c.start())

        for sign in (1, -1):
            r = row + sign * (n - 1)
            live = (r >= 0) & (r < lines) & (n <= lines)
            if sign < 0:
                live = live & (n > 1)
            for e in range(1, across):
                for side in (1, -1):
                    q = col + side * e

                    @pl.when(live & (q >= 0) & (q < across))
                    def _(r=r, q=q):
                        arrived(r, q, core, s)
                        each_send(r, q, s, lambda c: c.start())

        @pl.when(n == 1)
        def _():
            @pl.loop(0, fold // PARTS)
            def _(j):
                weigh(s * (fold // PARTS) + j)

        hop, early = lax.div(k, WORD_STEPS), lax.rem(k, WORD_STEPS)
        for sign in (1, -1):
            r = row + sign * hop

            @pl.when(bearer & (early == 0) & (hop > 0) & (hop < lines) & (r >= 0) & (r < lines))
            def _(r=r):
                word_arrived(r)
                each_word(r, lambda c: c.start())

        last = jnp.maximum(k - 1, 0)
        m, t = lax.div(last, PARTS) + 1, lax.rem(last, PARTS)

        @pl.when((m == 2) & (k > 0))
        def _():
            score_store(row, t)

        for sign in (1, -1):
            r = row + sign * (m - 1)

            @pl.when((m > 1) & (r >= 0) & (r < lines))
            def _(r=r):
                score_store(r, t)

    norm = 0.5 * jnp.sum(norms[...].T, axis=0, keepdims=True)
    value = (scores[...] - norm).T
    peak_own = jnp.max(value, axis=0, keepdims=True)
    expo = jnp.exp(value - peak_own)
    stats[...] = jnp.zeros_like(stats)
    stats[0:1, :] = peak_own
    stats[1:2, :] = jnp.sum(expo, axis=0, keepdims=True)

    def stat_copy(s):
        return pltpu.make_async_remote_copy(
            src_ref=stats,
            dst_ref=landed.at[s],
            send_sem=stat_send.at[s],
            recv_sem=stat_recv.at[s],
            device_id=(group, lax.rem(place + s, orient)),
            device_id_type=mesh_ids,
        )

    @pl.loop(1, orient)
    def _(s):
        stat_copy(s).start()

    landed[0] = stats[...]

    @pl.when(bearer)
    def _():
        words_in[row] = words[...]

    @pl.when(jnp.logical_not(bearer))
    def _():
        for r in range(lines):
            word_arrived(r)

    places_ref[...] = words_in[...]

    @pl.when(bearer)
    def _():
        each_word(row, lambda c: c.wait_send(), None)
        for r in range(lines):

            @pl.when(row != r)
            def _(r=r):
                each_word(r, lambda c: c.wait_send())

    for r in range(lines):
        store_copy(r).wait()

    @pl.loop(0, PARTS)
    def _(s):
        each_send(row, col, s, lambda c: c.wait_send(), None)
        for r in range(lines):
            for q in range(across):

                @pl.when((row != r) | (col != q))
                def _(r=r, q=q):
                    each_send(r, q, s, lambda c: c.wait_send())

    @pl.loop(1, orient)
    def _(s):
        stat_copy(s).wait()

    peak = peak_own
    for s in range(1, orient):
        peak = jnp.maximum(peak, landed[s, 0:1, :])
    total = jnp.zeros_like(peak)
    for s in range(orient):
        total = total + landed[s, 1:2, :] * jnp.exp(landed[s, 0:1, :] - peak)
    posterior = (expo * (jnp.exp(peak_own - peak) / total))[:, :images]
    post_ref[...] = posterior.astype(jnp.bfloat16)
    mass = jnp.sum(posterior, axis=1, keepdims=True)
    mass_t = jnp.broadcast_to(mass, (count, LANES)).T
    for h in range(count // LANES):
        mass_ref[h : h + 1, :] = mass_t[:1, h * LANES : (h + 1) * LANES]


def gather_scores(images, templates, index, interp, noise_flat, orient):
    own, pixels = images.shape
    count, side = index.shape
    fold = PARTS
    while own * fold % 16:
        fold += PARTS
    width = pixels // fold
    total = own * orient
    padded = -(-total // LANES) * LANES
    vmem = pl.BlockSpec(memory_space=pltpu.VMEM)
    hbm = pl.BlockSpec(memory_space=pl.ANY)
    chips = orient // 2
    return pl.pallas_call(
        functools.partial(gather_kernel, orient),
        out_shape=(
            jax.ShapeDtypeStruct((total, pixels), jnp.bfloat16),
            jax.ShapeDtypeStruct((count, total), jnp.bfloat16),
            jax.ShapeDtypeStruct((count // LANES, LANES), jnp.float32),
            jax.ShapeDtypeStruct((LINES, side, count), jnp.int32),
            jax.ShapeDtypeStruct((side * count // BATCH, BATCH), jnp.int32),
            jax.ShapeDtypeStruct((8, side), jnp.int32),
        ),
        in_specs=[vmem, hbm, vmem, vmem, vmem],
        out_specs=(hbm, vmem, vmem, vmem, vmem, vmem),
        scratch_shapes=[
            pltpu.VMEM((own * fold, width), jnp.bfloat16),
            pltpu.VMEM((own * fold, width), jnp.float32),
            pltpu.VMEM((side, count), jnp.int32),
            pltpu.VMEM((LINES, side, count), jnp.int32),
            pltpu.VMEM((orient, own * fold, width), jnp.bfloat16),
            pltpu.VMEM((count, pixels), jnp.bfloat16),
            pltpu.VMEM((total, pixels), jnp.bfloat16),
            pltpu.VMEM((padded, count), jnp.float32),
            pltpu.VMEM((count, LANES), jnp.float32),
            pltpu.VMEM((8, padded), jnp.float32),
            pltpu.VMEM((orient, 8, padded), jnp.float32),
            pltpu.SemaphoreType.DMA((fold,)),
            pltpu.SemaphoreType.DMA((LINES,)),
            pltpu.SemaphoreType.DMA((chips, PARTS, 5)),
            pltpu.SemaphoreType.DMA((orient, PARTS)),
            pltpu.SemaphoreType.DMA((orient,)),
            pltpu.SemaphoreType.DMA((orient,)),
            pltpu.SemaphoreType.DMA((LINES, 3)),
            pltpu.SemaphoreType.DMA((LINES,)),
        ],
        compiler_params=pltpu.CompilerParams(
            collective_id=1, has_side_effects=True, vmem_limit_bytes=VMEM_LIMIT
        ),
    )(images, templates, noise_flat, index, interp)


def finish_kernel(data_ref, weight_ref, data_out, weight_out):
    data_out[...] = data_ref[...]
    weight_out[...] = weight_ref[...]


def finish(data, weight):
    shape = jax.ShapeDtypeStruct(data.shape, data.dtype)
    return pl.pallas_call(finish_kernel, out_shape=(shape, shape))(data, weight)


def shards(groups, orient, images, templates, index, interp, inv_noise):
    side = inv_noise.shape[0]
    gathered, post, mass, places, voxels, clash = gather_scores(
        images, templates, index, interp, inv_noise.reshape(1, -1), orient
    )
    volume = insert_data(post, gathered, interp, voxels, clash, side * side)
    return finish(*reduce_rows(volume, mass, places, inv_noise, groups, orient))


def solution(mesh):
    placed = (
        P(("dp", "orient"), None),
        P("orient", None),
        P("orient", None),
        P("orient", None),
        P(),
    )
    return jax.shard_map(
        functools.partial(shards, mesh.shape["dp"], mesh.shape["orient"]),
        mesh=mesh,
        in_specs=placed,
        out_specs=(P(("dp", "orient"), None), P(("dp", "orient"), None)),
        check_vma=False,
    )
```

```python
import functools

import jax
import jax.numpy as jnp
from jax import lax
from jax.experimental import pallas as pl
from jax.experimental.pallas import tpu as pltpu
from jax.sharding import PartitionSpec as P

LANES = 128
ROWS_STEP = 8
ACCS = 4
SUB = 4
BATCH = 128
SLOT = 512
COLS = 2
CHUNKS = 16
WORD_STEPS = 3
LINES = 4
PARTS = 4
NORM_COLS = 1024
LEVELS = 65535
SHIFT = 65536
LOW_BITS = 6
LOW = 1 << LOW_BITS
VMEM_LIMIT = 56 * 2**20


def data_kernel(
    post_hbm,
    images_hbm,
    interp_hbm,
    idx_ref,
    clash_ref,
    out_ref,
    rows_ref,
    post_ref,
    images_two,
    interp_ref,
    idx,
    idx_sem,
    image_sem,
    once_sem,
    out_sem,
    *accs,
):
    step, steps = pl.program_id(0), pl.num_programs(0)
    count, side = post_ref.shape[0], out_ref.shape[1]
    volume_rows = out_ref.shape[0]
    wide = ROWS_STEP * side
    halves = count // BATCH
    slots = ROWS_STEP * count // SLOT
    each = SLOT // BATCH

    def fetch(at, u):
        return pltpu.make_async_copy(
            idx_ref.at[pl.ds((at * slots + u) * each, each)], idx.at[u], idx_sem.at[u]
        )

    def load(at):
        cols = pl.ds(pl.multiple_of(at * wide, wide), wide)
        two = lax.rem(at, 2)
        return pltpu.make_async_copy(
            images_hbm.at[:, cols], images_two.at[two], image_sem.at[two]
        )

    post_copy = pltpu.make_async_copy(post_hbm, post_ref, once_sem.at[0])
    interp_copy = pltpu.make_async_copy(interp_hbm, interp_ref, once_sem.at[1])

    @pl.when(step == 0)
    def _():
        post_copy.start()
        interp_copy.start()
        load(step).start()
        for u in range(slots):
            fetch(step, u).start()

        @pl.loop(0, volume_rows // 64)
        def _(c):
            rows = pl.ds(pl.multiple_of(c * 64, 64), 64)
            for acc in accs:
                acc[rows, :] = jnp.zeros((64, side), jnp.float32)

        post_copy.wait()
        interp_copy.wait()

    load(step).wait()

    @pl.when(step < steps - 1)
    def _():
        load(step + 1).start()

    images_ref = images_two.at[lax.rem(step, 2)]
    interp = pltpu.roll(interp_ref[...], lax.rem(side - step * ROWS_STEP, side), axis=1)
    for j in range(0, ROWS_STEP, COLS):
        block = jnp.dot(
            post_ref[...],
            images_ref[:, j * side : (j + COLS) * side],
            preferred_element_type=jnp.float32,
        )
        for i in range(COLS):
            rows_ref[(j + i) * count : (j + i + 1) * count, :] = (
                block[:, i * side : (i + 1) * side] * interp[:, j + i : j + i + 1]
            )

    for u in range(slots):
        fetch(step, u).wait()
        for b in range(each):
            base = (u * each + b) * BATCH
            clash = clash_ref[b % halves, step * ROWS_STEP + base // count]

            @pl.when(clash == 0)
            def _(u=u, b=b, base=base):
                pending = [()] * ACCS

                def flush(a):
                    for voxel, value in pending[a]:
                        accs[a][pl.ds(voxel, 1), :] = value

                for n in range(BATCH // SUB):
                    a = n % ACCS
                    flush(a)
                    pending[a] = []
                    for k in range(n * SUB, (n + 1) * SUB):
                        voxel = idx[u, b, k]
                        value = accs[a][pl.ds(voxel, 1), :] + rows_ref[base + k : base + k + 1, :]
                        pending[a].append((voxel, value))
                for a in range(ACCS):
                    flush(a)

            @pl.when(clash != 0)
            def _(u=u, b=b, base=base):
                @pl.loop(0, BATCH // ACCS)
                def _(q):
                    first = q * ACCS
                    targets = [idx[u, b, first + a] for a in range(ACCS)]
                    summed = [
                        accs[a][pl.ds(targets[a], 1), :]
                        + rows_ref[pl.ds(base + first + a, 1), :]
                        for a in range(ACCS)
                    ]
                    for a in range(ACCS):
                        accs[a][pl.ds(targets[a], 1), :] = summed[a]

        @pl.when(step < steps - 1)
        def _(u=u):
            fetch(step + 1, u).start()

    @pl.when(step == steps - 1)
    def _():
        chunk = volume_rows // CHUNKS

        def write(p):
            rows = pl.ds(pl.multiple_of(p * chunk, chunk), chunk)
            return pltpu.make_async_copy(accs[0].at[rows], out_ref.at[rows], out_sem.at[p])

        @pl.loop(0, CHUNKS)
        def _(p):
            @pl.loop(0, chunk // 64)
            def _(c):
                rows = pl.ds(pl.multiple_of(p * chunk + c * 64, 64), 64)
                total = accs[0][rows, :]
                for acc in accs[1:]:
                    total = total + acc[rows, :]
                accs[0][rows, :] = total

            write(p).start()

        @pl.loop(0, CHUNKS)
        def _(p):
            write(p).wait()


def insert_data(post, gathered, interp, voxels, clash, volume_rows):
    count, images = post.shape
    side = interp.shape[1]
    slots = ROWS_STEP * count // SLOT
    return pl.pallas_call(
        data_kernel,
        grid=(side // ROWS_STEP,),
        out_shape=jax.ShapeDtypeStruct((volume_rows, side), jnp.float32),
        in_specs=[
            pl.BlockSpec(memory_space=pl.ANY),
            pl.BlockSpec(memory_space=pl.ANY),
            pl.BlockSpec(memory_space=pl.ANY),
            pl.BlockSpec(memory_space=pl.ANY),
            pl.BlockSpec(memory_space=pltpu.SMEM),
        ],
        out_specs=pl.BlockSpec(memory_space=pl.ANY),
        scratch_shapes=[
            pltpu.VMEM((ROWS_STEP * count, side), jnp.float32),
            pltpu.VMEM((count, images), jnp.bfloat16),
            pltpu.VMEM((2, images, ROWS_STEP * side), jnp.bfloat16),
            pltpu.VMEM((count, side), jnp.float32),
            pltpu.SMEM((slots, SLOT // BATCH, BATCH), jnp.int32),
            pltpu.SemaphoreType.DMA((slots,)),
            pltpu.SemaphoreType.DMA((2,)),
            pltpu.SemaphoreType.DMA((2,)),
            pltpu.SemaphoreType.DMA((CHUNKS,)),
        ]
        + [pltpu.VMEM((volume_rows, side), jnp.float32)] * ACCS,
        compiler_params=pltpu.CompilerParams(vmem_limit_bytes=VMEM_LIMIT),
        cost_estimate=pl.CostEstimate(
            flops=200_000_000_000, bytes_accessed=200_000_000, transcendentals=0
        ),
    )(post, gathered, interp, voxels, clash)


def reduce_kernel(
    groups,
    orient,
    blocks_ref,
    mass_ref,
    places_hbm,
    noise_ref,
    out_ref,
    weight_ref,
    places_ref,
    places_sem,
    grid_ref,
    mass_row,
    mine,
    theirs,
    first_x,
    first_x_in,
    first_y,
    first_y_in,
    second_x,
    second_x_in,
    second_y,
    second_y_in,
    last,
    last_in,
    masses,
    twin,
    twin_in,
    own_sem,
    pair_send,
    pair_recv,
    fx_send,
    fx_recv,
    fy_send,
    fy_recv,
    sx_send,
    sx_recv,
    sy_send,
    sy_recv,
    last_send,
    last_recv,
    mass_send,
    mass_recv,
    twin_send,
    twin_recv,
):
    lines, across = LINES, orient // (2 * LINES)
    devices = groups * orient
    group, place = lax.axis_index("dp"), lax.axis_index("orient")
    core, chip = lax.rem(place, 2), lax.div(place, 2)
    row, col = lax.div(chip, across), lax.rem(chip, across)
    rank = group * orient + place
    half = out_ref.shape[0] // 2
    mesh_ids = pl.DeviceIdType.MESH

    def ranked(d):
        return (lax.div(d, orient), lax.rem(d, orient))

    def line(k):
        return lax.rem(row + k + 1, lines)

    def group_at(i):
        return lax.rem(group + i, groups)

    def col_at(j):
        return lax.rem(col + j, across)

    def block(x, r, q):
        return (x * lines + r) * across + q

    def remote(source, target, send, recv, x, r, q, c):
        return pltpu.make_async_remote_copy(
            src_ref=source,
            dst_ref=target,
            send_sem=send,
            recv_sem=recv,
            device_id=(x, (r * across + q) * 2 + c),
            device_id_type=mesh_ids,
        )

    barrier = pltpu.get_barrier_semaphore()

    @pl.loop(1, devices)
    def _(s):
        pl.semaphore_signal(
            barrier,
            inc=1,
            device_id=ranked(lax.rem(rank + s, devices)),
            device_id_type=mesh_ids,
        )

    def own_copy(k, i, j):
        p = block(group_at(i), line(k), col_at(j))
        return pltpu.make_async_copy(
            blocks_ref.at[p, core], mine.at[p], own_sem.at[k, i * across + j]
        )

    for i in reversed(range(groups)):
        for j in reversed(range(across)):

            @pl.loop(0, lines)
            def _(k, i=i, j=j):
                own_copy(k, i, j).start()

    places_copy = pltpu.make_async_copy(places_hbm, places_ref, places_sem)
    places_copy.start()

    pl.semaphore_wait(barrier, devices - 1)

    def mass_copy(s):
        return pltpu.make_async_remote_copy(
            src_ref=mass_ref,
            dst_ref=masses.at[s],
            send_sem=mass_send.at[s],
            recv_sem=mass_recv.at[s],
            device_id=ranked(lax.rem(rank + s, devices)),
            device_id_type=mesh_ids,
        )

    def pair_copy(k, i, j):
        p, n = block(group_at(i), line(k), col_at(j)), i * across + j
        return remote(
            blocks_ref.at[p, 1 - core],
            theirs.at[p],
            pair_send.at[k, n],
            pair_recv.at[k, n],
            group,
            row,
            col,
            1 - core,
        )

    def first_x_copy(k, i):
        return remote(
            first_x.at[i - 1, k],
            first_x_in.at[i - 1, k],
            fx_send.at[i - 1, k],
            fx_recv.at[i - 1, k],
            group_at(i),
            row,
            col,
            core,
        )

    def first_y_copy(k, j):
        return remote(
            first_y.at[j - 1, k],
            first_y_in.at[j - 1, k],
            fy_send.at[j - 1, k],
            fy_recv.at[j - 1, k],
            group,
            row,
            col_at(j),
            core,
        )

    def second_x_copy(k, i):
        return remote(
            second_x.at[i - 1, k],
            second_x_in.at[i - 1, k],
            sx_send.at[i - 1, k],
            sx_recv.at[i - 1, k],
            group_at(i),
            row,
            col,
            core,
        )

    def second_y_copy(k, j):
        return remote(
            second_y.at[j - 1, k],
            second_y_in.at[j - 1, k],
            sy_send.at[j - 1, k],
            sy_recv.at[j - 1, k],
            group,
            row,
            col_at(j),
            core,
        )

    def last_copy(k):
        return remote(
            last.at[k],
            last_in.at[k],
            last_send.at[k],
            last_recv.at[k],
            group,
            line(k),
            col,
            core,
        )

    @pl.loop(0, lines)
    def _(k):
        for i in reversed(range(groups)):
            for j in reversed(range(across)):
                pair_copy(k, i, j).start()

    twin_group = group + 1 - 2 * lax.rem(group, 2)

    def column(d):
        return lax.rem(lax.div(lax.rem(d, orient), 2), across)

    def mass_sent(s):
        target = lax.rem(rank + s, devices)
        return (lax.rem(lax.div(target, orient), 2) == core) & (column(target) == col)

    @pl.loop(1, devices)
    def _(s):
        @pl.when(mass_sent(s))
        def _():
            mass_copy(s).start()

    def narrow(value):
        return value.astype(jnp.bfloat16)

    def begin(k):
        for i in reversed(range(groups)):
            for j in reversed(range(across)):
                x, q = group_at(i), col_at(j)
                p = block(x, line(k), q)
                own_copy(k, i, j).wait()
                pair_copy(k, i, j).wait()
                if i == 0 or j == 0:
                    total = mine[p] + theirs[p]
                    mine[p] = total
                    if i:
                        first_x[i - 1, k, q] = narrow(total[:half])
                    if j:
                        first_y[j - 1, k, x] = narrow(total[half:])
                else:
                    first_x[i - 1, k, q] = narrow(mine[p, :half] + theirs[p, :half])
                    first_y[j - 1, k, x] = narrow(mine[p, half:] + theirs[p, half:])
            if i:
                first_x_copy(k, i).start()
        for j in range(1, across):
            first_y_copy(k, j).start()

    def middle(k):
        for i in range(1, groups):
            first_x_copy(k, i).wait()
        for j in reversed(range(across)):
            q = col_at(j)
            p = block(group, line(k), q)
            total = mine[p, :half]
            for i in range(1, groups):
                total = total + first_x_in[i - 1, k, q].astype(jnp.float32)
            if j:
                second_y[j - 1, k] = narrow(total)
                second_y_copy(k, j).start()
            else:
                mine[p, :half] = total
        for j in range(1, across):
            first_y_copy(k, j).wait()
        for i in reversed(range(groups)):
            x = group_at(i)
            p = block(x, line(k), col)
            total = mine[p, half:]
            for j in range(1, across):
                total = total + first_y_in[j - 1, k, x].astype(jnp.float32)
            if i:
                second_x[i - 1, k] = narrow(total)
                second_x_copy(k, i).start()
            else:
                mine[p, half:] = total

    def end(k):
        p = block(group, line(k), col)
        for j in range(1, across):
            second_y_copy(k, j).wait()
        top = mine[p, :half]
        for j in range(1, across):
            top = top + second_y_in[j - 1, k].astype(jnp.float32)
        for i in range(1, groups):
            second_x_copy(k, i).wait()
        low = mine[p, half:]
        for i in range(1, groups):
            low = low + second_x_in[i - 1, k].astype(jnp.float32)

        @pl.when(k < lines - 1)
        def _():
            last[k, :half] = narrow(top)
            last[k, half:] = narrow(low)
            last_copy(k).start()

        @pl.when(k == lines - 1)
        def _():
            out_ref[:half] = top
            out_ref[half:] = low

    mass_row[...] = jnp.zeros_like(mass_row)
    mass_rows = mass_ref.shape[0]

    def add_mass(d, ref):
        start = lax.div(lax.rem(d, orient), 2 * across) * (mass_rows * LANES)
        for k in range(mass_rows):
            lanes = pl.ds(pl.multiple_of(start + k * LANES, LANES), LANES)
            mass_row[:, lanes] += ref[k : k + 1, :]

    steps, slots = noise_ref.shape[0] // ROWS_STEP, 3 * (lines + 2)

    def weigh(w):
        rows = out_ref.shape[0]
        firsts = [
            (x * orient + (row * across + col_at(j)) * 2 + core) * rows
            for x in (group, twin_group)
            for j in range(across)
        ]
        weight_step(w, firsts, places_ref, mass_row, grid_ref)

    def twin_copy(n):
        return remote(
            twin.at[n - 1],
            twin_in.at[n - 1],
            twin_send.at[n - 1],
            twin_recv.at[n - 1],
            (group, twin_group)[n // across],
            row,
            col_at(n % across),
            core,
        )

    @pl.loop(0, slots)
    def _(slot):
        k, turn = lax.div(slot, 3), lax.rem(slot, 3)

        @pl.when((turn == 0) & (k < lines))
        def _():
            begin(k)

        @pl.when((turn == 1) & (k >= 1) & (k < lines + 1))
        def _():
            middle(k - 1)

        @pl.when((turn == 2) & (k >= 2))
        def _():
            end(k - 2)

        @pl.when(slot == 1)
        def _():
            places_copy.wait()

            @pl.when(core == lax.rem(group, 2))
            def _():
                add_mass(rank, mass_ref)

            @pl.loop(1, devices)
            def _(s):
                sender = lax.rem(rank + devices - s, devices)

                @pl.when((lax.rem(sender, 2) == lax.rem(group, 2)) & (column(sender) == col))
                def _():
                    mass_copy(s).wait_recv()
                    add_mass(sender, masses.at[s])

                @pl.when(mass_sent(s))
                def _():
                    mass_copy(s).wait_send()

        @pl.when((slot >= 2) & (slot < 2 + steps // 2))
        def _():
            weigh(2 * slot - 4)
            weigh(2 * slot - 3)

        @pl.when(slot == 2 + steps // 2)
        def _():
            for n in range(1, 2 * across):
                weight_rows(noise_ref, twin.at[n - 1], grid_ref, n, 2 * across)
                twin_copy(n).start()

    weight_rows(noise_ref, weight_ref, grid_ref, 0, 2 * across)
    for n in range(1, 2 * across):
        twin_copy(n).wait()
        weight_ref[...] += twin_in[n - 1].astype(jnp.float32)
    for k in range(lines - 1):
        last_copy(k).wait()
        out_ref[...] += last_in[k].astype(jnp.float32)


def reduce_rows(volume, mass_rows, places_t, inv_noise, groups, orient):
    chips = groups * orient // 2
    lines, across = LINES, orient // (2 * LINES)
    rows, side = volume.shape[0] // (2 * chips), volume.shape[1]
    half = rows // 2
    parts = (chips, rows, side)
    masses = (2 * chips,) + mass_rows.shape
    shapes = [
        (groups - 1, lines, across, half, side),
        (across - 1, lines, groups, half, side),
        (groups - 1, lines, half, side),
        (across - 1, lines, half, side),
        (lines - 1, rows, side),
    ]
    sems = [
        (groups - 1, lines),
        (across - 1, lines),
        (groups - 1, lines),
        (across - 1, lines),
        (lines - 1,),
        (2 * chips,),
    ]
    return pl.pallas_call(
        functools.partial(reduce_kernel, groups, orient),
        out_shape=(
            jax.ShapeDtypeStruct((rows, side), jnp.float32),
            jax.ShapeDtypeStruct((rows, side), jnp.float32),
        ),
        in_specs=[
            pl.BlockSpec(memory_space=pl.ANY),
            pl.BlockSpec(memory_space=pltpu.VMEM),
            pl.BlockSpec(memory_space=pl.ANY),
            pl.BlockSpec(memory_space=pltpu.VMEM),
        ],
        out_specs=(
            pl.BlockSpec(memory_space=pltpu.VMEM),
            pl.BlockSpec(memory_space=pltpu.VMEM),
        ),
        scratch_shapes=[
            pltpu.VMEM(places_t.shape, jnp.int32),
            pltpu.SemaphoreType.DMA,
            pltpu.VMEM((2 * across * side * max(8, rows // LOW), LANES), jnp.float32),
            pltpu.VMEM((1, places_t.shape[0] * places_t.shape[2]), jnp.float32),
        ]
        + [pltpu.VMEM(parts, jnp.float32)] * 2
        + [pltpu.VMEM(s, jnp.bfloat16) for s in shapes for _ in range(2)]
        + [pltpu.VMEM(masses, jnp.float32)]
        + [pltpu.VMEM((2 * across - 1, rows, side), jnp.bfloat16)] * 2
        + [pltpu.SemaphoreType.DMA((lines, groups * across))] * 3
        + [pltpu.SemaphoreType.DMA(s) for s in sems for _ in range(2)]
        + [pltpu.SemaphoreType.DMA((2 * across - 1,))] * 2,
        compiler_params=pltpu.CompilerParams(
            collective_id=0, has_side_effects=True, vmem_limit_bytes=VMEM_LIMIT
        ),
    )(volume.reshape(chips, 2, rows, side), mass_rows, places_t, inv_noise)


def weight_step(step, firsts, places_ref, mass_row, grid_ref):
    blocks, side, each = places_ref.shape
    count = blocks * each
    high_rows = grid_ref.shape[0] // side
    nt = (((1,), (1,)), ((), ()))
    one, zero = jnp.float32(1), jnp.float32(0)
    spot = lax.broadcasted_iota(jnp.int32, (high_rows, count), 0)
    each_high = high_rows // len(firsts)
    iota_high = spot
    for n, first in enumerate(firsts):
        shift = lax.div(first, LOW) - n * each_high
        iota_high = jnp.where(spot // each_high == n, spot + shift, iota_high)
    iota_low = lax.broadcasted_iota(jnp.int32, (LOW, count), 0)
    block = pl.ds(pl.multiple_of(step * ROWS_STEP, ROWS_STEP), ROWS_STEP)
    words = jnp.concatenate([places_ref[d, block, :] for d in range(blocks)], axis=1)
    voxels = words >> 16
    weights = (words & (SHIFT - 1)).astype(jnp.float32) * (1 / LEVELS) * mass_row[...]
    for j in range(ROWS_STEP):
        local = voxels[j : j + 1, :]
        hot = jnp.where(iota_high == (local >> LOW_BITS), one, zero)
        low = jnp.where(iota_low == (local & (LOW - 1)), weights[j : j + 1, :], zero)
        part = lax.dot_general(
            hot.astype(jnp.bfloat16),
            low.astype(jnp.bfloat16),
            nt,
            preferred_element_type=jnp.float32,
        )
        row = pl.multiple_of((step * ROWS_STEP + j) * high_rows, 8)
        grid_ref[pl.ds(row, high_rows), :LOW] = part


def weight_rows(noise_ref, out_ref, grid_ref, part, ranges):
    side = noise_ref.shape[0]
    high_rows = grid_ref.shape[0] // side
    noise = noise_ref[...].astype(jnp.bfloat16)
    for h in range(out_ref.shape[0] // LOW):
        first = part * (high_rows // ranges) + h
        block = lax.dot_general(
            grid_ref[pl.ds(first, side, stride=high_rows), :].astype(jnp.bfloat16),
            noise,
            (((0,), (0,)), ((), ())),
            preferred_element_type=jnp.float32,
        )
        out_ref[h * LOW : (h + 1) * LOW, :] = block[:LOW].astype(out_ref.dtype)


def gather_kernel(
    orient,
    own_ref,
    templates_ref,
    noise_ref,
    index_ref,
    interp_ref,
    gathered_ref,
    post_ref,
    mass_ref,
    places_ref,
    rows_ref,
    clash_ref,
    images_ref,
    wide,
    words,
    words_in,
    raw,
    weighted,
    whole,
    scores,
    norms,
    stats,
    landed,
    load_sem,
    store_sem,
    send_sem,
    recv_sem,
    stat_send,
    stat_recv,
    word_send,
    word_recv,
):
    lines, across = LINES, orient // (2 * LINES)
    group, place = lax.axis_index("dp"), lax.axis_index("orient")
    core = lax.rem(place, 2)
    chip = lax.div(place, 2)
    row, col = lax.div(chip, across), lax.rem(chip, across)
    mesh_ids = pl.DeviceIdType.MESH
    block_rows, width = images_ref.shape
    part = width // PARTS
    count = templates_ref.shape[0]
    fold = templates_ref.shape[1] // width
    line_images = 2 * across * block_rows // fold
    images = line_images * lines

    def at(r, q, c):
        return (r * across + q) * 2 + c

    barrier = pltpu.get_barrier_semaphore()

    @pl.loop(1, orient)
    def _(s):
        pl.semaphore_signal(
            barrier,
            inc=1,
            device_id=(group, lax.rem(place + s, orient)),
            device_id_type=mesh_ids,
        )

    def load_copy(k):
        cols = pl.ds(pl.multiple_of(k * width, width), width)
        return pltpu.make_async_copy(
            templates_ref.at[:, cols], weighted.at[:, cols], load_sem.at[k]
        )

    for k in range(fold):
        load_copy(k).start()

    own_rows = own_ref.shape[0]
    for k in range(fold):
        wide[k * own_rows : (k + 1) * own_rows, :] = own_ref[
            :, k * width : (k + 1) * width
        ].astype(jnp.float32)
    images_ref[...] = wide[...].astype(jnp.bfloat16)
    index = index_ref[...]
    near = jnp.zeros(index.shape, jnp.int32)
    spot = lax.broadcasted_iota(jnp.int32, index.shape, 0) % SUB
    for d in range(1, SUB):
        same = (index == pltpu.roll(index, d, axis=0)) & (spot >= d)
        near = near | same.astype(jnp.int32)
    clash_ref[...] = jnp.zeros_like(clash_ref)
    for h in range(count // BATCH):
        clash_ref[h : h + 1, :] = jnp.max(
            near[h * BATCH : (h + 1) * BATCH, :], axis=0, keepdims=True
        )
    index_t = index.T
    for h in range(count // BATCH):
        rows_ref[pl.ds(h, index_t.shape[0], stride=count // BATCH), :] = index_t[
            :, h * BATCH : (h + 1) * BATCH
        ]
    level = (interp_ref[...] * LEVELS + 0.5).astype(jnp.int32)
    words[...] = (index * SHIFT + level).T
    pl.semaphore_wait(barrier, orient - 1)

    bearer = lax.rem(group, 2) == core

    def word_copy(source, r, way, target):
        return pltpu.make_async_remote_copy(
            src_ref=words if source is None else words_in.at[r],
            dst_ref=words_in.at[r],
            send_sem=word_send.at[r, way],
            recv_sem=word_recv.at[r],
            device_id=(group, target),
            device_id_type=mesh_ids,
        )

    def word_arrived(r):
        word_copy(words_in, r, 2, place + 1 - 2 * core).wait_recv()

    def each_word(r, act, source=words_in):
        for way, step in ((0, 1), (1, -1)):
            onward = row + step
            along = (onward >= 0) & (onward < lines)
            if source is not None:
                along = along & ((row - r) * step > 0)

            @pl.when(along)
            def _(way=way, onward=onward):
                act(word_copy(source, r, way, at(onward, col, core)))

        act(word_copy(source, r, 2, place + 1 - 2 * core))

    @pl.when(bearer)
    def _():
        each_word(row, lambda c: c.start(), None)

    def copy(source, r, q, s, way, target):
        cols = pl.ds(pl.multiple_of(s * part, part), part)
        slot = at(r, q, core)
        ref = images_ref if source is None else raw.at[slot]
        return pltpu.make_async_remote_copy(
            src_ref=ref.at[:, cols],
            dst_ref=raw.at[slot, :, cols],
            send_sem=send_sem.at[lax.div(slot, 2), s, way],
            recv_sem=recv_sem.at[slot, s],
            device_id=(group, target),
            device_id_type=mesh_ids,
        )

    def arrived(r, q, c, s):
        cols = pl.ds(pl.multiple_of(s * part, part), part)
        slot = at(r, q, c)
        pltpu.make_async_remote_copy(
            src_ref=raw.at[slot, :, cols],
            dst_ref=raw.at[slot, :, cols],
            send_sem=send_sem.at[0, 0, 0],
            recv_sem=recv_sem.at[slot, s],
            device_id=(group, place + 1 - 2 * core),
            device_id_type=mesh_ids,
        ).wait_recv()

    def each_send(r, q, s, act, source=raw):
        for way, step in ((0, 1), (1, -1)):
            onward = row + step
            if source is None:
                along = (onward >= 0) & (onward < lines)
            else:
                along = (q == col) & (onward >= 0) & (onward < lines) & ((row - r) * step > 0)

            @pl.when(along)
            def _(way=way, onward=onward):
                act(copy(source, r, q, s, way, at(onward, col, core)))

        for way, step in ((2, 1), (3, -1)):
            onward = col + step
            beside = (onward >= 0) & (onward < across) & ((col - q) * step >= 0)

            @pl.when(beside)
            def _(way=way, onward=onward):
                act(copy(source, r, q, s, way, at(row, onward, core)))

        act(copy(source, r, q, s, 4, place + 1 - 2 * core))

    @pl.loop(0, PARTS)
    def _(s):
        each_send(row, col, s, lambda c: c.start(), None)

    raw[place] = images_ref[...]
    scores[...] = jnp.zeros_like(scores)
    norms[...] = jnp.zeros_like(norms)

    def weigh(k):
        load_copy(k).wait()

        @pl.loop(0, width // NORM_COLS)
        def _(g):
            cols = pl.ds(pl.multiple_of(k * width + g * NORM_COLS, NORM_COLS), NORM_COLS)
            for h in range(0, count, 64):
                tpl = weighted[h : h + 64, cols].astype(jnp.float32)
                noise = noise_ref[:, cols]
                scaled = tpl * noise
                square = tpl * tpl * noise
                total = square[:, :LANES]
                for j in range(1, NORM_COLS // LANES):
                    total = total + square[:, j * LANES : (j + 1) * LANES]
                norms[h : h + 64, :] += total
                weighted[h : h + 64, cols] = scaled.astype(jnp.bfloat16)

    def score(r, s):
        for q in range(across):
            arrived(r, q, 1 - core, s)
        cols = pl.ds(pl.multiple_of(s * part, part), part)
        slots = pl.ds(pl.multiple_of(r * (2 * across), 2 * across), 2 * across)
        block = raw[slots, :, cols].reshape(2 * across * block_rows, part)
        total = 2 * across * block_rows
        out_row = lax.broadcasted_iota(jnp.int32, (total, total), 0)
        from_row = lax.broadcasted_iota(jnp.int32, (total, total), 1)
        image, piece = out_row % line_images, out_row // line_images
        wanted = (image // own_rows) * block_rows + piece * own_rows + image % own_rows
        pick = jnp.where(from_row == wanted, 1.0, 0.0).astype(jnp.bfloat16)
        sorted_ = jnp.dot(pick, block, preferred_element_type=jnp.float32)
        sorted_ = sorted_.astype(jnp.bfloat16)
        rows = pl.ds(pl.multiple_of(r * line_images, line_images), line_images)
        added = scores[rows, :]
        for k in range(fold):
            piece = sorted_[k * line_images : (k + 1) * line_images, :]
            span = pl.ds(pl.multiple_of(k * width + s * part, part), part)
            whole[rows, span] = piece
            added = added + lax.dot_general(
                piece,
                weighted[:, span],
                (((1,), (1,)), ((), ())),
                preferred_element_type=jnp.float32,
            )
        scores[rows, :] = added

    def store_copy(r):
        rows = pl.ds(pl.multiple_of(r * line_images, line_images), line_images)
        return pltpu.make_async_copy(whole.at[rows], gathered_ref.at[rows], store_sem.at[r])

    def score_store(r, s):
        score(r, s)

        @pl.when(s == PARTS - 1)
        def _():
            store_copy(r).start()

    @pl.loop(0, lines * PARTS + 1)
    def _(k):
        n, s = lax.div(k, PARTS) + 1, lax.rem(k, PARTS)
        for sign in (1, -1):
            r = row + sign * n

            @pl.when((r >= 0) & (r < lines) & (n < lines))
            def _(r=r):
                arrived(r, col, core, s)
                each_send(r, col, s, lambda c: c.start())

        for sign in (1, -1):
            r = row + sign * (n - 1)
            live = (r >= 0) & (r < lines) & (n <= lines)
            if sign < 0:
                live = live & (n > 1)
            for e in range(1, across):
                for side in (1, -1):
                    q = col + side * e

                    @pl.when(live & (q >= 0) & (q < across))
                    def _(r=r, q=q):
                        arrived(r, q, core, s)
                        each_send(r, q, s, lambda c: c.start())

        @pl.when(n == 1)
        def _():
            @pl.loop(0, fold // PARTS)
            def _(j):
                weigh(s * (fold // PARTS) + j)

        hop, early = lax.div(k, WORD_STEPS), lax.rem(k, WORD_STEPS)
        for sign in (1, -1):
            r = row + sign * hop

            @pl.when(bearer & (early == 0) & (hop > 0) & (hop < lines) & (r >= 0) & (r < lines))
            def _(r=r):
                word_arrived(r)
                each_word(r, lambda c: c.start())

        last = jnp.maximum(k - 1, 0)
        m, t = lax.div(last, PARTS) + 1, lax.rem(last, PARTS)

        @pl.when((m == 2) & (k > 0))
        def _():
            score_store(row, t)

        for sign in (1, -1):
            r = row + sign * (m - 1)

            @pl.when((m > 1) & (r >= 0) & (r < lines))
            def _(r=r):
                score_store(r, t)

    norm = 0.5 * jnp.sum(norms[...].T, axis=0, keepdims=True)
    value = (scores[...] - norm).T
    peak_own = jnp.max(value, axis=0, keepdims=True)
    expo = jnp.exp(value - peak_own)
    stats[...] = jnp.zeros_like(stats)
    stats[0:1, :] = peak_own
    stats[1:2, :] = jnp.sum(expo, axis=0, keepdims=True)

    def stat_copy(s):
        return pltpu.make_async_remote_copy(
            src_ref=stats,
            dst_ref=landed.at[s],
            send_sem=stat_send.at[s],
            recv_sem=stat_recv.at[s],
            device_id=(group, lax.rem(place + s, orient)),
            device_id_type=mesh_ids,
        )

    @pl.loop(1, orient)
    def _(s):
        stat_copy(s).start()

    landed[0] = stats[...]

    @pl.when(bearer)
    def _():
        words_in[row] = words[...]

    @pl.when(jnp.logical_not(bearer))
    def _():
        for r in range(lines):
            word_arrived(r)

    places_ref[...] = words_in[...]

    @pl.when(bearer)
    def _():
        each_word(row, lambda c: c.wait_send(), None)
        for r in range(lines):

            @pl.when(row != r)
            def _(r=r):
                each_word(r, lambda c: c.wait_send())

    for r in range(lines):
        store_copy(r).wait()

    @pl.loop(0, PARTS)
    def _(s):
        each_send(row, col, s, lambda c: c.wait_send(), None)
        for r in range(lines):
            for q in range(across):

                @pl.when((row != r) | (col != q))
                def _(r=r, q=q):
                    each_send(r, q, s, lambda c: c.wait_send())

    @pl.loop(1, orient)
    def _(s):
        stat_copy(s).wait()

    peak = peak_own
    for s in range(1, orient):
        peak = jnp.maximum(peak, landed[s, 0:1, :])
    total = jnp.zeros_like(peak)
    for s in range(orient):
        total = total + landed[s, 1:2, :] * jnp.exp(landed[s, 0:1, :] - peak)
    posterior = (expo * (jnp.exp(peak_own - peak) / total))[:, :images]
    post_ref[...] = posterior.astype(jnp.bfloat16)
    mass = jnp.sum(posterior, axis=1, keepdims=True)
    mass_t = jnp.broadcast_to(mass, (count, LANES)).T
    for h in range(count // LANES):
        mass_ref[h : h + 1, :] = mass_t[:1, h * LANES : (h + 1) * LANES]


def gather_scores(images, templates, index, interp, noise_flat, orient):
    own, pixels = images.shape
    count, side = index.shape
    fold = PARTS
    while own * fold % 16:
        fold += PARTS
    width = pixels // fold
    total = own * orient
    padded = -(-total // LANES) * LANES
    vmem = pl.BlockSpec(memory_space=pltpu.VMEM)
    hbm = pl.BlockSpec(memory_space=pl.ANY)
    chips = orient // 2
    return pl.pallas_call(
        functools.partial(gather_kernel, orient),
        out_shape=(
            jax.ShapeDtypeStruct((total, pixels), jnp.bfloat16),
            jax.ShapeDtypeStruct((count, total), jnp.bfloat16),
            jax.ShapeDtypeStruct((count // LANES, LANES), jnp.float32),
            jax.ShapeDtypeStruct((LINES, side, count), jnp.int32),
            jax.ShapeDtypeStruct((side * count // BATCH, BATCH), jnp.int32),
            jax.ShapeDtypeStruct((8, side), jnp.int32),
        ),
        in_specs=[vmem, hbm, vmem, vmem, vmem],
        out_specs=(hbm, vmem, vmem, vmem, vmem, vmem),
        scratch_shapes=[
            pltpu.VMEM((own * fold, width), jnp.bfloat16),
            pltpu.VMEM((own * fold, width), jnp.float32),
            pltpu.VMEM((side, count), jnp.int32),
            pltpu.VMEM((LINES, side, count), jnp.int32),
            pltpu.VMEM((orient, own * fold, width), jnp.bfloat16),
            pltpu.VMEM((count, pixels), jnp.bfloat16),
            pltpu.VMEM((total, pixels), jnp.bfloat16),
            pltpu.VMEM((padded, count), jnp.float32),
            pltpu.VMEM((count, LANES), jnp.float32),
            pltpu.VMEM((8, padded), jnp.float32),
            pltpu.VMEM((orient, 8, padded), jnp.float32),
            pltpu.SemaphoreType.DMA((fold,)),
            pltpu.SemaphoreType.DMA((LINES,)),
            pltpu.SemaphoreType.DMA((chips, PARTS, 5)),
            pltpu.SemaphoreType.DMA((orient, PARTS)),
            pltpu.SemaphoreType.DMA((orient,)),
            pltpu.SemaphoreType.DMA((orient,)),
            pltpu.SemaphoreType.DMA((LINES, 3)),
            pltpu.SemaphoreType.DMA((LINES,)),
        ],
        compiler_params=pltpu.CompilerParams(
            collective_id=1, has_side_effects=True, vmem_limit_bytes=VMEM_LIMIT
        ),
    )(images, templates, noise_flat, index, interp)


def finish_kernel(data_ref, weight_ref, data_out, weight_out):
    data_out[...] = data_ref[...]
    weight_out[...] = weight_ref[...]


def finish(data, weight):
    shape = jax.ShapeDtypeStruct(data.shape, data.dtype)
    return pl.pallas_call(finish_kernel, out_shape=(shape, shape))(data, weight)


def shards(groups, orient, images, templates, index, interp, inv_noise):
    side = inv_noise.shape[0]
    gathered, post, mass, places, voxels, clash = gather_scores(
        images, templates, index, interp, inv_noise.reshape(1, -1), orient
    )
    volume = insert_data(post, gathered, interp, voxels, clash, side * side)
    return finish(*reduce_rows(volume, mass, places, inv_noise, groups, orient))


def solution(mesh):
    placed = (
        P(("dp", "orient"), None),
        P("orient", None),
        P("orient", None),
        P("orient", None),
        P(),
    )
    return jax.shard_map(
        functools.partial(shards, mesh.shape["dp"], mesh.shape["orient"]),
        mesh=mesh,
        in_specs=placed,
        out_specs=(P(("dp", "orient"), None), P(("dp", "orient"), None)),
        check_vma=False,
    )
```
